32 devices in a mesh: group: 4 (over y, core), inner: 8 (over z, x).
Axes of the slice: x: 2, y: 2, z: 4, core: 2. Of those that a mesh axis runs over, the one named last changes fastest.
Arguments:
- pair_rows: bfloat16 [512, 2048], P(('group', 'inner')), may hold values from -6 to 6
- group_ids: int32 [512, 1], P(('group', 'inner')), may hold values from 0 to 3; in each aligned block of 16 rows (0 to 15, 16 to 31, ...) at most 8 rows name the same one
- local_ids: int32 [512, 1], P(('group', 'inner')), may hold values from 0 to 1
- route_weight: float32 [512], P(('group', 'inner')), may hold values from 0.3 to 1
- w_up: bfloat16 [8, 2048, 8192], P('group', None, 'inner'), may hold values from -0.125 to 0.125
- w_down: bfloat16 [8, 8192, 2048], P('group', 'inner'), may hold values from -0.0625 to 0.0625
Outputs:
- mixed: bfloat16 [512, 2048], P(('group', 'inner'))
The draws below stay inside these ranges and needn't reach their ends.
Inputs may be any that keep to these rules, and one draw needn't show every extreme that they name: `group_ids`: among the rows of one device no value is named more than 8 times, a bound that some block reaches.
All inputs are finite; a program needn't handle non-finite values.
Results may differ from the reference program's by a relative error of at most 0.02.
Values may be sent and summed in bfloat16 or wider, within the bound.
No kernel may reach another device: no remote copies, remote signals or barrier semaphores. Data moves between devices by JAX's collectives and lax.ppermute only.
A program may use at most 64 MiB of HBM per device.

```python
import math
import jax
import jax.numpy as jnp
import numpy as np
from jax import lax

D = 2048
FF = 8192
EXP_GROUP = 2
ROWS_DEV = 16
GCAP = 8
EXPERTS = 8
TOKENS = 512
N_GROUP = 4
N_INNER = 8


def set_ends(array, key, smallest, largest):
    longest = array.shape.index(max(array.shape))
    spots = []
    for shift in (0, 1):
        where = [jax.random.randint(jax.random.fold_in(key, axis), (), 0, length) for axis, length in enumerate(array.shape)]
        where[longest] = (where[longest] + shift) % array.shape[longest]
        spots.append(tuple(where))
    return array.at[spots[0]].set(smallest).at[spots[1]].set(largest)


def levels(rng, extent, cuts, low, high):
    gain, own = 1.0, jax.random.fold_in(rng, 6)
    for dim, parts in cuts:
        heights = jnp.exp(jax.random.uniform(jax.random.fold_in(own, dim), (parts,), jnp.float32, low / len(cuts), high / len(cuts)))
        gain = gain * jnp.repeat(heights, extent[dim] // parts).reshape([-1 if axis == dim else 1 for axis in range(len(extent))])
    return gain


def shared_out(key, own, number, rows, number_of, top, most, slope):
    order = jax.random.permutation(key, number_of)
    packed, usual = load_shares(number_of, rows * top, most, slope, True), load_shares(number_of, rows * top, most, slope, False)
    places = jnp.arange(number_of)

    def named(tallies, rotation):
        used = int((tallies > 0).sum())
        fixed = max(1, used // 4)
        shifted = fixed + (places - fixed + rotation * (used - fixed)) % max(1, number_of - fixed)
        return jnp.zeros((number_of,), jnp.int32).at[order[jnp.where(places < fixed, places, shifted)]].set(jnp.asarray(tallies, jnp.int32))

    tallies = jnp.where(number % 4 == 0, named(packed, number // 4), named(usual, number - number // 4 - 1))
    mixed = jax.random.permutation(jax.random.fold_in(own, 3), number_of)
    giver, sink = mixed[0:number_of // 2 * 2:2], mixed[1:number_of // 2 * 2:2]
    margin = jnp.minimum(tallies[giver] - 1, most - tallies[sink]) // 2
    margin = jnp.where((giver == order[0]) | (sink == order[0]) | (tallies[sink] == 0), 0, jnp.maximum(margin, 0))
    shifted = jax.random.randint(jax.random.fold_in(own, 4), (number_of // 2,), 0, 1 << 20) % (margin + 1)
    tallies = tallies.at[giver].add(-shifted).at[sink].add(shifted)
    labels = jnp.searchsorted(jnp.cumsum(tallies), jnp.arange(rows * top), side="right").astype(jnp.int32)
    grid = labels.reshape(top, rows).T
    grid = grid[jax.random.permutation(jax.random.fold_in(own, 1), rows)]
    rotation = jax.random.randint(jax.random.fold_in(own, 2), (rows, 1), 0, top)
    return jnp.take_along_axis(grid, (jnp.arange(top)[None, :] + rotation) % top, axis=1)


def load_shares(amount, total, bound, lean, full):
    weights = [(1 << 20) // math.isqrt(standing ** lean) + 1 for standing in range(1, amount + 1)]
    largest = bound if full else min(bound, max(-(-total // amount), total * weights[0] // sum(weights)))
    least = 1 if total - largest >= amount - 1 else 0
    holding, rest = [largest] + [least] * (amount - 1), total - largest - least * (amount - 1)
    while rest > 0:
        candidates = [i for i in range(1, amount) if holding[i] < largest] or [i for i in range(1, amount) if holding[i] < bound]
        whole, remaining = sum([weights[i] for i in candidates]), rest
        for i in candidates:
            addition = min(bound - holding[i], max(1, remaining * weights[i] // whole), rest)
            holding[i] = holding[i] + addition
            rest = rest - addition
    return np.array(holding)


def gaussian(key, dims, deviation, limit, pieces=(), held_as=jnp.bfloat16):
    loudness = levels(key, dims, pieces, -0.22, 0.18) if pieces else 1.0
    entries = jax.random.normal(key, dims, jnp.float32) * deviation * loudness
    return jnp.minimum(jnp.maximum(entries, -limit), limit).astype(held_as)


def setup_inputs(seed: int = 0) -> dict:
    key_list = jax.random.split(jax.random.key(seed), 7)
    pair_rows = gaussian(key_list[0], (TOKENS, D), 1.0, 6.0, ((0, 32),))
    group_ids_keys = jax.random.split(jax.random.fold_in(key_list[1], 1), TOKENS // ROWS_DEV)
    group_ids_turns = jax.random.permutation(jax.random.fold_in(key_list[1], 3), TOKENS // ROWS_DEV)
    group_ids = jax.vmap(lambda own, number: shared_out(jax.random.fold_in(key_list[1], 2), own, number, ROWS_DEV, N_GROUP, 1, GCAP, 2))(group_ids_keys, group_ids_turns).reshape((TOKENS, 1))
    local_ids = set_ends(jax.random.randint(key_list[2], (TOKENS, 1), 0, EXP_GROUP), jax.random.fold_in(key_list[2], 1), 0, EXP_GROUP - 1).astype(jnp.int32)
    route_weight = jnp.clip(jnp.exp(math.log(1.0) - 1.2039728 * jax.random.uniform(key_list[3], (TOKENS,), jnp.float32) ** levels(key_list[3], (TOKENS,), ((0, 32),), -0.2, 0.2)), 0.3, 1.0)
    w_up = gaussian(key_list[4], (EXPERTS, D, FF), D ** -0.5, 0.125, ((0, 4), (2, 8)))
    w_down = gaussian(key_list[5], (EXPERTS, FF, D), FF ** -0.5, 0.0625, ((0, 4), (1, 8)))
    return dict(pair_rows=pair_rows, group_ids=group_ids, local_ids=local_ids, route_weight=route_weight, w_up=w_up, w_down=w_down)


def reference(pair_rows, group_ids, local_ids, route_weight, w_up, w_down):
    expert_of = (group_ids[:, 0] * EXP_GROUP + local_ids[:, 0]).astype(jnp.int32)
    sorted_rows = jnp.argsort(expert_of, stable=True).astype(jnp.int32)
    counts = jnp.sum((expert_of[:, None] == jnp.arange(EXPERTS, dtype=jnp.int32)[None, :]).astype(jnp.int32), 0)
    starts = (jnp.cumsum(counts) - counts).astype(jnp.int32)
    most_rows = GCAP * N_GROUP * N_INNER
    padded = jnp.concatenate([sorted_rows, jnp.zeros((most_rows,), jnp.int32)])
    slice_width = FF // N_INNER

    def expert_step(expert, summed_out):
        start = starts[expert]
        row_index = lax.dynamic_slice_in_dim(padded, start, most_rows)
        is_valid = jnp.arange(most_rows, dtype=jnp.int32) < counts[expert]
        picked = pair_rows[row_index]
        up_val = jnp.dot(picked, w_up[expert], preferred_element_type=jnp.float32)
        hidden = jax.nn.silu(up_val).astype(jnp.bfloat16)
        down_mat = w_down[expert]

        def add_slice(running, which):
            hidden_part = lax.dynamic_slice_in_dim(hidden, which * slice_width, slice_width, 1)
            down_part = lax.dynamic_slice_in_dim(down_mat, which * slice_width, slice_width, 0)
            partial_value = jnp.dot(hidden_part, down_part, preferred_element_type=jnp.float32).astype(jnp.bfloat16)
            partial_value = lax.optimization_barrier(partial_value)
            return running + partial_value.astype(jnp.float32), None

        summed, _ = lax.scan(add_slice, jnp.zeros((most_rows, D), jnp.float32), jnp.arange(N_INNER, dtype=jnp.int32))
        summed = jnp.where(is_valid[:, None], summed, jnp.zeros_like(summed))
        return summed_out.at[row_index].add(summed)

    summed_out = lax.fori_loop(0, EXPERTS, expert_step, jnp.zeros((TOKENS, D), jnp.float32))
    expert_out = summed_out.astype(jnp.bfloat16)
    return (expert_out.astype(jnp.float32) * route_weight[:, None]).astype(jnp.bfloat16)
```

```python
import functools

import jax
import jax.numpy as jnp
from jax import lax
from jax.experimental import pallas as pl
from jax.experimental.pallas import tpu as pltpu
from jax.sharding import PartitionSpec as P

LANES = 128
VMEM_SPEC = pl.BlockSpec(memory_space=pltpu.VMEM)
ANY_SPEC = pl.BlockSpec(memory_space=pl.ANY)


def tag_kernel(capacity, rows_ref, group_ref, local_ref, out_ref):
    count, width = rows_ref.shape
    across = lax.broadcasted_iota(jnp.int32, (count, count), 1)
    down = lax.broadcasted_iota(jnp.int32, (count, count), 0)
    group_across = jnp.broadcast_to(group_ref[...], (count, count))
    local_across = jnp.broadcast_to(local_ref[...], (count, count))
    diagonal = across == down
    group_down = jnp.sum(jnp.where(diagonal, group_across, 0), axis=1, keepdims=True)
    local_down = jnp.sum(jnp.where(diagonal, local_across, 0), axis=1, keepdims=True)
    before = (group_across == group_down) & (across < down)
    rank = jnp.sum(jnp.where(before, 1, 0), axis=1, keepdims=True)
    slot = group_down * capacity + rank
    lane = lax.broadcasted_iota(jnp.int32, (count, LANES), 1)
    tags = jnp.where(lane == 0, slot, jnp.where(lane == 1, local_down + 1, 0))
    out_ref[:, :width] = rows_ref[...]
    out_ref[:, width:] = tags.astype(jnp.float32).astype(jnp.bfloat16)


def placing(tag_refs, capacity, groups, turns):
    me = lax.axis_index("group")
    owners = len(tag_refs)
    block = owners * capacity
    count = tag_refs[0].shape[0]
    column = lax.broadcasted_iota(jnp.int32, (count, turns * block), 1)
    turn = column // block
    owner = (column % block) // capacity
    wanted = (me ^ turn) * capacity + column % capacity
    parts = []
    for which, tag_ref in enumerate(tag_refs):
        slot = tag_ref[:, 0:1].astype(jnp.float32).astype(jnp.int32)
        parts.append((slot == wanted) & (owner == which))
    return jnp.concatenate([p.astype(jnp.float32) for p in parts], axis=0).astype(jnp.bfloat16)


def pack_kernel(capacity, groups, owners, *refs):
    row_refs, out_refs = refs[:owners], refs[owners:]
    width = row_refs[0].shape[1] - LANES
    onehot = placing([r.at[:, width:] for r in row_refs], capacity, groups, groups)
    rows = jnp.concatenate([r[...] for r in row_refs], axis=0)
    packed = lax.dot_general(
        onehot, rows, (((0,), (0,)), ((), ())), preferred_element_type=jnp.float32
    ).astype(jnp.bfloat16)
    block = owners * capacity
    for turn, out_ref in enumerate(out_refs):
        out_ref[...] = packed[turn * block : (turn + 1) * block]


def expert_kernel(blocks, up_step, down_step, *refs):
    row_refs = refs[:blocks]
    up_ref, down_ref = refs[blocks], refs[blocks + 1]
    out_refs = refs[blocks + 2 : 2 * blocks + 2]
    rows, hidden, up_held, down_held, up_sem, down_sem = refs[2 * blocks + 2 :]
    experts, width, units = up_held.shape
    block = row_refs[0].shape[0]
    up_steps, down_steps = units // up_step, width // down_step

    def up_copy(expert, step):
        cols = pl.ds(step * up_step, up_step)
        return pltpu.make_async_copy(
            up_ref.at[expert, :, cols], up_held.at[expert, :, cols], up_sem.at[expert, step]
        )

    def down_copy(step):
        cols = pl.ds(step * down_step, down_step)
        return pltpu.make_async_copy(
            down_ref.at[:, :, cols], down_held.at[:, :, cols], down_sem.at[step]
        )

    for expert in range(experts):
        for step in range(up_steps):
            up_copy(expert, step).start()
    for step in range(down_steps):
        down_copy(step).start()

    for which, row_ref in enumerate(row_refs):
        rows[which * block : (which + 1) * block, :] = row_ref[...]
    chosen = rows[:, width:].astype(jnp.float32)[:, 1:2]
    for expert in range(experts):
        mine = chosen == float(expert + 1)
        for step in range(up_steps):
            up_copy(expert, step).wait()
            up_val = jnp.dot(
                rows[:, :width],
                up_held[expert, :, step * up_step : (step + 1) * up_step],
                preferred_element_type=jnp.float32,
            )
            value = jnp.where(mine, up_val / (1.0 + jnp.exp(-up_val)), 0.0)
            start = expert * units + step * up_step
            hidden[:, start : start + up_step] = value.astype(jnp.bfloat16)
    for step in range(down_steps):
        down_copy(step).wait()
        cols = slice(step * down_step, (step + 1) * down_step)
        total = jnp.dot(
            hidden[:, :units], down_held[0, :, cols], preferred_element_type=jnp.float32
        )
        for expert in range(1, experts):
            total += jnp.dot(
                hidden[:, expert * units : (expert + 1) * units],
                down_held[expert, :, cols],
                preferred_element_type=jnp.float32,
            )
        total = total.astype(jnp.bfloat16)
        for which, out_ref in enumerate(out_refs):
            out_ref[:, cols] = total[which * block : (which + 1) * block]


def unpack_kernel(capacity, groups, owners, copies, *refs):
    tag_refs = refs[:owners]
    part_refs = refs[owners : owners + groups * copies]
    out_refs = refs[owners + groups * copies :]
    width = part_refs[0].shape[1]
    onehot = placing([r.at[:, width:] for r in tag_refs], capacity, groups, groups)
    block = owners * capacity
    sums = []
    for turn in range(groups):
        value = part_refs[turn * copies][...].astype(jnp.float32)
        for copy in range(1, copies):
            value += part_refs[turn * copies + copy][...].astype(jnp.float32)
        sums.append(value.astype(jnp.bfloat16))
    summed = jnp.concatenate(sums, axis=0)
    dense = jnp.dot(onehot, summed, preferred_element_type=jnp.float32).astype(jnp.bfloat16)
    count = tag_refs[0].shape[0]
    for which, out_ref in enumerate(out_refs):
        out_ref[...] = dense[which * count : (which + 1) * count]


def body(pair_rows, group_ids, local_ids, route_weight, w_up, w_down):
    groups = lax.axis_size("group")
    inner = lax.axis_size("inner")
    near = 2 if inner % 2 == 0 else 1
    far = inner // near
    count, width = pair_rows.shape
    experts, _, units = w_up.shape
    capacity = 2 * count // groups
    block = far * capacity
    bf16 = jnp.bfloat16
    full = width + LANES

    tagged = pl.pallas_call(
        functools.partial(tag_kernel, capacity),
        out_shape=jax.ShapeDtypeStruct((count, full), bf16),
        in_specs=[VMEM_SPEC] * 3,
        out_specs=VMEM_SPEC,
        name="tag_rows",
    )(pair_rows, group_ids.reshape(1, count), local_ids.reshape(1, count))

    def along_far(value, shift):
        pairs = [
            (a * near + b, ((a + shift) % far) * near + b) for a in range(far) for b in range(near)
        ]
        return lax.ppermute(value, "inner", pairs)

    def in_plane(value, turn, swap):
        pairs = [
            (g * inner + a * near + b, (g ^ turn) * inner + a * near + (b ^ swap))
            for g in range(groups)
            for a in range(far)
            for b in range(near)
        ]
        return lax.ppermute(value, ("group", "inner"), pairs)

    owned = [tagged] + [along_far(tagged, s) for s in range(1, far)]

    packed = pl.pallas_call(
        functools.partial(pack_kernel, capacity, groups, far),
        out_shape=[jax.ShapeDtypeStruct((block, full), bf16)] * groups,
        in_specs=[VMEM_SPEC] * far,
        out_specs=[VMEM_SPEC] * groups,
        name="pack_slots",
    )(*owned)

    hops = [(turn, swap) for turn in range(groups) for swap in range(near)]
    arrived = [
        packed[turn] if (turn, swap) == (0, 0) else in_plane(packed[turn], turn, swap)
        for turn, swap in hops
    ]

    blocks = len(hops)
    up_step = min(256, units)
    down_step = min(256, width)
    partial = pl.pallas_call(
        functools.partial(expert_kernel, blocks, up_step, down_step),
        out_shape=[jax.ShapeDtypeStruct((block, width), bf16)] * blocks,
        in_specs=[VMEM_SPEC] * blocks + [ANY_SPEC] * 2,
        out_specs=[VMEM_SPEC] * blocks,
        scratch_shapes=[
            pltpu.VMEM((blocks * block, full), bf16),
            pltpu.VMEM((blocks * block, experts * units), bf16),
            pltpu.VMEM((experts, width, units), bf16),
            pltpu.VMEM((experts, units, width), bf16),
            pltpu.SemaphoreType.DMA((experts, units // up_step)),
            pltpu.SemaphoreType.DMA((width // down_step,)),
        ],
        compiler_params=pltpu.CompilerParams(vmem_limit_bytes=50 * 2**20),
        cost_estimate=pl.CostEstimate(
            flops=4 * blocks * block * width * experts * units,
            bytes_accessed=4 * experts * width * units,
            transcendentals=blocks * block * experts * units,
        ),
        name="experts",
    )(*arrived, w_up, w_down)

    back = [
        partial[i] if (turn, swap) == (0, 0) else in_plane(partial[i], turn, swap)
        for i, (turn, swap) in enumerate(hops)
    ]

    dense = pl.pallas_call(
        functools.partial(unpack_kernel, capacity, groups, far, near),
        out_shape=[jax.ShapeDtypeStruct((count, width), bf16)] * far,
        in_specs=[VMEM_SPEC] * (far + blocks),
        out_specs=[VMEM_SPEC] * far,
        name="unpack_slots",
    )(*owned, *back)

    total = dense[0].astype(jnp.float32)
    for s in range(1, far):
        total += along_far(dense[s], -s).astype(jnp.float32)
    expert_out = total.astype(bf16).astype(jnp.float32)
    return (expert_out * route_weight[:, None]).astype(bf16)


def solution(mesh):
    placed = (
        P(("group", "inner"), None),
        P(("group", "inner"), None),
        P(("group", "inner"), None),
        P(("group", "inner")),
        P("group", None, "inner"),
        P("group", "inner", None),
    )
    return jax.shard_map(
        body, mesh=mesh, in_specs=placed, out_specs=P(("group", "inner"), None), check_vma=False
    )
```

```python
import functools

import jax
import jax.numpy as jnp
from jax import lax
from jax.experimental import pallas as pl
from jax.experimental.pallas import tpu as pltpu
from jax.sharding import PartitionSpec as P

LANES = 128
MIB = 2**20
BF16 = jnp.bfloat16
F32 = jnp.float32
VMEM_SPEC = pl.BlockSpec(memory_space=pltpu.VMEM)
ANY_SPEC = pl.BlockSpec(memory_space=pl.ANY)
HBM_SPEC = pl.BlockSpec(memory_space=pltpu.HBM)


def call(kernel, name, outs, args, limit=4, scratch=(), flops=0, moved=0, specs=None):
    shapes = [jax.ShapeDtypeStruct(shape, dtype) for shape, dtype in outs]
    return pl.pallas_call(
        kernel,
        out_shape=shapes,
        in_specs=specs or [VMEM_SPEC] * len(args),
        out_specs=[VMEM_SPEC] * len(shapes),
        scratch_shapes=list(scratch),
        compiler_params=pltpu.CompilerParams(vmem_limit_bytes=limit * MIB),
        cost_estimate=pl.CostEstimate(flops=flops, bytes_accessed=moved, transcendentals=0),
        name=name,
    )(*args)


def column(row_ref, count):
    across = lax.broadcasted_iota(jnp.int32, (count, count), 1)
    down = lax.broadcasted_iota(jnp.int32, (count, count), 0)
    spread = jnp.broadcast_to(row_ref[...], (count, count))
    return jnp.sum(jnp.where(across == down, spread, jnp.zeros_like(spread)), axis=1, keepdims=True)


def tag_kernel(capacity, group_ref, local_ref, out_ref):
    count = out_ref.shape[0]
    across = lax.broadcasted_iota(jnp.int32, (count, count), 1)
    down = lax.broadcasted_iota(jnp.int32, (count, count), 0)
    group_down = column(group_ref, count)
    local_down = column(local_ref, count)
    before = (jnp.broadcast_to(group_ref[...], (count, count)) == group_down) & (across < down)
    slot = group_down * capacity + jnp.sum(jnp.where(before, 1, 0), axis=1, keepdims=True)
    lane = lax.broadcasted_iota(jnp.int32, (count, LANES), 1)
    tags = jnp.where(lane == 0, slot, jnp.where(lane == 1, local_down + 1, 0))
    out_ref[...] = tags.astype(F32).astype(BF16)


def stack_kernel(owners, *refs):
    row_refs, tag_refs, out_refs = refs[:owners], refs[owners : 2 * owners], refs[2 * owners + 1 :]
    count = row_refs[0].shape[0]
    for which in range(owners):
        here = slice(which * count, (which + 1) * count)
        start = 0
        for part, out_ref in enumerate(out_refs):
            width = out_ref.shape[1] - (LANES if part == 0 else 0)
            out_ref[here, :width] = row_refs[which][:, start : start + width]
            start += width
        out_refs[0][here, out_refs[0].shape[1] - LANES :] = tag_refs[which][...]


def pack_first_kernel(capacity, owners, blocks, *refs):
    row_refs = refs[:blocks]
    own_ref, other_ref, onehot_ref = refs[blocks:]
    me = lax.axis_index("group")
    rows, full = row_refs[0].shape
    count = rows // owners
    block = owners * capacity
    col = lax.broadcasted_iota(jnp.int32, (rows, 2 * block), 1)
    owner_col = (col % block) // capacity
    owner_row = lax.broadcasted_iota(jnp.int32, (rows, 2 * block), 0) // count
    wanted = (me ^ (col // block)) * capacity + col % capacity
    for which, ref in enumerate(row_refs):
        slot = ref[:, full - LANES :].astype(F32)[:, 0:1].astype(jnp.int32)
        onehot = ((slot == wanted) & (owner_col == owner_row)).astype(F32).astype(BF16)
        onehot_ref[which * rows : (which + 1) * rows, :] = onehot
        packed = lax.dot_general(
            onehot, ref[...], (((0,), (0,)), ((), ())), preferred_element_type=F32
        ).astype(BF16)
        own_ref[which * block : (which + 1) * block, :] = packed[:block]
        other_ref[which * block : (which + 1) * block, :] = packed[block:]


def pack_next_kernel(blocks, *refs):
    row_refs = refs[:blocks]
    onehot_ref, own_ref, other_ref = refs[blocks:]
    rows = row_refs[0].shape[0]
    block = onehot_ref.shape[1] // 2
    for which, ref in enumerate(row_refs):
        packed = lax.dot_general(
            onehot_ref[which * rows : (which + 1) * rows, :],
            ref[...],
            (((0,), (0,)), ((), ())),
            preferred_element_type=F32,
        ).astype(BF16)
        own_ref[which * block : (which + 1) * block, :] = packed[:block]
        other_ref[which * block : (which + 1) * block, :] = packed[block:]


def load_kernel(after_ref, weight_ref, held_ref, token_ref, sem):
    copies = [
        pltpu.make_async_copy(weight_ref.at[e], held_ref.at[e], sem.at[e])
        for e in range(weight_ref.shape[0])
    ]
    for copy in copies:
        copy.start()
    token_ref[...] = jnp.zeros_like(token_ref)
    for copy in copies:
        copy.wait()


def up_product(own_ref, other_ref, up_ref, expert, start, width, cols):
    rows = jnp.concatenate([own_ref[:, :width], other_ref[:, :width]], axis=0)
    return jnp.dot(rows, up_ref[expert, start : start + width, cols], preferred_element_type=F32)


def up_first_kernel(step, width, own_ref, other_ref, up_ref, acc_ref):
    experts, _, units = up_ref.shape
    for expert in range(experts):
        for at in range(0, units, step):
            acc_ref[:, expert * units + at : expert * units + at + step] = up_product(
                own_ref, other_ref, up_ref, expert, 0, width, slice(at, at + step)
            )


def up_last_kernel(step, start, width, own_tag, other_tag, own_ref, other_ref, up_ref, acc_ref, hidden_ref):
    experts, _, units = up_ref.shape
    full = own_tag.shape[1]
    chosen = jnp.concatenate(
        [own_tag[:, full - LANES :].astype(F32)[:, 1:2], other_tag[:, full - LANES :].astype(F32)[:, 1:2]],
        axis=0,
    )
    for expert in range(experts):
        mine = chosen == float(expert + 1)
        for at in range(0, units, step):
            cols = slice(expert * units + at, expert * units + at + step)
            value = acc_ref[:, cols] + up_product(
                own_ref, other_ref, up_ref, expert, start, width, slice(at, at + step)
            )
            value = jnp.where(mine, value / (1.0 + jnp.exp(-value)), 0.0)
            hidden_ref[:, cols] = value.astype(BF16)


def down_kernel(step, start, width, hidden_ref, down_ref, own_ref, other_ref):
    experts, units, _ = down_ref.shape
    half = own_ref.shape[0]
    for at in range(0, width, step):
        total = None
        for expert in range(experts):
            term = jnp.dot(
                hidden_ref[:, expert * units : (expert + 1) * units],
                down_ref[expert, :, start + at : start + at + step],
                preferred_element_type=F32,
            )
            total = term if total is None else total + term
        total = total.astype(BF16)
        own_ref[:, at : at + step] = total[:half]
        other_ref[:, at : at + step] = total[half:]


def unpack_kernel(blocks, onehot_ref, own_ref, other_ref, *out_refs):
    block = onehot_ref.shape[1] // 2
    rows = onehot_ref.shape[0] // blocks
    for which, out_ref in enumerate(out_refs):
        here = slice(which * block, (which + 1) * block)
        slots = jnp.concatenate([own_ref[here, :], other_ref[here, :]], axis=0)
        onehot = onehot_ref[which * rows : (which + 1) * rows, :]
        out_ref[...] = jnp.dot(onehot, slots, preferred_element_type=F32).astype(BF16)


def add_kernel(terms, pieces, *refs):
    outs = len(refs) // (terms + pieces)
    for which in range(outs):
        total = refs[which * terms][...].astype(F32)
        for other in range(1, terms):
            total += refs[which * terms + other][...].astype(F32)
        total = total.astype(BF16)
        count = total.shape[0] // pieces
        for piece in range(pieces):
            refs[outs * terms + which * pieces + piece][...] = total[piece * count : (piece + 1) * count]


def finish_kernel(chunks, owners, weight_ref, *refs):
    out_ref = refs[-1]
    weight = column(weight_ref, out_ref.shape[0])
    start = 0
    for chunk in range(chunks):
        parts = refs[chunk * owners : (chunk + 1) * owners]
        total = parts[0][...].astype(F32)
        for part in parts[1:]:
            total += part[...].astype(F32)
        width = total.shape[1]
        out_ref[:, start : start + width] = (total.astype(BF16).astype(F32) * weight).astype(BF16)
        start += width


def body(pair_rows, group_ids, local_ids, route_weight, w_up, w_down):
    groups = lax.axis_size("group")
    inner = lax.axis_size("inner")
    near, turns = 2, groups // 2
    far = inner // near
    count, model = pair_rows.shape
    experts, _, units = w_up.shape
    capacity = 2 * count // groups
    block = far * capacity
    blocks = turns * near
    rows = far * count
    half = blocks * block
    widths = [model // 2, model // 2]
    chunks = len(widths)
    starts = [sum(widths[:i]) for i in range(chunks)]
    step = min(256, units)

    def along_far(value, shift):
        pairs = [(a * near + b, (a ^ shift) * near + b) for a in range(far) for b in range(near)]
        return lax.ppermute(value, "inner", pairs)

    def along_near(value):
        pairs = [(a * near + b, a * near + (b ^ 1)) for a in range(far) for b in range(near)]
        return lax.ppermute(value, "inner", pairs)

    def along_group(value, flip):
        return lax.ppermute(value, "group", [(g, g ^ flip) for g in range(groups)])

    (tags,) = call(
        functools.partial(tag_kernel, capacity),
        "tag_rows",
        [((count, LANES), BF16)],
        [group_ids.reshape(1, count), local_ids.reshape(1, count)],
    )
    up_held, token = call(
        load_kernel,
        "load_weights",
        [(w_up.shape, BF16), ((8, LANES), F32)],
        [tags, w_up],
        specs=[ANY_SPEC, HBM_SPEC],
        scratch=[pltpu.SemaphoreType.DMA((experts,))],
        moved=4 * w_up.size,
        limit=47,
    )
    tag_pieces = [tags] + [along_far(tags, s) for s in range(1, far)]
    nearest, _ = lax.optimization_barrier((pair_rows, tag_pieces[-1]))
    row_pieces = [pair_rows, along_far(nearest, 1)] + [along_far(pair_rows, s) for s in range(2, far)]
    parts = call(
        functools.partial(stack_kernel, far),
        "stack_rows",
        [((rows, w + (LANES if i == 0 else 0)), BF16) for i, w in enumerate(widths)],
        [*row_pieces, *tag_pieces, token],
    )

    gathered = []
    for chunk, stacked in enumerate(parts):
        held = {(0, 0): stacked}
        if chunk % 2 == 0:
            held[0, 1] = along_near(stacked)
            for turn in range(1, turns):
                held[turn, 0] = along_group(stacked, 2 * turn)
                held[turn, 1] = along_group(held[0, 1], 2 * turn)
        else:
            for turn in range(1, turns):
                held[turn, 0] = along_group(stacked, 2 * turn)
            held[0, 1] = along_near(stacked)
            for turn in range(1, turns):
                held[turn, 1] = along_near(held[turn, 0])
        gathered.append([held[turn, swap] for turn in range(turns) for swap in range(near)])

    onehot = None
    slots = []
    for chunk, pieces in enumerate(gathered):
        wide = pieces[0].shape[1]
        outs = [((half, wide), BF16)] * 2
        if onehot is None:
            own, other, onehot = call(
                functools.partial(pack_first_kernel, capacity, far, blocks),
                "pack_first",
                outs + [((blocks * rows, 2 * block), BF16)],
                pieces,
            )
        else:
            own, other = call(
                functools.partial(pack_next_kernel, blocks), "pack_next", outs, pieces + [onehot]
            )
        slots.append((own, along_group(other, 1)))

    work = 2 * 2 * half * experts * units
    acc = call(
        functools.partial(up_first_kernel, step, widths[0]),
        "up_first",
        [((2 * half, experts * units), F32)],
        [*slots[0], up_held],
        limit=8,
        flops=work * widths[0],
    )[0]
    (hidden,) = call(
        functools.partial(up_last_kernel, step, starts[1], widths[1]),
        "up_last",
        [((2 * half, experts * units), BF16)],
        [*slots[0], *slots[1], up_held, acc],
        limit=8,
        flops=work * widths[1],
    )

    finals = []
    for chunk, width in enumerate(widths):
        own, other = call(
            functools.partial(down_kernel, min(256, width), starts[chunk], width),
            f"down_{chunk}",
            [((half, width), BF16)] * 2,
            [hidden, w_down],
            limit=8,
            flops=work * width,
        )
        back = along_group(other, 1)
        dense = call(
            functools.partial(unpack_kernel, blocks),
            "unpack_slots",
            [((rows, width), BF16)] * blocks,
            [onehot, own, back],
        )
        held = {(turn, swap): dense[turn * near + swap] for turn in range(turns) for swap in range(near)}
        if chunk % 2 == 0:
            terms = []
            for turn in reversed(range(turns)):
                terms += [held[turn, 0], along_near(held[turn, 1])]
            sums = call(
                functools.partial(add_kernel, 2, 1), "add_near", [((rows, width), BF16)] * turns, terms
            )
            last = [sums[turns - 1]] + [
                along_group(sums[turns - 1 - turn], 2 * turn) for turn in range(1, turns)
            ]
        else:
            terms = []
            for swap in reversed(range(near)):
                terms += [held[0, swap]]
                terms += [along_group(held[turn, swap], 2 * turn) for turn in range(1, turns)]
            sums = call(
                functools.partial(add_kernel, turns, 1), "add_group", [((rows, width), BF16)] * near, terms
            )
            last = [sums[1], along_near(sums[0])]
        pieces = call(
            functools.partial(add_kernel, len(last), far), "add_last", [((count, width), BF16)] * far, last
        )
        finals += [pieces[0]] + [along_far(pieces[s], s) for s in range(1, far)]

    return call(
        functools.partial(finish_kernel, chunks, far),
        "finish",
        [((count, model), BF16)],
        [route_weight.reshape(1, count), *finals],
    )[0]


def solution(mesh):
    placed = (
        P(("group", "inner"), None),
        P(("group", "inner"), None),
        P(("group", "inner"), None),
        P(("group", "inner")),
        P("group", None, "inner"),
        P("group", "inner", None),
    )
    return jax.shard_map(
        body, mesh=mesh, in_specs=placed, out_specs=P(("group", "inner"), None), check_vma=False
    )
```

```python
import functools

import jax
import jax.numpy as jnp
from jax import lax
from jax.experimental import pallas as pl
from jax.experimental.pallas import tpu as pltpu
from jax.sharding import PartitionSpec as P

LANES = 128
MIB = 2**20
BF16 = jnp.bfloat16
F32 = jnp.float32
VMEM_SPEC = pl.BlockSpec(memory_space=pltpu.VMEM)
ANY_SPEC = pl.BlockSpec(memory_space=pl.ANY)
HBM_SPEC = pl.BlockSpec(memory_space=pltpu.HBM)
SMEM_SPEC = pl.BlockSpec(memory_space=pltpu.SMEM)


def call(kernel, name, outs, args, limit=4, scratch=(), flops=0, moved=0, specs=None):
    shapes = [jax.ShapeDtypeStruct(shape, dtype) for shape, dtype in outs]
    return pl.pallas_call(
        kernel,
        out_shape=shapes,
        in_specs=specs or [VMEM_SPEC] * len(args),
        out_specs=[VMEM_SPEC] * len(shapes),
        scratch_shapes=list(scratch),
        compiler_params=pltpu.CompilerParams(vmem_limit_bytes=limit * MIB),
        cost_estimate=pl.CostEstimate(flops=flops, bytes_accessed=moved, transcendentals=0),
        name=name,
    )(*args)


def column(row_ref, count):
    across = lax.broadcasted_iota(jnp.int32, (count, count), 1)
    down = lax.broadcasted_iota(jnp.int32, (count, count), 0)
    spread = jnp.broadcast_to(row_ref[...], (count, count))
    return jnp.sum(jnp.where(across == down, spread, jnp.zeros_like(spread)), axis=1, keepdims=True)


def tag_kernel(capacity, rows_ref, group_ref, local_ref, out_ref, sem):
    count, width = rows_ref.shape
    copy = pltpu.make_async_copy(rows_ref, out_ref.at[:, :width], sem)
    copy.start()
    row = lax.broadcasted_iota(jnp.int32, (count, LANES), 0)
    lane = lax.broadcasted_iota(jnp.int32, (count, LANES), 1)
    tags = jnp.zeros((count, LANES), jnp.int32)
    names = [group_ref[0, r] for r in range(count)]
    for r in range(count):
        rank = jnp.int32(0)
        for earlier in range(r):
            rank += (names[earlier] == names[r]).astype(jnp.int32)
        tags = jnp.where((row == r) & (lane == 0), names[r] * capacity + rank, tags)
        tags = jnp.where((row == r) & (lane == 1), local_ref[0, r] + 1, tags)
    out_ref[:, width:] = tags.astype(F32).astype(BF16)
    copy.wait()


def stack_kernel(count, *refs):
    out_ref = refs[-1]
    rows = refs[0].shape[0]
    for which in range(count):
        out_ref[which * rows : (which + 1) * rows, :] = refs[which][...]


def pack_kernel(capacity, owners, start, width, first, *refs):
    held_refs = refs[:2]
    if first:
        own_ref, other_ref, onehot_ref = refs[2:]
    else:
        onehot_ref, own_ref, other_ref = refs[2:]
    block = owners * capacity
    blocks = own_ref.shape[0] // block
    rows = 2 * held_refs[0].shape[0] // blocks
    model = held_refs[0].shape[1] - LANES
    count = rows // owners
    if first:
        me = lax.axis_index("group")
        col = lax.broadcasted_iota(jnp.int32, (rows, 2 * block), 1)
        owner_col = (col % block) // capacity
        owner_row = lax.broadcasted_iota(jnp.int32, (rows, 2 * block), 0) // count
        wanted = (me ^ (col // block)) * capacity + col % capacity
    for which in range(blocks):
        ref = held_refs[2 * which // blocks]
        at = which % (blocks // 2) * rows
        here = slice(which * block, (which + 1) * block)
        if first:
            tags = ref[at : at + rows, model:]
            slot = tags.astype(F32)[:, 0:1].astype(jnp.int32)
            onehot = ((slot == wanted) & (owner_col == owner_row)).astype(F32).astype(BF16)
            onehot_ref[which * rows : (which + 1) * rows, :] = onehot
        else:
            onehot = onehot_ref[which * rows : (which + 1) * rows, :]

        def packed(value):
            return lax.dot_general(
                onehot, value, (((0,), (0,)), ((), ())), preferred_element_type=F32
            ).astype(BF16)

        value = packed(ref[at : at + rows, start : start + width])
        own_ref[here, :width] = value[:block]
        other_ref[here, :width] = value[block:]
        if first:
            value = packed(tags)
            own_ref[here, width:] = value[:block]
            other_ref[here, width:] = value[block:]


def load_kernel(after_ref, weight_ref, held_ref, token_ref, sem):
    copies = [
        pltpu.make_async_copy(weight_ref.at[e], held_ref.at[e], sem.at[e])
        for e in range(weight_ref.shape[0])
    ]
    for copy in copies:
        copy.start()
    token_ref[...] = jnp.zeros_like(token_ref)
    for copy in copies:
        copy.wait()


def up_product(own_ref, other_ref, up_ref, expert, start, width, cols):
    rows = jnp.concatenate([own_ref[:, :width], other_ref[:, :width]], axis=0)
    return jnp.dot(rows, up_ref[expert, start : start + width, cols], preferred_element_type=F32)


def up_first_kernel(step, width, own_ref, other_ref, up_ref, acc_ref):
    experts, _, units = up_ref.shape
    for expert in range(experts):
        for at in range(0, units, step):
            acc_ref[:, expert * units + at : expert * units + at + step] = up_product(
                own_ref, other_ref, up_ref, expert, 0, width, slice(at, at + step)
            )


def up_last_kernel(step, start, width, own_tag, other_tag, own_ref, other_ref, up_ref, acc_ref, hidden_ref):
    experts, _, units = up_ref.shape
    full = own_tag.shape[1]
    chosen = jnp.concatenate(
        [own_tag[:, full - LANES :].astype(F32)[:, 1:2], other_tag[:, full - LANES :].astype(F32)[:, 1:2]],
        axis=0,
    )
    for expert in range(experts):
        mine = chosen == float(expert + 1)
        for at in range(0, units, step):
            cols = slice(expert * units + at, expert * units + at + step)
            value = acc_ref[:, cols] + up_product(
                own_ref, other_ref, up_ref, expert, start, width, slice(at, at + step)
            )
            value = jnp.where(mine, value / (1.0 + jnp.exp(-value)), 0.0)
            hidden_ref[:, cols] = value.astype(BF16)


def down_kernel(step, start, width, hidden_ref, down_ref, own_ref, other_ref):
    experts, units, _ = down_ref.shape
    half = own_ref.shape[0]
    for at in range(0, width, step):
        total = None
        for expert in range(experts):
            term = jnp.dot(
                hidden_ref[:, expert * units : (expert + 1) * units],
                down_ref[expert, :, start + at : start + at + step],
                preferred_element_type=F32,
            )
            total = term if total is None else total + term
        total = total.astype(BF16)
        own_ref[:, at : at + step] = total[:half]
        other_ref[:, at : at + step] = total[half:]


def unpack_kernel(chunks, blocks, onehot_ref, *refs):
    out_refs = refs[2 * chunks :]
    block = onehot_ref.shape[1] // 2
    rows = onehot_ref.shape[0] // blocks
    for which in range(blocks):
        here = slice(which * block, (which + 1) * block)
        onehot = onehot_ref[which * rows : (which + 1) * rows, :]
        out_ref = out_refs[2 * which // blocks]
        at = which % (blocks // 2) * rows
        start = 0
        for chunk in range(chunks):
            own_ref, other_ref = refs[2 * chunk], refs[2 * chunk + 1]
            slots = jnp.concatenate([own_ref[here, :], other_ref[here, :]], axis=0)
            width = slots.shape[1]
            out_ref[at : at + rows, start : start + width] = jnp.dot(
                onehot, slots, preferred_element_type=F32
            ).astype(BF16)
            start += width


def add_kernel(left_ref, right_ref, *out_refs):
    total = (left_ref[...].astype(F32) + right_ref[...].astype(F32)).astype(BF16)
    count = total.shape[0] // len(out_refs)
    for piece, out_ref in enumerate(out_refs):
        out_ref[...] = total[piece * count : (piece + 1) * count]


def finish_kernel(weight_ref, *refs):
    out_ref = refs[-1]
    weight = column(weight_ref, out_ref.shape[0])
    total = refs[0][...].astype(F32)
    for ref in refs[1:-1]:
        total += ref[...].astype(F32)
    out_ref[...] = (total.astype(BF16).astype(F32) * weight).astype(BF16)


def body(pair_rows, group_ids, local_ids, route_weight, w_up, w_down):
    groups = lax.axis_size("group")
    inner = lax.axis_size("inner")
    near, turns = 2, groups // 2
    far = inner // near
    count, model = pair_rows.shape
    experts, _, units = w_up.shape
    capacity = 2 * count // groups
    block = far * capacity
    blocks = turns * near
    rows = far * count
    half = blocks * block
    widths = [model // 2, model // 2]
    chunks = len(widths)
    starts = [sum(widths[:i]) for i in range(chunks)]
    step = min(256, units)

    steps = (blocks - 1).bit_length()

    def along_far(value, shift):
        pairs = [(a * near + b, (a ^ shift) * near + b) for a in range(far) for b in range(near)]
        return lax.ppermute(value, "inner", pairs)

    def along_group(value, flip):
        return lax.ppermute(value, "group", [(g, g ^ flip) for g in range(groups)])

    def in_plane(value, step):
        pairs = []
        for g in range(groups):
            axis = (step + g % 2) % steps
            for i in range(inner):
                to = (g, i ^ 1) if axis == 0 else (g ^ (1 << axis), i)
                pairs.append((g * inner + i, to[0] * inner + to[1]))
        return lax.ppermute(value, ("group", "inner"), pairs)

    full = model + LANES
    (tagged,) = call(
        functools.partial(tag_kernel, capacity),
        "tag_rows",
        [((count, full), BF16)],
        [pair_rows, group_ids.reshape(1, count), local_ids.reshape(1, count)],
        specs=[HBM_SPEC, SMEM_SPEC, SMEM_SPEC],
        scratch=[pltpu.SemaphoreType.DMA],
        limit=56,
    )
    up_held, token = call(
        load_kernel,
        "load_weights",
        [(w_up.shape, BF16), ((8, LANES), F32)],
        [tagged, w_up],
        specs=[ANY_SPEC, HBM_SPEC],
        scratch=[pltpu.SemaphoreType.DMA((experts,))],
        moved=4 * w_up.size,
        limit=40,
    )
    pieces = [tagged] + [along_far(tagged, s) for s in range(1, far)]
    (held,) = call(
        functools.partial(stack_kernel, far), "stack_far", [((rows, full), BF16)], [*pieces, token]
    )
    for at in range(steps):
        came = in_plane(held, at)
        if at < steps - 1:
            (held,) = call(
                functools.partial(stack_kernel, 2),
                "stack_plane",
                [((2 * held.shape[0], full), BF16)],
                [held, came],
            )

    onehot = None
    slots = []
    for chunk, width in enumerate(widths):
        first = chunk == 0
        outs = [((half, width + LANES * first), BF16)] * 2
        if first:
            outs.append(((blocks * rows, 2 * block), BF16))
        packed = call(
            functools.partial(pack_kernel, capacity, far, starts[chunk], width, first),
            f"pack_{chunk}",
            outs,
            [held, came] if first else [held, came, onehot],
        )
        if first:
            onehot = packed[2]
        slots.append((packed[0], along_group(packed[1], 1)))

    work = 2 * 2 * half * experts * units
    acc = call(
        functools.partial(up_first_kernel, step, widths[0]),
        "up_first",
        [((2 * half, experts * units), F32)],
        [*slots[0], up_held],
        limit=8,
        flops=work * widths[0],
    )[0]
    (hidden,) = call(
        functools.partial(up_last_kernel, step, starts[1], widths[1]),
        "up_last",
        [((2 * half, experts * units), BF16)],
        [*slots[0], *slots[1], up_held, acc],
        limit=8,
        flops=work * widths[1],
    )

    partial = []
    for chunk, width in enumerate(widths):
        own, other = call(
            functools.partial(down_kernel, min(256, width), starts[chunk], width),
            f"down_{chunk}",
            [((half, width), BF16)] * 2,
            [hidden, w_down],
            limit=8,
            flops=work * width,
        )
        partial += [own, along_group(other, 1)]

    kept, sent = call(
        functools.partial(unpack_kernel, chunks, blocks),
        "unpack_slots",
        [((blocks * rows // 2, model), BF16)] * 2,
        [onehot, *partial],
    )
    for at in reversed(range(steps)):
        came = in_plane(sent, at)
        pieces = 2 if at else far
        outs = [((kept.shape[0] // pieces, model), BF16)] * pieces
        sums = call(add_kernel, "add_plane", outs, [kept, came])
        if at:
            kept, sent = sums
    parts = [sums[0]] + [along_far(sums[s], s) for s in range(1, far)]
    return call(
        finish_kernel, "finish", [((count, model), BF16)], [route_weight.reshape(1, count), *parts]
    )[0]


def solution(mesh):
    placed = (
        P(("group", "inner"), None),
        P(("group", "inner"), None),
        P(("group", "inner"), None),
        P(("group", "inner")),
        P("group", None, "inner"),
        P("group", "inner", None),
    )
    return jax.shard_map(
        body, mesh=mesh, in_specs=placed, out_specs=P(("group", "inner"), None), check_vma=False
    )
```

```python
import functools

import jax
import jax.numpy as jnp
from jax import lax
from jax.experimental import pallas as pl
from jax.experimental.pallas import tpu as pltpu
from jax.sharding import PartitionSpec as P

LANES = 128
MIB = 2**20
BF16 = jnp.bfloat16
F32 = jnp.float32
VMEM_SPEC = pl.BlockSpec(memory_space=pltpu.VMEM)
ANY_SPEC = pl.BlockSpec(memory_space=pl.ANY)
HBM_SPEC = pl.BlockSpec(memory_space=pltpu.HBM)


def call(kernel, name, outs, args, limit=4, scratch=(), flops=0, moved=0, specs=None, out_specs=None):
    shapes = [jax.ShapeDtypeStruct(shape, dtype) for shape, dtype in outs]
    return pl.pallas_call(
        kernel,
        out_shape=shapes,
        in_specs=specs or [VMEM_SPEC] * len(args),
        out_specs=out_specs or [VMEM_SPEC] * len(shapes),
        scratch_shapes=list(scratch),
        compiler_params=pltpu.CompilerParams(vmem_limit_bytes=limit * MIB),
        cost_estimate=pl.CostEstimate(flops=flops, bytes_accessed=moved, transcendentals=0),
        name=name,
    )(*args)


def column(row_ref, count):
    across = lax.broadcasted_iota(jnp.int32, (count, count), 1)
    down = lax.broadcasted_iota(jnp.int32, (count, count), 0)
    spread = jnp.broadcast_to(row_ref[...], (count, count))
    return jnp.sum(jnp.where(across == down, spread, jnp.zeros_like(spread)), axis=1, keepdims=True)


def tag_kernel(capacity, rows_ref, group_ref, local_ref, out_ref, group_held, local_held, tags_held, sem):
    count, width = rows_ref.shape
    copies = [
        pltpu.make_async_copy(group_ref, group_held, sem.at[0]),
        pltpu.make_async_copy(local_ref, local_held, sem.at[1]),
        pltpu.make_async_copy(rows_ref, out_ref.at[:, :width], sem.at[2]),
    ]
    for copy in copies:
        copy.start()
    across = lax.broadcasted_iota(jnp.int32, (count, count), 1)
    down = lax.broadcasted_iota(jnp.int32, (count, count), 0)
    lane = lax.broadcasted_iota(jnp.int32, (count, LANES), 1)
    copies[0].wait()
    copies[1].wait()
    group_down = column(group_held, count)
    local_down = column(local_held, count)
    before = (jnp.broadcast_to(group_held[...], (count, count)) == group_down) & (across < down)
    slot = group_down * capacity + jnp.sum(jnp.where(before, 1, 0), axis=1, keepdims=True)
    tags = jnp.where(lane == 0, slot, jnp.where(lane == 1, local_down + 1, 0))
    tags_held[...] = tags.astype(F32).astype(BF16)
    last = pltpu.make_async_copy(tags_held, out_ref.at[:, width:], sem.at[3])
    last.start()
    copies[2].wait()
    last.wait()


def stack_kernel(owners, *refs):
    out_ref = refs[-1]
    rows = refs[0].shape[0]
    for which in range(owners):
        out_ref[which * rows : (which + 1) * rows, :] = refs[which][...]


def pack_kernel(capacity, owners, blocks, start, width, first, *refs):
    if first:
        own_ref, other_ref, onehot_ref = refs[blocks + 1 :]
    else:
        onehot_ref, own_ref, other_ref = refs[blocks:]
    block = owners * capacity
    rows = refs[0].shape[0]
    model = refs[0].shape[1] - LANES
    count = rows // owners
    if first:
        me = lax.axis_index("group")
        col = lax.broadcasted_iota(jnp.int32, (rows, 2 * block), 1)
        owner_col = (col % block) // capacity
        owner_row = lax.broadcasted_iota(jnp.int32, (rows, 2 * block), 0) // count
        wanted = (me ^ (col // block)) * capacity + col % capacity
    for which in range(blocks):
        ref = refs[which]
        here = slice(which * block, (which + 1) * block)
        if first:
            tags = ref[:, model:]
            slot = tags.astype(F32)[:, 0:1].astype(jnp.int32)
            onehot = ((slot == wanted) & (owner_col == owner_row)).astype(F32).astype(BF16)
            onehot_ref[which * rows : (which + 1) * rows, :] = onehot
        else:
            onehot = onehot_ref[which * rows : (which + 1) * rows, :]

        def packed(value):
            return lax.dot_general(
                onehot, value, (((0,), (0,)), ((), ())), preferred_element_type=F32
            ).astype(BF16)

        value = packed(ref[:, start : start + width])
        own_ref[here, :width] = value[:block]
        other_ref[here, :width] = value[block:]
        if first:
            value = packed(tags)
            own_ref[here, width:] = value[:block]
            other_ref[here, width:] = value[block:]


def load_kernel(after_ref, weight_ref, held_ref, token_ref, sem):
    copies = [
        pltpu.make_async_copy(weight_ref.at[e], held_ref.at[e], sem.at[e])
        for e in range(weight_ref.shape[0])
    ]
    for copy in copies:
        copy.start()
    token_ref[...] = jnp.zeros_like(token_ref)
    for copy in copies:
        copy.wait()


def up_product(own_ref, other_ref, up_ref, expert, start, width, cols):
    rows = jnp.concatenate([own_ref[:, :width], other_ref[:, :width]], axis=0)
    return jnp.dot(rows, up_ref[expert, start : start + width, cols], preferred_element_type=F32)


def up_first_kernel(step, width, own_ref, other_ref, up_ref, acc_ref):
    experts, _, units = up_ref.shape
    for expert in range(experts):
        for at in range(0, units, step):
            acc_ref[:, expert * units + at : expert * units + at + step] = up_product(
                own_ref, other_ref, up_ref, expert, 0, width, slice(at, at + step)
            )


def up_last_kernel(step, start, width, own_tag, other_tag, own_ref, other_ref, up_ref, acc_ref, hidden_ref):
    experts, _, units = up_ref.shape
    full = own_tag.shape[1]
    chosen = jnp.concatenate(
        [own_tag[:, full - LANES :].astype(F32)[:, 1:2], other_tag[:, full - LANES :].astype(F32)[:, 1:2]],
        axis=0,
    )
    for expert in range(experts):
        mine = chosen == float(expert + 1)
        for at in range(0, units, step):
            cols = slice(expert * units + at, expert * units + at + step)
            value = acc_ref[:, cols] + up_product(
                own_ref, other_ref, up_ref, expert, start, width, slice(at, at + step)
            )
            value = jnp.where(mine, value / (1.0 + jnp.exp(-value)), 0.0)
            hidden_ref[:, cols] = value.astype(BF16)


def down_kernel(step, start, width, hidden_ref, down_ref, own_ref, other_ref):
    experts, units, _ = down_ref.shape
    half = own_ref.shape[0]
    for at in range(0, width, step):
        total = None
        for expert in range(experts):
            term = jnp.dot(
                hidden_ref[:, expert * units : (expert + 1) * units],
                down_ref[expert, :, start + at : start + at + step],
                preferred_element_type=F32,
            )
            total = term if total is None else total + term
        total = total.astype(BF16)
        own_ref[:, at : at + step] = total[:half]
        other_ref[:, at : at + step] = total[half:]


def dense_block(which, block, rows, onehot_ref, own_ref, other_ref):
    here = slice(which * block, (which + 1) * block)
    slots = jnp.concatenate([own_ref[here, :], other_ref[here, :]], axis=0)
    onehot = onehot_ref[which * rows : (which + 1) * rows, :]
    return jnp.dot(onehot, slots, preferred_element_type=F32).astype(BF16)


def unpack_kernel(blocks, onehot_ref, own_ref, other_ref, out_ref):
    block = onehot_ref.shape[1] // 2
    rows = onehot_ref.shape[0] // blocks
    for which in range(blocks):
        here = slice(which * rows, (which + 1) * rows)
        out_ref[here, :] = dense_block(which, block, rows, onehot_ref, own_ref, other_ref)


def unpack_last_kernel(onehot_ref, own_ref, other_ref, *refs):
    ready_ref, out_refs = refs[0], refs[1:]
    blocks = len(out_refs)
    block = onehot_ref.shape[1] // 2
    rows = onehot_ref.shape[0] // blocks
    width = own_ref.shape[1]
    for which, out_ref in enumerate(out_refs):
        out_ref[:, width:] = ready_ref[which * rows : (which + 1) * rows, :]
        out_ref[:, :width] = dense_block(which, block, rows, onehot_ref, own_ref, other_ref)


def add_kernel(terms, *refs):
    out_refs = refs[terms:]
    total = refs[0][...].astype(F32)
    for ref in refs[1:terms]:
        total += ref[...].astype(F32)
    total = total.astype(BF16)
    count = total.shape[0] // len(out_refs)
    for piece, out_ref in enumerate(out_refs):
        out_ref[...] = total[piece * count : (piece + 1) * count]


def finish_kernel(weight_ref, *refs):
    out_ref = refs[-1]
    weight = column(weight_ref, out_ref.shape[0])
    total = refs[0][...].astype(F32)
    for ref in refs[1:-1]:
        total += ref[...].astype(F32)
    out_ref[...] = (total.astype(BF16).astype(F32) * weight).astype(BF16)


def body(pair_rows, group_ids, local_ids, route_weight, w_up, w_down):
    groups = lax.axis_size("group")
    inner = lax.axis_size("inner")
    near, turns = 2, groups // 2
    far = inner // near
    count, model = pair_rows.shape
    experts, _, units = w_up.shape
    capacity = 2 * count // groups
    block = far * capacity
    blocks = turns * near
    rows = far * count
    half = blocks * block
    widths = [model // 2, model // 2]
    chunks = len(widths)
    starts = [sum(widths[:i]) for i in range(chunks)]
    step = min(256, units)


    def along_far(value, shift):
        pairs = [(a * near + b, (a ^ shift) * near + b) for a in range(far) for b in range(near)]
        return lax.ppermute(value, "inner", pairs)

    def along_group(value, flip):
        return lax.ppermute(value, "group", [(g, g ^ flip) for g in range(groups)])

    def in_plane(value, turn, swap):
        pairs = [
            (g * inner + i, (g ^ 2 * turn) * inner + (i ^ swap))
            for g in range(groups)
            for i in range(inner)
        ]
        return lax.ppermute(value, ("group", "inner"), pairs)

    full = model + LANES
    (tagged,) = call(
        functools.partial(tag_kernel, capacity),
        "tag_rows",
        [((count, full), BF16)],
        [pair_rows, group_ids.reshape(1, count), local_ids.reshape(1, count)],
        specs=[HBM_SPEC] * 3,
        out_specs=[HBM_SPEC],
        scratch=[pltpu.VMEM((1, count), jnp.int32)] * 2
        + [pltpu.VMEM((count, LANES), BF16), pltpu.SemaphoreType.DMA((4,))],
        limit=56,
    )
    def load(name, after, weight, limit):
        return call(
            load_kernel,
            name,
            [(weight.shape, BF16), ((8, LANES), F32)],
            [after, weight],
            specs=[ANY_SPEC, HBM_SPEC],
            scratch=[pltpu.SemaphoreType.DMA((experts,))],
            moved=4 * weight.size,
            limit=limit,
        )

    up_held, up_token = load("load_up", tagged, w_up, 40)
    pieces = [tagged] + [along_far(tagged, s) for s in range(1, far)]
    (held,) = call(
        functools.partial(stack_kernel, far), "stack_far", [((rows, full), BF16)], [*pieces, up_token]
    )
    hops = [(turn, swap) for turn in range(turns) for swap in range(near)]
    down_held, down_token = load("load_down", held, w_down, 44)
    arrived = [held] + [in_plane(held, *hop) for hop in hops[1:]]

    onehot = None
    slots = []
    for chunk, width in enumerate(widths):
        first = chunk == 0
        outs = [((half, width + LANES * first), BF16)] * 2
        if first:
            outs.append(((blocks * rows, 2 * block), BF16))
        packed = call(
            functools.partial(pack_kernel, capacity, far, blocks, starts[chunk], width, first),
            f"pack_{chunk}",
            outs,
            [*arrived, down_token] if first else [*arrived, onehot],
        )
        if first:
            onehot = packed[2]
        slots.append((packed[0], along_group(packed[1], 1)))

    work = 2 * 2 * half * experts * units
    acc = call(
        functools.partial(up_first_kernel, step, widths[0]),
        "up_first",
        [((2 * half, experts * units), F32)],
        [*slots[0], up_held],
        limit=8,
        flops=work * widths[0],
    )[0]
    (hidden,) = call(
        functools.partial(up_last_kernel, step, starts[1], widths[1]),
        "up_last",
        [((2 * half, experts * units), BF16)],
        [*slots[0], *slots[1], up_held, acc],
        limit=8,
        flops=work * widths[1],
    )

    dense = None
    for chunk in (1, 0):
        width = widths[chunk]
        own, other = call(
            functools.partial(down_kernel, min(256, width), starts[chunk], width),
            f"down_{chunk}",
            [((half, width), BF16)] * 2,
            [hidden, down_held],
            limit=8,
            flops=work * width,
        )
        back = along_group(other, 1)
        if chunk:
            dense = call(
                functools.partial(unpack_kernel, blocks),
                "unpack_slots",
                [((blocks * rows, width), BF16)],
                [onehot, own, back],
            )
        else:
            dense = call(
                unpack_last_kernel,
                "unpack_last",
                [((rows, model), BF16)] * blocks,
                [onehot, own, back, *dense],
            )
    terms = [dense[0]] + [in_plane(dense[i], *hops[i]) for i in range(blocks - 1, 0, -1)]
    sums = call(
        functools.partial(add_kernel, blocks), "add_plane", [((count, model), BF16)] * far, terms
    )
    parts = [sums[0]] + [along_far(sums[s], s) for s in range(far - 1, 0, -1)]
    return call(
        finish_kernel, "finish", [((count, model), BF16)], [route_weight.reshape(1, count), *parts]
    )[0]


def solution(mesh):
    placed = (
        P(("group", "inner"), None),
        P(("group", "inner"), None),
        P(("group", "inner"), None),
        P(("group", "inner")),
        P("group", None, "inner"),
        P("group", "inner", None),
    )
    return jax.shard_map(
        body, mesh=mesh, in_specs=placed, out_specs=P(("group", "inner"), None), check_vma=False
    )
```

```python
import functools

import jax
import jax.numpy as jnp
from jax import lax
from jax.experimental import pallas as pl
from jax.experimental.pallas import tpu as pltpu
from jax.sharding import PartitionSpec as P

LANES = 128
MIB = 2**20
BF16 = jnp.bfloat16
F32 = jnp.float32
VMEM_SPEC = pl.BlockSpec(memory_space=pltpu.VMEM)
ANY_SPEC = pl.BlockSpec(memory_space=pl.ANY)
HBM_SPEC = pl.BlockSpec(memory_space=pltpu.HBM)


def call(kernel, name, outs, args, limit=4, scratch=(), flops=0, moved=0, specs=None):
    shapes = [jax.ShapeDtypeStruct(shape, dtype) for shape, dtype in outs]
    return pl.pallas_call(
        kernel,
        out_shape=shapes,
        in_specs=specs or [VMEM_SPEC] * len(args),
        out_specs=[VMEM_SPEC] * len(shapes),
        scratch_shapes=list(scratch),
        compiler_params=pltpu.CompilerParams(vmem_limit_bytes=limit * MIB),
        cost_estimate=pl.CostEstimate(flops=flops, bytes_accessed=moved, transcendentals=0),
        name=name,
    )(*args)


def column(row_ref, count):
    across = lax.broadcasted_iota(jnp.int32, (count, count), 1)
    down = lax.broadcasted_iota(jnp.int32, (count, count), 0)
    spread = jnp.broadcast_to(row_ref[...], (count, count))
    return jnp.sum(jnp.where(across == down, spread, jnp.zeros_like(spread)), axis=1, keepdims=True)


def tag_kernel(capacity, rows_ref, group_ref, local_ref, out_ref):
    count, width = rows_ref.shape
    across = lax.broadcasted_iota(jnp.int32, (count, count), 1)
    down = lax.broadcasted_iota(jnp.int32, (count, count), 0)
    lane = lax.broadcasted_iota(jnp.int32, (count, LANES), 1)
    group_down = column(group_ref, count)
    local_down = column(local_ref, count)
    before = (jnp.broadcast_to(group_ref[...], (count, count)) == group_down) & (across < down)
    slot = group_down * capacity + jnp.sum(jnp.where(before, 1, 0), axis=1, keepdims=True)
    tags = jnp.where(lane == 0, slot, jnp.where(lane == 1, local_down + 1, 0))
    out_ref[:, :width] = rows_ref[...]
    out_ref[:, width:] = tags.astype(F32).astype(BF16)


def stack_kernel(owners, *refs):
    out_ref = refs[-1]
    rows = refs[0].shape[0]
    for which in range(owners):
        out_ref[which * rows : (which + 1) * rows, :] = refs[which][...]


def pack_kernel(capacity, owners, blocks, start, width, first, *refs):
    if first:
        own_ref, other_ref, onehot_ref = refs[blocks + 1 :]
    else:
        onehot_ref, own_ref, other_ref = refs[blocks:]
    block = owners * capacity
    rows = refs[0].shape[0]
    model = refs[0].shape[1] - LANES
    count = rows // owners
    if first:
        me = lax.axis_index("group")
        col = lax.broadcasted_iota(jnp.int32, (rows, 2 * block), 1)
        owner_col = (col % block) // capacity
        owner_row = lax.broadcasted_iota(jnp.int32, (rows, 2 * block), 0) // count
        wanted = (me ^ (col // block)) * capacity + col % capacity
    for which in range(blocks):
        ref = refs[which]
        here = slice(which * block, (which + 1) * block)
        if first:
            tags = ref[:, model:]
            slot = tags.astype(F32)[:, 0:1].astype(jnp.int32)
            onehot = ((slot == wanted) & (owner_col == owner_row)).astype(F32).astype(BF16)
            onehot_ref[which * rows : (which + 1) * rows, :] = onehot
        else:
            onehot = onehot_ref[which * rows : (which + 1) * rows, :]

        def packed(value):
            return lax.dot_general(
                onehot, value, (((0,), (0,)), ((), ())), preferred_element_type=F32
            ).astype(BF16)

        value = packed(ref[:, start : start + width])
        own_ref[here, :width] = value[:block]
        other_ref[here, :width] = value[block:]
        if first:
            value = packed(tags)
            own_ref[here, width:] = value[:block]
            other_ref[here, width:] = value[block:]


def load_kernel(after_ref, weight_ref, held_ref, token_ref, sem):
    copies = [
        pltpu.make_async_copy(weight_ref.at[e], held_ref.at[e], sem.at[e])
        for e in range(weight_ref.shape[0])
    ]
    for copy in copies:
        copy.start()
    token_ref[...] = jnp.zeros_like(token_ref)
    for copy in copies:
        copy.wait()


def up_product(own_ref, other_ref, up_ref, expert, start, width, cols):
    rows = jnp.concatenate([own_ref[:, :width], other_ref[:, :width]], axis=0)
    return jnp.dot(rows, up_ref[expert, start : start + width, cols], preferred_element_type=F32)


def up_first_kernel(step, width, own_ref, other_ref, up_ref, acc_ref):
    experts, _, units = up_ref.shape
    for expert in range(experts):
        for at in range(0, units, step):
            acc_ref[:, expert * units + at : expert * units + at + step] = up_product(
                own_ref, other_ref, up_ref, expert, 0, width, slice(at, at + step)
            )


def up_last_kernel(step, start, width, own_tag, other_tag, own_ref, other_ref, up_ref, acc_ref, hidden_ref):
    experts, _, units = up_ref.shape
    full = own_tag.shape[1]
    chosen = jnp.concatenate(
        [own_tag[:, full - LANES :].astype(F32)[:, 1:2], other_tag[:, full - LANES :].astype(F32)[:, 1:2]],
        axis=0,
    )
    for expert in range(experts):
        mine = chosen == float(expert + 1)
        for at in range(0, units, step):
            cols = slice(expert * units + at, expert * units + at + step)
            value = acc_ref[:, cols] + up_product(
                own_ref, other_ref, up_ref, expert, start, width, slice(at, at + step)
            )
            value = jnp.where(mine, value / (1.0 + jnp.exp(-value)), 0.0)
            hidden_ref[:, cols] = value.astype(BF16)


def down_kernel(step, start, width, hidden_ref, down_ref, own_ref, other_ref):
    experts, units, _ = down_ref.shape
    half = own_ref.shape[0]
    for at in range(0, width, step):
        total = None
        for expert in range(experts):
            term = jnp.dot(
                hidden_ref[:, expert * units : (expert + 1) * units],
                down_ref[expert, :, start + at : start + at + step],
                preferred_element_type=F32,
            )
            total = term if total is None else total + term
        total = total.astype(BF16)
        own_ref[:, at : at + step] = total[:half]
        other_ref[:, at : at + step] = total[half:]


def dense_block(which, block, rows, onehot_ref, own_ref, other_ref):
    here = slice(which * block, (which + 1) * block)
    slots = jnp.concatenate([own_ref[here, :], other_ref[here, :]], axis=0)
    onehot = onehot_ref[which * rows : (which + 1) * rows, :]
    return jnp.dot(onehot, slots, preferred_element_type=F32).astype(BF16)


def unpack_kernel(onehot_ref, own_ref, other_ref, *out_refs):
    block = onehot_ref.shape[1] // 2
    rows = out_refs[0].shape[0]
    for which, out_ref in enumerate(out_refs):
        here = slice(which * block, (which + 1) * block)
        slots = jnp.concatenate([own_ref[here, :], other_ref[here, :]], axis=0)
        onehot = onehot_ref[which * rows : (which + 1) * rows, :]
        out_ref[...] = jnp.dot(onehot, slots, preferred_element_type=F32).astype(BF16)


def add_kernel(chunks, terms, *refs):
    out_refs = refs[chunks * terms :]
    count = out_refs[0].shape[0]
    start = 0
    for chunk in range(chunks):
        blocks = refs[chunk * terms : (chunk + 1) * terms]
        total = blocks[0][...].astype(F32)
        for ref in blocks[1:]:
            total += ref[...].astype(F32)
        total = total.astype(BF16)
        width = total.shape[1]
        for piece, out_ref in enumerate(out_refs):
            out_ref[:, start : start + width] = total[piece * count : (piece + 1) * count]
        start += width


def finish_kernel(weight_ref, *refs):
    out_ref = refs[-1]
    weight = column(weight_ref, out_ref.shape[0])
    total = refs[0][...].astype(F32)
    for ref in refs[1:-1]:
        total += ref[...].astype(F32)
    out_ref[...] = (total.astype(BF16).astype(F32) * weight).astype(BF16)


def body(pair_rows, group_ids, local_ids, route_weight, w_up, w_down):
    groups = lax.axis_size("group")
    inner = lax.axis_size("inner")
    near, turns = 2, groups // 2
    far = inner // near
    count, model = pair_rows.shape
    experts, _, units = w_up.shape
    capacity = 2 * count // groups
    block = far * capacity
    blocks = turns * near
    rows = far * count
    half = blocks * block
    widths = [model // 2, model // 2]
    chunks = len(widths)
    starts = [sum(widths[:i]) for i in range(chunks)]
    step = min(256, units)


    mixed = far == blocks

    def exchange(value, wide, index):
        pairs = []
        for g in range(groups):
            for i in range(inner):
                if wide != (mixed and g % 2 == 1):
                    to = (g ^ 2 * (index // near)) * inner + (i ^ index % near)
                else:
                    to = g * inner + (i ^ near * index)
                pairs.append((g * inner + i, to))
        return lax.ppermute(value, ("group", "inner"), pairs)

    def along_group(value, flip):
        return lax.ppermute(value, "group", [(g, g ^ flip) for g in range(groups)])

    full = model + LANES
    (tagged,) = call(
        functools.partial(tag_kernel, capacity),
        "tag_rows",
        [((count, full), BF16)],
        [pair_rows, group_ids.reshape(1, count), local_ids.reshape(1, count)],
        limit=56,
    )
    def load(name, after, weight, limit):
        return call(
            load_kernel,
            name,
            [(weight.shape, BF16), ((8, LANES), F32)],
            [after, weight],
            specs=[ANY_SPEC, HBM_SPEC],
            scratch=[pltpu.SemaphoreType.DMA((experts,))],
            moved=4 * weight.size,
            limit=limit,
        )

    up_held, up_token = load("load_up", tagged, w_up, 40)
    pieces = [tagged] + [exchange(tagged, False, s) for s in range(1, far)]
    (held,) = call(
        functools.partial(stack_kernel, far), "stack_far", [((rows, full), BF16)], [*pieces, up_token]
    )
    down_held, down_token = load("load_down", held, w_down, 44)
    arrived = [held] + [exchange(held, True, s) for s in range(1, blocks)]

    onehot = None
    slots = []
    for chunk, width in enumerate(widths):
        first = chunk == 0
        outs = [((half, width + LANES * first), BF16)] * 2
        if first:
            outs.append(((blocks * rows, 2 * block), BF16))
        packed = call(
            functools.partial(pack_kernel, capacity, far, blocks, starts[chunk], width, first),
            f"pack_{chunk}",
            outs,
            [*arrived, down_token] if first else [*arrived, onehot],
        )
        if first:
            onehot = packed[2]
        slots.append((packed[0], along_group(packed[1], 1)))

    work = 2 * 2 * half * experts * units
    acc = call(
        functools.partial(up_first_kernel, step, widths[0]),
        "up_first",
        [((2 * half, experts * units), F32)],
        [*slots[0], up_held],
        limit=8,
        flops=work * widths[0],
    )[0]
    (hidden,) = call(
        functools.partial(up_last_kernel, step, starts[1], widths[1]),
        "up_last",
        [((2 * half, experts * units), BF16)],
        [*slots[0], *slots[1], up_held, acc],
        limit=8,
        flops=work * widths[1],
    )

    terms = [None] * chunks
    for chunk in reversed(range(chunks)):
        width = widths[chunk]
        own, other = call(
            functools.partial(down_kernel, min(256, width), starts[chunk], width),
            f"down_{chunk}",
            [((half, width), BF16)] * 2,
            [hidden, down_held],
            limit=8,
            flops=work * width,
        )
        dense = call(
            unpack_kernel,
            "unpack_slots",
            [((rows, width), BF16)] * blocks,
            [onehot, own, along_group(other, 1)],
        )
        terms[chunk] = [dense[0]] + [exchange(dense[s], True, s) for s in range(blocks - 1, 0, -1)]
    sums = call(
        functools.partial(add_kernel, chunks, blocks),
        "add_plane",
        [((count, model), BF16)] * far,
        sum(terms, []),
    )
    parts = [sums[0]] + [exchange(sums[s], False, s) for s in range(far - 1, 0, -1)]
    return call(
        finish_kernel, "finish", [((count, model), BF16)], [route_weight.reshape(1, count), *parts]
    )[0]


def solution(mesh):
    placed = (
        P(("group", "inner"), None),
        P(("group", "inner"), None),
        P(("group", "inner"), None),
        P(("group", "inner")),
        P("group", None, "inner"),
        P("group", "inner", None),
    )
    return jax.shard_map(
        body, mesh=mesh, in_specs=placed, out_specs=P(("group", "inner"), None), check_vma=False
    )
```

```python
import functools

import jax
import jax.numpy as jnp
from jax import lax
from jax.experimental import pallas as pl
from jax.experimental.pallas import tpu as pltpu
from jax.sharding import PartitionSpec as P

LANES = 128
HOLD_FLOPS = 6 * 10**9
MIB = 2**20
BF16 = jnp.bfloat16
F32 = jnp.float32
VMEM_SPEC = pl.BlockSpec(memory_space=pltpu.VMEM)
ANY_SPEC = pl.BlockSpec(memory_space=pl.ANY)
HBM_SPEC = pl.BlockSpec(memory_space=pltpu.HBM)


def call(kernel, name, outs, args, limit=4, scratch=(), flops=0, moved=0, specs=None):
    shapes = [jax.ShapeDtypeStruct(shape, dtype) for shape, dtype in outs]
    return pl.pallas_call(
        kernel,
        out_shape=shapes,
        in_specs=specs or [VMEM_SPEC] * len(args),
        out_specs=[VMEM_SPEC] * len(shapes),
        scratch_shapes=list(scratch),
        compiler_params=pltpu.CompilerParams(vmem_limit_bytes=limit * MIB),
        cost_estimate=pl.CostEstimate(flops=flops, bytes_accessed=moved, transcendentals=0),
        name=name,
    )(*args)


def column(row_ref, count):
    across = lax.broadcasted_iota(jnp.int32, (count, count), 1)
    down = lax.broadcasted_iota(jnp.int32, (count, count), 0)
    spread = jnp.broadcast_to(row_ref[...], (count, count))
    return jnp.sum(jnp.where(across == down, spread, jnp.zeros_like(spread)), axis=1, keepdims=True)


def tag_kernel(capacity, rows_ref, group_ref, local_ref, out_ref):
    count, width = rows_ref.shape
    across = lax.broadcasted_iota(jnp.int32, (count, count), 1)
    down = lax.broadcasted_iota(jnp.int32, (count, count), 0)
    lane = lax.broadcasted_iota(jnp.int32, (count, LANES), 1)
    group_down = column(group_ref, count)
    local_down = column(local_ref, count)
    before = (jnp.broadcast_to(group_ref[...], (count, count)) == group_down) & (across < down)
    slot = group_down * capacity + jnp.sum(jnp.where(before, 1, 0), axis=1, keepdims=True)
    tags = jnp.where(lane == 0, slot, jnp.where(lane == 1, local_down + 1, 0))
    out_ref[:, :width] = rows_ref[...]
    out_ref[:, width:] = tags.astype(F32).astype(BF16)


def stack_kernel(owners, *refs):
    whole_ref, out_refs = refs[owners], refs[owners + 1 :]
    count, full = refs[0].shape
    for which in range(owners):
        here = slice(which * count, (which + 1) * count)
        whole_ref[here, :] = refs[which][...]
        start = 0
        for part, out_ref in enumerate(out_refs):
            width = out_ref.shape[1] - (LANES if part == 0 else 0)
            out_ref[here, :width] = refs[which][:, start : start + width]
            start += width
        out_refs[0][here, out_refs[0].shape[1] - LANES :] = refs[which][:, full - LANES :]


def copy_kernel(ref, out_ref):
    out_ref[...] = ref[...]


def pack_kernel(capacity, owners, blocks, start, width, first, *refs):
    if first:
        own_ref, other_ref, onehot_ref = refs[blocks:]
    else:
        onehot_ref, own_ref, other_ref = refs[blocks:]
    block = owners * capacity
    rows = refs[0].shape[0]
    count = rows // owners
    if first:
        me = lax.axis_index("group")
        col = lax.broadcasted_iota(jnp.int32, (rows, 2 * block), 1)
        owner_col = (col % block) // capacity
        owner_row = lax.broadcasted_iota(jnp.int32, (rows, 2 * block), 0) // count
        wanted = (me ^ (col // block)) * capacity + col % capacity
    for which in range(blocks):
        ref = refs[which]
        here = slice(which * block, (which + 1) * block)
        if first:
            tags = ref[:, ref.shape[1] - LANES :]
            slot = tags.astype(F32)[:, 0:1].astype(jnp.int32)
            onehot = ((slot == wanted) & (owner_col == owner_row)).astype(F32).astype(BF16)
            onehot_ref[which * rows : (which + 1) * rows, :] = onehot
        else:
            onehot = onehot_ref[which * rows : (which + 1) * rows, :]

        def packed(value):
            return lax.dot_general(
                onehot, value, (((0,), (0,)), ((), ())), preferred_element_type=F32
            ).astype(BF16)

        at = start if which == 1 else 0
        value = packed(ref[:, at : at + width])
        own_ref[here, :width] = value[:block]
        other_ref[here, :width] = value[block:]
        if first:
            value = packed(tags)
            own_ref[here, width:] = value[:block]
            other_ref[here, width:] = value[block:]


def up_product(own_ref, other_ref, up_ref, expert, start, width, cols):
    rows = jnp.concatenate([own_ref[:, :width], other_ref[:, :width]], axis=0)
    return jnp.dot(rows, up_ref[expert, start : start + width, cols], preferred_element_type=F32)


def up_first_kernel(step, width, own_ref, other_ref, up_ref, acc_ref):
    experts, _, units = up_ref.shape
    for expert in range(experts):
        for at in range(0, units, step):
            acc_ref[:, expert * units + at : expert * units + at + step] = up_product(
                own_ref, other_ref, up_ref, expert, 0, width, slice(at, at + step)
            )


def up_last_kernel(step, start, width, own_tag, other_tag, own_ref, other_ref, up_ref, acc_ref, hidden_ref):
    experts, _, units = up_ref.shape
    full = own_tag.shape[1]
    chosen = jnp.concatenate(
        [own_tag[:, full - LANES :].astype(F32)[:, 1:2], other_tag[:, full - LANES :].astype(F32)[:, 1:2]],
        axis=0,
    )
    for expert in range(experts):
        mine = chosen == float(expert + 1)
        for at in range(0, units, step):
            cols = slice(expert * units + at, expert * units + at + step)
            value = acc_ref[:, cols] + up_product(
                own_ref, other_ref, up_ref, expert, start, width, slice(at, at + step)
            )
            value = jnp.where(mine, value / (1.0 + jnp.exp(-value)), 0.0)
            hidden_ref[:, cols] = value.astype(BF16)


def down_kernel(step, start, width, hidden_ref, down_ref, own_ref, other_ref):
    experts, units, _ = down_ref.shape
    half = own_ref.shape[0]
    for at in range(0, width, step):
        total = None
        for expert in range(experts):
            term = jnp.dot(
                hidden_ref[:, expert * units : (expert + 1) * units],
                down_ref[expert, :, start + at : start + at + step],
                preferred_element_type=F32,
            )
            total = term if total is None else total + term
        total = total.astype(BF16)
        own_ref[:, at : at + step] = total[:half]
        other_ref[:, at : at + step] = total[half:]


def dense_block(which, block, rows, onehot_ref, own_ref, other_ref):
    here = slice(which * block, (which + 1) * block)
    slots = jnp.concatenate([own_ref[here, :], other_ref[here, :]], axis=0)
    onehot = onehot_ref[which * rows : (which + 1) * rows, :]
    return jnp.dot(onehot, slots, preferred_element_type=F32).astype(BF16)


def unpack_kernel(onehot_ref, own_ref, other_ref, *out_refs):
    block = onehot_ref.shape[1] // 2
    rows = out_refs[0].shape[0]
    for which, out_ref in enumerate(out_refs):
        here = slice(which * block, (which + 1) * block)
        slots = jnp.concatenate([own_ref[here, :], other_ref[here, :]], axis=0)
        onehot = onehot_ref[which * rows : (which + 1) * rows, :]
        out_ref[...] = jnp.dot(onehot, slots, preferred_element_type=F32).astype(BF16)


def join_kernel(*refs):
    start = 0
    for ref in refs[:-1]:
        refs[-1][:, start : start + ref.shape[1]] = ref[...]
        start += ref.shape[1]


def pair_kernel(*refs):
    outs = len(refs) // 3
    for which in range(outs):
        left, right = refs[2 * which][...].astype(F32), refs[2 * which + 1][...].astype(F32)
        refs[2 * outs + which][...] = (left + right).astype(BF16)


def add_kernel(chunks, terms, whole_ref, *refs):
    out_refs = refs[chunks * terms :]
    count = out_refs[0].shape[0]
    start = 0
    for chunk in range(chunks):
        blocks = refs[chunk * terms : (chunk + 1) * terms]
        width = blocks[0].shape[1]
        total = whole_ref[:, start : start + width].astype(F32)
        for ref in blocks:
            total += ref[...].astype(F32)
        total = total.astype(BF16)
        for piece, out_ref in enumerate(out_refs):
            out_ref[:, start : start + width] = total[piece * count : (piece + 1) * count]
        start += width


def finish_kernel(weight_ref, *refs):
    out_ref = refs[-1]
    weight = column(weight_ref, out_ref.shape[0])
    total = refs[0][...].astype(F32)
    for ref in refs[1:-1]:
        total += ref[...].astype(F32)
    out_ref[...] = (total.astype(BF16).astype(F32) * weight).astype(BF16)


def body(pair_rows, group_ids, local_ids, route_weight, w_up, w_down):
    groups = lax.axis_size("group")
    inner = lax.axis_size("inner")
    near, turns = 2, groups // 2
    far = inner // near
    count, model = pair_rows.shape
    experts, _, units = w_up.shape
    capacity = 2 * count // groups
    block = far * capacity
    blocks = turns * near
    rows = far * count
    half = blocks * block
    widths = [model // 2, model // 2]
    chunks = len(widths)
    starts = [sum(widths[:i]) for i in range(chunks)]
    step = min(256, units)


    mixed = far == blocks

    def exchange(value, wide, index):
        far_index, plane_index = index if isinstance(index, tuple) else (index, index)
        pairs = []
        for g in range(groups):
            for i in range(inner):
                if wide != (mixed and g % 2 == 1):
                    to = (g ^ 2 * (plane_index // near)) * inner + (i ^ plane_index % near)
                else:
                    to = g * inner + (i ^ near * far_index)
                pairs.append((g * inner + i, to))
        return lax.ppermute(value, ("group", "inner"), pairs)

    over = [(2 * turn + 1, 2 * turn) for turn in range(1, turns)]

    def along_group(value, flip):
        return lax.ppermute(value, "group", [(g, g ^ flip) for g in range(groups)])

    full = model + LANES
    (tagged,) = call(
        functools.partial(tag_kernel, capacity),
        "tag_rows",
        [((count, full), BF16)],
        [pair_rows, group_ids.reshape(1, count), local_ids.reshape(1, count)],
        limit=56,
    )
    pieces = [tagged] + [exchange(tagged, False, s) for s in range(1, far)]
    def hand_on(value):
        return call(copy_kernel, "hand_on", [(value.shape, BF16)], [value], flops=HOLD_FLOPS)[0]

    whole, *parts = call(
        functools.partial(stack_kernel, far),
        "stack_far",
        [((rows, full), BF16)]
        + [((rows, w + (LANES if i == 0 else 0)), BF16) for i, w in enumerate(widths)],
        pieces,
        flops=HOLD_FLOPS,
    )
    sent = [[exchange(part, True, o) for o in over] for part in parts]
    handed = [[exchange(hand_on(came), True, 1) for came in row] for row in sent]
    beside = exchange(lax.optimization_barrier((whole, sent[0]))[0], True, 1)

    onehot = None
    slots = []
    for chunk, width in enumerate(widths):
        arrived = [parts[chunk], beside]
        for pair in zip(sent[chunk], handed[chunk]):
            arrived += pair
        first = chunk == 0
        outs = [((half, width + LANES * first), BF16)] * 2
        if first:
            outs.append(((blocks * rows, 2 * block), BF16))
        packed = call(
            functools.partial(pack_kernel, capacity, far, blocks, starts[chunk], width, first),
            f"pack_{chunk}",
            outs,
            arrived if first else [*arrived, onehot],
            flops=HOLD_FLOPS,
        )
        if first:
            onehot = packed[2]
        slots.append((packed[0], along_group(packed[1], 1)))

    work = 2 * 2 * half * experts * units
    acc = call(
        functools.partial(up_first_kernel, step, widths[0]),
        "up_first",
        [((2 * half, experts * units), F32)],
        [*slots[0], w_up],
        limit=8,
        flops=work * widths[0],
    )[0]
    (hidden,) = call(
        functools.partial(up_last_kernel, step, starts[1], widths[1]),
        "up_last",
        [((2 * half, experts * units), BF16)],
        [*slots[0], *slots[1], w_up, acc],
        limit=8,
        flops=work * widths[1],
    )

    terms, nearest = [None] * chunks, [None] * chunks
    for chunk in reversed(range(chunks)):
        width = widths[chunk]
        own, other = call(
            functools.partial(down_kernel, min(256, width), starts[chunk], width),
            f"down_{chunk}",
            [((half, width), BF16)] * 2,
            [hidden, w_down],
            limit=8,
            flops=work * width,
        )
        dense = call(
            unpack_kernel,
            "unpack_slots",
            [((rows, width), BF16)] * blocks,
            [onehot, own, along_group(other, 1)],
        )
        handed = [exchange(dense[2 * t + 1], True, 1) for t in range(1, turns)]
        pairs = sum([[dense[2 * t], handed[t - 1]] for t in range(1, turns)], [])
        pair_sums = call(
            pair_kernel, "add_pair", [((rows, width), BF16)] * (turns - 1), pairs, flops=HOLD_FLOPS
        )
        terms[chunk] = [dense[0]] + [exchange(pair_sums[t], True, over[t]) for t in range(turns - 1)]
        nearest[chunk] = dense[1]
    (whole,) = call(join_kernel, "join_near", [((rows, model), BF16)], nearest)
    sums = call(
        functools.partial(add_kernel, chunks, turns),
        "add_plane",
        [((count, model), BF16)] * far,
        [exchange(whole, True, 1)] + sum(terms, []),
    )
    parts = [sums[0]] + [exchange(sums[s], False, s) for s in range(far - 1, 0, -1)]
    return call(
        finish_kernel, "finish", [((count, model), BF16)], [route_weight.reshape(1, count), *parts]
    )[0]


def solution(mesh):
    placed = (
        P(("group", "inner"), None),
        P(("group", "inner"), None),
        P(("group", "inner"), None),
        P(("group", "inner")),
        P("group", None, "inner"),
        P("group", "inner", None),
    )
    return jax.shard_map(
        body, mesh=mesh, in_specs=placed, out_specs=P(("group", "inner"), None), check_vma=False
    )
```

```python
import functools

import jax
import jax.numpy as jnp
from jax import lax
from jax.experimental import pallas as pl
from jax.experimental.pallas import tpu as pltpu
from jax.sharding import PartitionSpec as P

LANES = 128
MIB = 2**20
BF16 = jnp.bfloat16
F32 = jnp.float32
VMEM_SPEC = pl.BlockSpec(memory_space=pltpu.VMEM)
ANY_SPEC = pl.BlockSpec(memory_space=pl.ANY)
HBM_SPEC = pl.BlockSpec(memory_space=pltpu.HBM)


def call(kernel, name, outs, args, limit=4, scratch=(), flops=0, moved=0, specs=None):
    shapes = [jax.ShapeDtypeStruct(shape, dtype) for shape, dtype in outs]
    return pl.pallas_call(
        kernel,
        out_shape=shapes,
        in_specs=specs or [VMEM_SPEC] * len(args),
        out_specs=[VMEM_SPEC] * len(shapes),
        scratch_shapes=list(scratch),
        compiler_params=pltpu.CompilerParams(vmem_limit_bytes=limit * MIB),
        cost_estimate=pl.CostEstimate(flops=flops, bytes_accessed=moved, transcendentals=0),
        name=name,
    )(*args)


def column(row_ref, count):
    across = lax.broadcasted_iota(jnp.int32, (count, count), 1)
    down = lax.broadcasted_iota(jnp.int32, (count, count), 0)
    spread = jnp.broadcast_to(row_ref[...], (count, count))
    return jnp.sum(jnp.where(across == down, spread, jnp.zeros_like(spread)), axis=1, keepdims=True)


def tag_kernel(capacity, rows_ref, group_ref, local_ref, out_ref):
    count, width = rows_ref.shape
    across = lax.broadcasted_iota(jnp.int32, (count, count), 1)
    down = lax.broadcasted_iota(jnp.int32, (count, count), 0)
    lane = lax.broadcasted_iota(jnp.int32, (count, LANES), 1)
    group_down = column(group_ref, count)
    local_down = column(local_ref, count)
    before = (jnp.broadcast_to(group_ref[...], (count, count)) == group_down) & (across < down)
    slot = group_down * capacity + jnp.sum(jnp.where(before, 1, 0), axis=1, keepdims=True)
    tags = jnp.where(lane == 0, slot, jnp.where(lane == 1, local_down + 1, 0))
    out_ref[:, :width] = rows_ref[...]
    out_ref[:, width:] = tags.astype(F32).astype(BF16)


def copy_kernel(ref, out_ref):
    out_ref[...] = ref[...]


def stack_kernel(owners, *refs):
    out_ref = refs[-1]
    rows = refs[0].shape[0]
    for which in range(owners):
        out_ref[which * rows : (which + 1) * rows, :] = refs[which][...]


def pack_kernel(capacity, owners, blocks, start, width, first, *refs):
    if first:
        own_ref, other_ref, onehot_ref = refs[blocks + 1 :]
    else:
        onehot_ref, own_ref, other_ref = refs[blocks:]
    block = owners * capacity
    rows = refs[0].shape[0]
    model = refs[0].shape[1] - LANES
    count = rows // owners
    if first:
        me = lax.axis_index("group")
        col = lax.broadcasted_iota(jnp.int32, (rows, 2 * block), 1)
        owner_col = (col % block) // capacity
        owner_row = lax.broadcasted_iota(jnp.int32, (rows, 2 * block), 0) // count
        wanted = (me ^ (col // block)) * capacity + col % capacity
    for which in range(blocks):
        ref = refs[which]
        here = slice(which * block, (which + 1) * block)
        if first:
            tags = ref[:, model:]
            slot = tags.astype(F32)[:, 0:1].astype(jnp.int32)
            onehot = ((slot == wanted) & (owner_col == owner_row)).astype(F32).astype(BF16)
            onehot_ref[which * rows : (which + 1) * rows, :] = onehot
        else:
            onehot = onehot_ref[which * rows : (which + 1) * rows, :]

        def packed(value):
            return lax.dot_general(
                onehot, value, (((0,), (0,)), ((), ())), preferred_element_type=F32
            ).astype(BF16)

        value = packed(ref[:, start : start + width])
        own_ref[here, :width] = value[:block]
        other_ref[here, :width] = value[block:]
        if first:
            value = packed(tags)
            own_ref[here, width:] = value[:block]
            other_ref[here, width:] = value[block:]


def load_kernel(after_ref, weight_ref, held_ref, token_ref, sem):
    copies = [
        pltpu.make_async_copy(weight_ref.at[e], held_ref.at[e], sem.at[e])
        for e in range(weight_ref.shape[0])
    ]
    for copy in copies:
        copy.start()
    token_ref[...] = jnp.zeros_like(token_ref)
    for copy in copies:
        copy.wait()


def up_product(own_ref, other_ref, up_ref, expert, start, width, cols):
    rows = jnp.concatenate([own_ref[:, :width], other_ref[:, :width]], axis=0)
    return jnp.dot(rows, up_ref[expert, start : start + width, cols], preferred_element_type=F32)


def up_first_kernel(step, width, own_ref, other_ref, up_ref, acc_ref):
    experts, _, units = up_ref.shape
    for expert in range(experts):
        for at in range(0, units, step):
            acc_ref[:, expert * units + at : expert * units + at + step] = up_product(
                own_ref, other_ref, up_ref, expert, 0, width, slice(at, at + step)
            )


def up_last_kernel(step, start, width, own_tag, other_tag, own_ref, other_ref, up_ref, acc_ref, hidden_ref):
    experts, _, units = up_ref.shape
    full = own_tag.shape[1]
    chosen = jnp.concatenate(
        [own_tag[:, full - LANES :].astype(F32)[:, 1:2], other_tag[:, full - LANES :].astype(F32)[:, 1:2]],
        axis=0,
    )
    for expert in range(experts):
        mine = chosen == float(expert + 1)
        for at in range(0, units, step):
            cols = slice(expert * units + at, expert * units + at + step)
            value = acc_ref[:, cols] + up_product(
                own_ref, other_ref, up_ref, expert, start, width, slice(at, at + step)
            )
            value = jnp.where(mine, value / (1.0 + jnp.exp(-value)), 0.0)
            hidden_ref[:, cols] = value.astype(BF16)


def down_kernel(step, start, width, hidden_ref, down_ref, own_ref, other_ref):
    experts, units, _ = down_ref.shape
    half = own_ref.shape[0]
    for at in range(0, width, step):
        total = None
        for expert in range(experts):
            term = jnp.dot(
                hidden_ref[:, expert * units : (expert + 1) * units],
                down_ref[expert, :, start + at : start + at + step],
                preferred_element_type=F32,
            )
            total = term if total is None else total + term
        total = total.astype(BF16)
        own_ref[:, at : at + step] = total[:half]
        other_ref[:, at : at + step] = total[half:]


def dense_block(which, block, rows, onehot_ref, own_ref, other_ref):
    here = slice(which * block, (which + 1) * block)
    slots = jnp.concatenate([own_ref[here, :], other_ref[here, :]], axis=0)
    onehot = onehot_ref[which * rows : (which + 1) * rows, :]
    return jnp.dot(onehot, slots, preferred_element_type=F32).astype(BF16)


def unpack_kernel(onehot_ref, own_ref, other_ref, *out_refs):
    block = onehot_ref.shape[1] // 2
    rows = out_refs[0].shape[0]
    for which, out_ref in enumerate(out_refs):
        here = slice(which * block, (which + 1) * block)
        slots = jnp.concatenate([own_ref[here, :], other_ref[here, :]], axis=0)
        onehot = onehot_ref[which * rows : (which + 1) * rows, :]
        out_ref[...] = jnp.dot(onehot, slots, preferred_element_type=F32).astype(BF16)


def add_kernel(chunks, terms, *refs):
    out_refs = refs[chunks * terms :]
    count = out_refs[0].shape[0]
    start = 0
    for chunk in range(chunks):
        blocks = refs[chunk * terms : (chunk + 1) * terms]
        total = blocks[0][...].astype(F32)
        for ref in blocks[1:]:
            total += ref[...].astype(F32)
        total = total.astype(BF16)
        width = total.shape[1]
        for piece, out_ref in enumerate(out_refs):
            out_ref[:, start : start + width] = total[piece * count : (piece + 1) * count]
        start += width


def finish_kernel(weight_ref, *refs):
    out_ref = refs[-1]
    weight = column(weight_ref, out_ref.shape[0])
    total = refs[0][...].astype(F32)
    for ref in refs[1:-1]:
        total += ref[...].astype(F32)
    out_ref[...] = (total.astype(BF16).astype(F32) * weight).astype(BF16)


def body(pair_rows, group_ids, local_ids, route_weight, w_up, w_down):
    groups = lax.axis_size("group")
    inner = lax.axis_size("inner")
    near, turns = 2, groups // 2
    far = inner // near
    count, model = pair_rows.shape
    experts, _, units = w_up.shape
    capacity = 2 * count // groups
    block = far * capacity
    blocks = turns * near
    rows = far * count
    half = blocks * block
    widths = [model // 2, model // 2]
    chunks = len(widths)
    starts = [sum(widths[:i]) for i in range(chunks)]
    step = min(256, units)


    mixed = far == blocks

    def exchange(value, wide, index):
        pairs = []
        for g in range(groups):
            for i in range(inner):
                if wide != (mixed and g % 2 == 1):
                    to = (g ^ 2 * (index // near)) * inner + (i ^ index % near)
                else:
                    to = g * inner + (i ^ near * index)
                pairs.append((g * inner + i, to))
        return lax.ppermute(value, ("group", "inner"), pairs)

    def along_group(value, flip):
        return lax.ppermute(value, "group", [(g, g ^ flip) for g in range(groups)])

    full = model + LANES
    (tagged,) = call(
        functools.partial(tag_kernel, capacity),
        "tag_rows",
        [((count, full), BF16)],
        [pair_rows, group_ids.reshape(1, count), local_ids.reshape(1, count)],
        limit=56,
    )
    def load(name, after, weight, limit):
        return call(
            load_kernel,
            name,
            [(weight.shape, BF16), ((8, LANES), F32)],
            [after, weight],
            specs=[ANY_SPEC, HBM_SPEC],
            scratch=[pltpu.SemaphoreType.DMA((experts,))],
            moved=4 * weight.size,
            limit=limit,
        )

    (own,) = call(copy_kernel, "hold_rows", [((count, full), BF16)], [tagged], flops=10**9)
    pieces = [exchange(tagged, False, s) for s in range(far - 1, 0, -1)] + [own]
    pieces.reverse()
    (held,) = call(
        functools.partial(stack_kernel, far), "stack_far", [((rows, full), BF16)], pieces
    )
    up_held, up_token = load("load_up", held, w_up, 38)
    down_held, down_token = load("load_down", up_token, w_down, 38)
    arrived = [held] + [exchange(held, True, s) for s in range(1, blocks)]

    onehot = None
    slots = []
    for chunk, width in enumerate(widths):
        first = chunk == 0
        outs = [((half, width + LANES * first), BF16)] * 2
        if first:
            outs.append(((blocks * rows, 2 * block), BF16))
        packed = call(
            functools.partial(pack_kernel, capacity, far, blocks, starts[chunk], width, first),
            f"pack_{chunk}",
            outs,
            [*arrived, down_token] if first else [*arrived, onehot],
        )
        if first:
            onehot = packed[2]
        slots.append((packed[0], along_group(packed[1], 1)))

    work = 2 * 2 * half * experts * units
    acc = call(
        functools.partial(up_first_kernel, step, widths[0]),
        "up_first",
        [((2 * half, experts * units), F32)],
        [*slots[0], up_held],
        limit=8,
        flops=work * widths[0],
    )[0]
    (hidden,) = call(
        functools.partial(up_last_kernel, step, starts[1], widths[1]),
        "up_last",
        [((2 * half, experts * units), BF16)],
        [*slots[0], *slots[1], up_held, acc],
        limit=8,
        flops=work * widths[1],
    )

    terms = [None] * chunks
    for chunk in reversed(range(chunks)):
        width = widths[chunk]
        own, other = call(
            functools.partial(down_kernel, min(256, width), starts[chunk], width),
            f"down_{chunk}",
            [((half, width), BF16)] * 2,
            [hidden, down_held],
            limit=8,
            flops=work * width,
        )
        dense = call(
            unpack_kernel,
            "unpack_slots",
            [((rows, width), BF16)] * blocks,
            [onehot, own, along_group(other, 1)],
        )
        terms[chunk] = [dense[0]] + [exchange(dense[s], True, s) for s in range(blocks - 1, 0, -1)]
    sums = call(
        functools.partial(add_kernel, chunks, blocks),
        "add_plane",
        [((count, model), BF16)] * far,
        sum(terms, []),
    )
    parts = [sums[0]] + [exchange(sums[s], False, s) for s in range(far - 1, 0, -1)]
    return call(
        finish_kernel, "finish", [((count, model), BF16)], [route_weight.reshape(1, count), *parts]
    )[0]


def solution(mesh):
    placed = (
        P(("group", "inner"), None),
        P(("group", "inner"), None),
        P(("group", "inner"), None),
        P(("group", "inner")),
        P("group", None, "inner"),
        P("group", "inner", None),
    )
    return jax.shard_map(
        body, mesh=mesh, in_specs=placed, out_specs=P(("group", "inner"), None), check_vma=False
    )
```

```python
import functools

import jax
import jax.numpy as jnp
from jax import lax
from jax.experimental import pallas as pl
from jax.experimental.pallas import tpu as pltpu
from jax.sharding import PartitionSpec as P

LANES = 128
MIB = 2**20
BF16 = jnp.bfloat16
F32 = jnp.float32
VMEM_SPEC = pl.BlockSpec(memory_space=pltpu.VMEM)
ANY_SPEC = pl.BlockSpec(memory_space=pl.ANY)
HBM_SPEC = pl.BlockSpec(memory_space=pltpu.HBM)


def call(kernel, name, outs, args, limit=4, scratch=(), flops=0, moved=0, specs=None):
    shapes = [jax.ShapeDtypeStruct(shape, dtype) for shape, dtype in outs]
    return pl.pallas_call(
        kernel,
        out_shape=shapes,
        in_specs=specs or [VMEM_SPEC] * len(args),
        out_specs=[VMEM_SPEC] * len(shapes),
        scratch_shapes=list(scratch),
        compiler_params=pltpu.CompilerParams(vmem_limit_bytes=limit * MIB),
        cost_estimate=pl.CostEstimate(flops=flops, bytes_accessed=moved, transcendentals=0),
        name=name,
    )(*args)


def column(row_ref, count):
    across = lax.broadcasted_iota(jnp.int32, (count, count), 1)
    down = lax.broadcasted_iota(jnp.int32, (count, count), 0)
    spread = jnp.broadcast_to(row_ref[...], (count, count))
    return jnp.sum(jnp.where(across == down, spread, jnp.zeros_like(spread)), axis=1, keepdims=True)


def tag_kernel(capacity, rows_ref, group_ref, local_ref, out_ref):
    count, width = rows_ref.shape
    across = lax.broadcasted_iota(jnp.int32, (count, count), 1)
    down = lax.broadcasted_iota(jnp.int32, (count, count), 0)
    lane = lax.broadcasted_iota(jnp.int32, (count, LANES), 1)
    group_down = column(group_ref, count)
    local_down = column(local_ref, count)
    before = (jnp.broadcast_to(group_ref[...], (count, count)) == group_down) & (across < down)
    slot = group_down * capacity + jnp.sum(jnp.where(before, 1, 0), axis=1, keepdims=True)
    tags = jnp.where(lane == 0, slot, jnp.where(lane == 1, local_down + 1, 0))
    out_ref[:, :width] = rows_ref[...]
    out_ref[:, width:] = tags.astype(F32).astype(BF16)


def copy_kernel(ref, out_ref):
    out_ref[...] = ref[...]


def stack_kernel(owners, *refs):
    out_refs = refs[owners:]
    count, full = refs[0].shape
    for which in range(owners):
        ref = refs[owners - 1 - which]
        here = slice(which * count, (which + 1) * count)
        start = 0
        for out_ref in out_refs:
            width = out_ref.shape[1] - LANES
            out_ref[here, :width] = ref[:, start : start + width]
            out_ref[here, width:] = ref[:, full - LANES :]
            start += width


def pack_kernel(capacity, owners, blocks, *refs):
    own_ref, other_ref, onehot_ref = refs[-3:]
    block = owners * capacity
    rows, full = refs[0].shape
    count = rows // owners
    me = lax.axis_index("group")
    col = lax.broadcasted_iota(jnp.int32, (rows, 2 * block), 1)
    owner_col = (col % block) // capacity
    owner_row = lax.broadcasted_iota(jnp.int32, (rows, 2 * block), 0) // count
    wanted = (me ^ (col // block)) * capacity + col % capacity
    for which in range(blocks):
        slot = refs[which][:, full - LANES :].astype(F32)[:, 0:1].astype(jnp.int32)
        onehot = ((slot == wanted) & (owner_col == owner_row)).astype(F32).astype(BF16)
        onehot_ref[which * rows : (which + 1) * rows, :] = onehot
        packed = lax.dot_general(
            onehot, refs[which][...], (((0,), (0,)), ((), ())), preferred_element_type=F32
        ).astype(BF16)
        own_ref[which * block : (which + 1) * block, :] = packed[:block]
        other_ref[which * block : (which + 1) * block, :] = packed[block:]


def load_kernel(after_ref, weight_ref, held_ref, token_ref, sem):
    copies = [
        pltpu.make_async_copy(weight_ref.at[e], held_ref.at[e], sem.at[e])
        for e in range(weight_ref.shape[0])
    ]
    for copy in copies:
        copy.start()
    token_ref[...] = jnp.zeros_like(token_ref)
    for copy in copies:
        copy.wait()


def up_product(own_ref, other_ref, up_ref, expert, start, width, cols):
    rows = jnp.concatenate([own_ref[:, :width], other_ref[:, :width]], axis=0)
    return jnp.dot(rows, up_ref[expert, start : start + width, cols], preferred_element_type=F32)


def up_first_kernel(step, width, own_ref, other_ref, up_ref, acc_ref):
    experts, _, units = up_ref.shape
    for expert in range(experts):
        for at in range(0, units, step):
            acc_ref[:, expert * units + at : expert * units + at + step] = up_product(
                own_ref, other_ref, up_ref, expert, 0, width, slice(at, at + step)
            )


def up_last_kernel(step, start, width, own_tag, other_tag, own_ref, other_ref, up_ref, acc_ref, hidden_ref):
    experts, _, units = up_ref.shape
    full = own_tag.shape[1]
    chosen = jnp.concatenate(
        [own_tag[:, full - LANES :].astype(F32)[:, 1:2], other_tag[:, full - LANES :].astype(F32)[:, 1:2]],
        axis=0,
    )
    for expert in range(experts):
        mine = chosen == float(expert + 1)
        for at in range(0, units, step):
            cols = slice(expert * units + at, expert * units + at + step)
            value = acc_ref[:, cols] + up_product(
                own_ref, other_ref, up_ref, expert, start, width, slice(at, at + step)
            )
            value = jnp.where(mine, value / (1.0 + jnp.exp(-value)), 0.0)
            hidden_ref[:, cols] = value.astype(BF16)


def down_kernel(step, start, width, hidden_ref, down_ref, own_ref, other_ref):
    experts, units, _ = down_ref.shape
    half = own_ref.shape[0]
    for at in range(0, width, step):
        total = None
        for expert in range(experts):
            term = jnp.dot(
                hidden_ref[:, expert * units : (expert + 1) * units],
                down_ref[expert, :, start + at : start + at + step],
                preferred_element_type=F32,
            )
            total = term if total is None else total + term
        total = total.astype(BF16)
        own_ref[:, at : at + step] = total[:half]
        other_ref[:, at : at + step] = total[half:]


def dense_block(which, block, rows, onehot_ref, own_ref, other_ref):
    here = slice(which * block, (which + 1) * block)
    slots = jnp.concatenate([own_ref[here, :], other_ref[here, :]], axis=0)
    onehot = onehot_ref[which * rows : (which + 1) * rows, :]
    return jnp.dot(onehot, slots, preferred_element_type=F32).astype(BF16)


def unpack_kernel(onehot_ref, own_ref, other_ref, *out_refs):
    block = onehot_ref.shape[1] // 2
    rows = out_refs[0].shape[0]
    for which, out_ref in enumerate(out_refs):
        here = slice(which * block, (which + 1) * block)
        slots = jnp.concatenate([own_ref[here, :], other_ref[here, :]], axis=0)
        onehot = onehot_ref[which * rows : (which + 1) * rows, :]
        out_ref[...] = jnp.dot(onehot, slots, preferred_element_type=F32).astype(BF16)


def add_kernel(*refs):
    total = refs[0][...].astype(F32)
    for ref in refs[1:-1]:
        total += ref[...].astype(F32)
    refs[-1][...] = total.astype(BF16)


def add_last_kernel(terms, ready_ref, *refs):
    out_refs = refs[terms:]
    total = refs[0][...].astype(F32)
    for ref in refs[1:terms]:
        total += ref[...].astype(F32)
    total = total.astype(BF16)
    count, width = out_refs[0].shape[0], total.shape[1]
    for piece, out_ref in enumerate(out_refs):
        here = slice(piece * count, (piece + 1) * count)
        out_ref[:, :width] = total[here]
        out_ref[:, width:] = ready_ref[here, :]


def finish_kernel(weight_ref, *refs):
    out_ref = refs[-1]
    weight = column(weight_ref, out_ref.shape[0])
    total = refs[0][...].astype(F32)
    for ref in refs[1:-1]:
        total += ref[...].astype(F32)
    out_ref[...] = (total.astype(BF16).astype(F32) * weight).astype(BF16)


def body(pair_rows, group_ids, local_ids, route_weight, w_up, w_down):
    groups = lax.axis_size("group")
    inner = lax.axis_size("inner")
    near, turns = 2, groups // 2
    far = inner // near
    count, model = pair_rows.shape
    experts, _, units = w_up.shape
    capacity = 2 * count // groups
    block = far * capacity
    blocks = turns * near
    rows = far * count
    half = blocks * block
    widths = [model // 2, model // 2]
    chunks = len(widths)
    starts = [sum(widths[:i]) for i in range(chunks)]
    step = min(256, units)


    mixed = far == blocks

    def exchange(value, wide, index):
        pairs = []
        for g in range(groups):
            for i in range(inner):
                if wide != (mixed and g % 2 == 1):
                    to = (g ^ 2 * (index // near)) * inner + (i ^ index % near)
                else:
                    to = g * inner + (i ^ near * index)
                pairs.append((g * inner + i, to))
        return lax.ppermute(value, ("group", "inner"), pairs)

    def along_group(value, flip):
        return lax.ppermute(value, "group", [(g, g ^ flip) for g in range(groups)])

    full = model + LANES
    (tagged,) = call(
        functools.partial(tag_kernel, capacity),
        "tag_rows",
        [((count, full), BF16)],
        [pair_rows, group_ids.reshape(1, count), local_ids.reshape(1, count)],
        limit=56,
    )
    def load(name, after, weight, limit):
        return call(
            load_kernel,
            name,
            [(weight.shape, BF16), ((8, LANES), F32)],
            [after, weight],
            specs=[ANY_SPEC, HBM_SPEC],
            scratch=[pltpu.SemaphoreType.DMA((experts,))],
            moved=4 * weight.size,
            limit=limit,
        )

    (own,) = call(copy_kernel, "hold_rows", [((count, full), BF16)], [tagged], flops=10**9)
    pieces = [exchange(tagged, False, s) for s in range(far - 1, 0, -1)] + [own]
    mine, given = call(
        functools.partial(stack_kernel, far),
        "stack_rows",
        [((rows, w + LANES), BF16) for w in widths],
        pieces,
    )
    taken = along_group(given, 1)
    up_held, up_token = load("load_up", given, w_up, 38)
    down_held, down_token = load("load_down", up_token, w_down, 38)
    packs = []
    for value, wide in ((mine, True), (taken, False)):
        arrived = [value] + [exchange(value, wide, s) for s in range(1, blocks)]
        packs.append(
            call(
                functools.partial(pack_kernel, capacity, far, blocks),
                "pack_rows",
                [((half, value.shape[1]), BF16)] * 2 + [((blocks * rows, 2 * block), BF16)],
                [*arrived, down_token],
            )
        )
    (first_own, first_sent, first_onehot), (last_own, last_sent, last_onehot) = packs
    first = [first_own, along_group(first_sent, 1)]
    last = [along_group(last_sent, 1), last_own]

    work = 2 * 2 * half * experts * units
    acc = call(
        functools.partial(up_first_kernel, step, widths[0]),
        "up_first",
        [((2 * half, experts * units), F32)],
        [*first, up_held],
        limit=8,
        flops=work * widths[0],
    )[0]
    (hidden,) = call(
        functools.partial(up_last_kernel, step, starts[1], widths[1]),
        "up_last",
        [((2 * half, experts * units), BF16)],
        [*first, *last, up_held, acc],
        limit=8,
        flops=work * widths[1],
    )

    def down(chunk):
        return call(
            functools.partial(down_kernel, min(256, widths[chunk]), starts[chunk], widths[chunk]),
            f"down_{chunk}",
            [((half, widths[chunk]), BF16)] * 2,
            [hidden, down_held],
            limit=8,
            flops=work * widths[chunk],
        )

    def unpack(onehot, kept, came):
        width = kept.shape[1]
        outs = [((rows, width), BF16)] * blocks
        return call(unpack_kernel, "unpack_slots", outs, [onehot, kept, came])

    sent, kept = down(1)
    dense = unpack(last_onehot, kept, along_group(sent, 1))
    terms = [dense[0]] + [exchange(dense[s], False, s) for s in range(blocks - 1, 0, -1)]
    (total,) = call(add_kernel, "add_second", [((rows, widths[1]), BF16)], terms)
    ready = along_group(total, 1)

    kept, sent = down(0)
    dense = unpack(first_onehot, kept, along_group(sent, 1))
    terms = [dense[0]] + [exchange(dense[s], True, s) for s in range(blocks - 1, 0, -1)]
    sums = call(
        functools.partial(add_last_kernel, blocks),
        "add_first",
        [((count, model), BF16)] * far,
        [ready, *terms],
    )
    parts = [sums[0]] + [exchange(sums[s], False, s) for s in range(far - 1, 0, -1)]
    return call(
        finish_kernel, "finish", [((count, model), BF16)], [route_weight.reshape(1, count), *parts]
    )[0]


def solution(mesh):
    placed = (
        P(("group", "inner"), None),
        P(("group", "inner"), None),
        P(("group", "inner"), None),
        P(("group", "inner")),
        P("group", None, "inner"),
        P("group", "inner", None),
    )
    return jax.shard_map(
        body, mesh=mesh, in_specs=placed, out_specs=P(("group", "inner"), None), check_vma=False
    )
```

```python
import functools

import jax
import jax.numpy as jnp
from jax import lax
from jax.experimental import pallas as pl
from jax.experimental.pallas import tpu as pltpu
from jax.sharding import PartitionSpec as P

LANES = 128
MIB = 2**20
BF16 = jnp.bfloat16
F32 = jnp.float32
VMEM_SPEC = pl.BlockSpec(memory_space=pltpu.VMEM)
ANY_SPEC = pl.BlockSpec(memory_space=pl.ANY)
HBM_SPEC = pl.BlockSpec(memory_space=pltpu.HBM)


def call(kernel, name, outs, args, limit=4, scratch=(), flops=0, moved=0, specs=None):
    shapes = [jax.ShapeDtypeStruct(shape, dtype) for shape, dtype in outs]
    return pl.pallas_call(
        kernel,
        out_shape=shapes,
        in_specs=specs or [VMEM_SPEC] * len(args),
        out_specs=[VMEM_SPEC] * len(shapes),
        scratch_shapes=list(scratch),
        compiler_params=pltpu.CompilerParams(vmem_limit_bytes=limit * MIB),
        cost_estimate=pl.CostEstimate(flops=flops, bytes_accessed=moved, transcendentals=0),
        name=name,
    )(*args)


def column(row_ref, count):
    across = lax.broadcasted_iota(jnp.int32, (count, count), 1)
    down = lax.broadcasted_iota(jnp.int32, (count, count), 0)
    spread = jnp.broadcast_to(row_ref[...], (count, count))
    return jnp.sum(jnp.where(across == down, spread, jnp.zeros_like(spread)), axis=1, keepdims=True)


def tag_kernel(capacity, after_ref, group_ref, local_ref, out_ref):
    count = out_ref.shape[0]
    across = lax.broadcasted_iota(jnp.int32, (count, count), 1)
    down = lax.broadcasted_iota(jnp.int32, (count, count), 0)
    lane = lax.broadcasted_iota(jnp.int32, (count, LANES), 1)
    group_down = column(group_ref, count)
    local_down = column(local_ref, count)
    before = (jnp.broadcast_to(group_ref[...], (count, count)) == group_down) & (across < down)
    slot = group_down * capacity + jnp.sum(jnp.where(before, 1, 0), axis=1, keepdims=True)
    tags = jnp.where(lane == 0, slot, jnp.where(lane == 1, local_down + 1, 0))
    out_ref[...] = tags.astype(F32).astype(BF16)


def copy_kernel(ref, out_ref):
    out_ref[...] = ref[...]


def stack_kernel(owners, *refs):
    tag_refs, row_refs, out_ref = refs[:owners], refs[owners : 2 * owners], refs[-1]
    count, width = row_refs[0].shape
    for which in range(owners):
        here = slice(which * count, (which + 1) * count)
        out_ref[here, :width] = row_refs[which][...]
        out_ref[here, width:] = tag_refs[which][...]


def pack_kernel(capacity, owners, blocks, start, width, first, *refs):
    if first:
        own_ref, other_ref, onehot_ref = refs[blocks + 1 :]
    else:
        onehot_ref, own_ref, other_ref = refs[blocks:]
    block = owners * capacity
    rows = refs[0].shape[0]
    model = refs[0].shape[1] - LANES
    count = rows // owners
    if first:
        me = lax.axis_index("group")
        col = lax.broadcasted_iota(jnp.int32, (rows, 2 * block), 1)
        owner_col = (col % block) // capacity
        owner_row = lax.broadcasted_iota(jnp.int32, (rows, 2 * block), 0) // count
        wanted = (me ^ (col // block)) * capacity + col % capacity
    for which in range(blocks):
        ref = refs[which]
        here = slice(which * block, (which + 1) * block)
        if first:
            tags = ref[:, model:]
            slot = tags.astype(F32)[:, 0:1].astype(jnp.int32)
            onehot = ((slot == wanted) & (owner_col == owner_row)).astype(F32).astype(BF16)
            onehot_ref[which * rows : (which + 1) * rows, :] = onehot
        else:
            onehot = onehot_ref[which * rows : (which + 1) * rows, :]

        def packed(value):
            return lax.dot_general(
                onehot, value, (((0,), (0,)), ((), ())), preferred_element_type=F32
            ).astype(BF16)

        value = packed(ref[:, start : start + width])
        own_ref[here, :width] = value[:block]
        other_ref[here, :width] = value[block:]
        if first:
            value = packed(tags)
            own_ref[here, width:] = value[:block]
            other_ref[here, width:] = value[block:]


def load_kernel(after_ref, weight_ref, held_ref, token_ref, sem):
    copies = [
        pltpu.make_async_copy(weight_ref.at[e], held_ref.at[e], sem.at[e])
        for e in range(weight_ref.shape[0])
    ]
    for copy in copies:
        copy.start()
    token_ref[...] = jnp.zeros_like(token_ref)
    for copy in copies:
        copy.wait()


def up_product(own_ref, other_ref, up_ref, expert, start, width, cols):
    rows = jnp.concatenate([own_ref[:, :width], other_ref[:, :width]], axis=0)
    return jnp.dot(rows, up_ref[expert, start : start + width, cols], preferred_element_type=F32)


def up_first_kernel(step, width, own_ref, other_ref, up_ref, acc_ref):
    experts, _, units = up_ref.shape
    for expert in range(experts):
        for at in range(0, units, step):
            acc_ref[:, expert * units + at : expert * units + at + step] = up_product(
                own_ref, other_ref, up_ref, expert, 0, width, slice(at, at + step)
            )


def up_last_kernel(step, start, width, own_tag, other_tag, own_ref, other_ref, up_ref, acc_ref, hidden_ref):
    experts, _, units = up_ref.shape
    full = own_tag.shape[1]
    chosen = jnp.concatenate(
        [own_tag[:, full - LANES :].astype(F32)[:, 1:2], other_tag[:, full - LANES :].astype(F32)[:, 1:2]],
        axis=0,
    )
    for expert in range(experts):
        mine = chosen == float(expert + 1)
        for at in range(0, units, step):
            cols = slice(expert * units + at, expert * units + at + step)
            value = acc_ref[:, cols] + up_product(
                own_ref, other_ref, up_ref, expert, start, width, slice(at, at + step)
            )
            value = jnp.where(mine, value / (1.0 + jnp.exp(-value)), 0.0)
            hidden_ref[:, cols] = value.astype(BF16)


def down_kernel(step, start, width, hidden_ref, down_ref, own_ref, other_ref):
    experts, units, _ = down_ref.shape
    half = own_ref.shape[0]
    for at in range(0, width, step):
        total = None
        for expert in range(experts):
            term = jnp.dot(
                hidden_ref[:, expert * units : (expert + 1) * units],
                down_ref[expert, :, start + at : start + at + step],
                preferred_element_type=F32,
            )
            total = term if total is None else total + term
        total = total.astype(BF16)
        own_ref[:, at : at + step] = total[:half]
        other_ref[:, at : at + step] = total[half:]


def dense_block(which, block, rows, onehot_ref, own_ref, other_ref):
    here = slice(which * block, (which + 1) * block)
    slots = jnp.concatenate([own_ref[here, :], other_ref[here, :]], axis=0)
    onehot = onehot_ref[which * rows : (which + 1) * rows, :]
    return jnp.dot(onehot, slots, preferred_element_type=F32).astype(BF16)


def unpack_kernel(onehot_ref, own_ref, other_ref, *out_refs):
    block = onehot_ref.shape[1] // 2
    rows = out_refs[0].shape[0]
    for which, out_ref in enumerate(out_refs):
        here = slice(which * block, (which + 1) * block)
        slots = jnp.concatenate([own_ref[here, :], other_ref[here, :]], axis=0)
        onehot = onehot_ref[which * rows : (which + 1) * rows, :]
        out_ref[...] = jnp.dot(onehot, slots, preferred_element_type=F32).astype(BF16)


def add_kernel(chunks, terms, *refs):
    out_refs = refs[chunks * terms :]
    count = out_refs[0].shape[0]
    start = 0
    for chunk in range(chunks):
        blocks = refs[chunk * terms : (chunk + 1) * terms]
        total = blocks[0][...].astype(F32)
        for ref in blocks[1:]:
            total += ref[...].astype(F32)
        total = total.astype(BF16)
        width = total.shape[1]
        for piece, out_ref in enumerate(out_refs):
            out_ref[:, start : start + width] = total[piece * count : (piece + 1) * count]
        start += width


def finish_kernel(weight_ref, *refs):
    out_ref = refs[-1]
    weight = column(weight_ref, out_ref.shape[0])
    total = refs[0][...].astype(F32)
    for ref in refs[1:-1]:
        total += ref[...].astype(F32)
    out_ref[...] = (total.astype(BF16).astype(F32) * weight).astype(BF16)


def body(pair_rows, group_ids, local_ids, route_weight, w_up, w_down):
    groups = lax.axis_size("group")
    inner = lax.axis_size("inner")
    near, turns = 2, groups // 2
    far = inner // near
    count, model = pair_rows.shape
    experts, _, units = w_up.shape
    capacity = 2 * count // groups
    block = far * capacity
    blocks = turns * near
    rows = far * count
    half = blocks * block
    widths = [model // 2, model // 2]
    chunks = len(widths)
    starts = [sum(widths[:i]) for i in range(chunks)]
    step = min(256, units)


    mixed = far == blocks

    def exchange(value, wide, index):
        pairs = []
        for g in range(groups):
            for i in range(inner):
                if wide != (mixed and g % 2 == 1):
                    to = (g ^ 2 * (index // near)) * inner + (i ^ index % near)
                else:
                    to = g * inner + (i ^ near * index)
                pairs.append((g * inner + i, to))
        return lax.ppermute(value, ("group", "inner"), pairs)

    def along_group(value, flip):
        return lax.ppermute(value, "group", [(g, g ^ flip) for g in range(groups)])

    full = model + LANES
    def load(name, after, weight, limit):
        return call(
            load_kernel,
            name,
            [(weight.shape, BF16), ((8, LANES), F32)],
            [after, weight],
            specs=[ANY_SPEC, HBM_SPEC],
            scratch=[pltpu.SemaphoreType.DMA((experts,))],
            moved=4 * weight.size,
            limit=limit,
        )

    (own,) = call(copy_kernel, "hold_rows", [((count, model), BF16)], [pair_rows], flops=6 * 10**9)
    (tags,) = call(
        functools.partial(tag_kernel, capacity),
        "tag_rows",
        [((count, LANES), BF16)],
        [own, group_ids.reshape(1, count), local_ids.reshape(1, count)],
    )
    row_pieces = [own] + [exchange(pair_rows, False, s) for s in range(1, far)]
    tag_pieces = [tags] + [exchange(tags, False, s) for s in range(1, far)]
    (held,) = call(
        functools.partial(stack_kernel, far),
        "stack_rows",
        [((rows, full), BF16)],
        [*tag_pieces, *row_pieces],
    )
    up_held, up_token = load("load_up", held, w_up, 38)
    down_held, down_token = load("load_down", up_token, w_down, 38)
    arrived = [held] + [exchange(held, True, s) for s in range(1, blocks)]

    onehot = None
    slots = []
    for chunk, width in enumerate(widths):
        first = chunk == 0
        outs = [((half, width + LANES * first), BF16)] * 2
        if first:
            outs.append(((blocks * rows, 2 * block), BF16))
        packed = call(
            functools.partial(pack_kernel, capacity, far, blocks, starts[chunk], width, first),
            f"pack_{chunk}",
            outs,
            [*arrived, down_token] if first else [*arrived, onehot],
        )
        if first:
            onehot = packed[2]
        slots.append((packed[0], along_group(packed[1], 1)))

    work = 2 * 2 * half * experts * units
    acc = call(
        functools.partial(up_first_kernel, step, widths[0]),
        "up_first",
        [((2 * half, experts * units), F32)],
        [*slots[0], up_held],
        limit=8,
        flops=work * widths[0],
    )[0]
    (hidden,) = call(
        functools.partial(up_last_kernel, step, starts[1], widths[1]),
        "up_last",
        [((2 * half, experts * units), BF16)],
        [*slots[0], *slots[1], up_held, acc],
        limit=8,
        flops=work * widths[1],
    )

    back_widths = [model - model // 4, model // 4]
    terms = [None] * chunks
    for chunk in reversed(range(chunks)):
        width = back_widths[chunk]
        own, other = call(
            functools.partial(down_kernel, min(256, width), chunk * back_widths[0], width),
            f"down_{chunk}",
            [((half, width), BF16)] * 2,
            [hidden, down_held],
            limit=8,
            flops=work * width,
        )
        dense = call(
            unpack_kernel,
            "unpack_slots",
            [((rows, width), BF16)] * blocks,
            [onehot, own, along_group(other, 1)],
        )
        terms[chunk] = [dense[0]] + [exchange(dense[s], True, s) for s in range(blocks - 1, 0, -1)]
    sums = call(
        functools.partial(add_kernel, chunks, blocks),
        "add_plane",
        [((count, model), BF16)] * far,
        sum(terms, []),
    )
    parts = [sums[0]] + [exchange(sums[s], False, s) for s in range(far - 1, 0, -1)]
    return call(
        finish_kernel, "finish", [((count, model), BF16)], [route_weight.reshape(1, count), *parts]
    )[0]


def solution(mesh):
    placed = (
        P(("group", "inner"), None),
        P(("group", "inner"), None),
        P(("group", "inner"), None),
        P(("group", "inner")),
        P("group", None, "inner"),
        P("group", "inner", None),
    )
    return jax.shard_map(
        body, mesh=mesh, in_specs=placed, out_specs=P(("group", "inner"), None), check_vma=False
    )
```

```python
import functools

import jax
import jax.numpy as jnp
from jax import lax
from jax.experimental import pallas as pl
from jax.experimental.pallas import tpu as pltpu
from jax.sharding import PartitionSpec as P

LANES = 128
MIB = 2**20
BF16 = jnp.bfloat16
F32 = jnp.float32
VMEM_SPEC = pl.BlockSpec(memory_space=pltpu.VMEM)
ANY_SPEC = pl.BlockSpec(memory_space=pl.ANY)
HBM_SPEC = pl.BlockSpec(memory_space=pltpu.HBM)


def call(kernel, name, outs, args, limit=4, scratch=(), flops=0, moved=0, specs=None):
    shapes = [jax.ShapeDtypeStruct(shape, dtype) for shape, dtype in outs]
    return pl.pallas_call(
        kernel,
        out_shape=shapes,
        in_specs=specs or [VMEM_SPEC] * len(args),
        out_specs=[VMEM_SPEC] * len(shapes),
        scratch_shapes=list(scratch),
        compiler_params=pltpu.CompilerParams(vmem_limit_bytes=limit * MIB),
        cost_estimate=pl.CostEstimate(flops=flops, bytes_accessed=moved, transcendentals=0),
        name=name,
    )(*args)


def column(row_ref, count):
    across = lax.broadcasted_iota(jnp.int32, (count, count), 1)
    down = lax.broadcasted_iota(jnp.int32, (count, count), 0)
    spread = jnp.broadcast_to(row_ref[...], (count, count))
    return jnp.sum(jnp.where(across == down, spread, jnp.zeros_like(spread)), axis=1, keepdims=True)


def tag_kernel(capacity, experts, rows_ref, expert_ref, out_ref):
    count, width = rows_ref.shape
    across = lax.broadcasted_iota(jnp.int32, (count, count), 1)
    down = lax.broadcasted_iota(jnp.int32, (count, count), 0)
    lane = lax.broadcasted_iota(jnp.int32, (count, LANES), 1)
    group_across = expert_ref[...] // experts
    expert_down = column(expert_ref, count)
    group_down = expert_down // experts
    before = (jnp.broadcast_to(group_across, (count, count)) == group_down) & (across < down)
    slot = group_down * capacity + jnp.sum(jnp.where(before, 1, 0), axis=1, keepdims=True)
    local_down = expert_down % experts
    tags = jnp.where(lane == 0, slot, jnp.where(lane == 1, local_down + 1, 0))
    out_ref[:, :width] = rows_ref[...]
    out_ref[:, width:] = tags.astype(F32).astype(BF16)


def stack_kernel(owners, *refs):
    out_ref = refs[-1]
    rows = refs[0].shape[0]
    for which in range(owners):
        out_ref[which * rows : (which + 1) * rows, :] = refs[which][...]


def pack_kernel(capacity, owners, blocks, start, width, first, *refs):
    if first:
        own_ref, other_ref, onehot_ref = refs[blocks + 1 :]
    else:
        onehot_ref, own_ref, other_ref = refs[blocks:]
    block = owners * capacity
    rows = refs[0].shape[0]
    model = refs[0].shape[1] - LANES
    count = rows // owners
    if first:
        me = lax.axis_index("group")
        col = lax.broadcasted_iota(jnp.int32, (rows, 2 * block), 1)
        owner_col = (col % block) // capacity
        owner_row = lax.broadcasted_iota(jnp.int32, (rows, 2 * block), 0) // count
        wanted = (me ^ (col // block)) * capacity + col % capacity
    for which in range(blocks):
        ref = refs[which]
        here = slice(which * block, (which + 1) * block)
        if first:
            tags = ref[:, model:]
            slot = tags.astype(F32)[:, 0:1].astype(jnp.int32)
            onehot = ((slot == wanted) & (owner_col == owner_row)).astype(F32).astype(BF16)
            onehot_ref[which * rows : (which + 1) * rows, :] = onehot
        else:
            onehot = onehot_ref[which * rows : (which + 1) * rows, :]

        def packed(value):
            return lax.dot_general(
                onehot, value, (((0,), (0,)), ((), ())), preferred_element_type=F32
            ).astype(BF16)

        value = packed(ref[:, start : start + width])
        own_ref[here, :width] = value[:block]
        other_ref[here, :width] = value[block:]
        if first:
            value = packed(tags)
            own_ref[here, width:] = value[:block]
            other_ref[here, width:] = value[block:]


def load_kernel(after_ref, weight_ref, held_ref, token_ref, sem):
    copies = [
        pltpu.make_async_copy(weight_ref.at[e], held_ref.at[e], sem.at[e])
        for e in range(weight_ref.shape[0])
    ]
    for copy in copies:
        copy.start()
    token_ref[...] = jnp.zeros_like(token_ref)
    for copy in copies:
        copy.wait()


def up_product(own_ref, other_ref, up_ref, expert, start, width, cols):
    rows = jnp.concatenate([own_ref[:, :width], other_ref[:, :width]], axis=0)
    return jnp.dot(rows, up_ref[expert, start : start + width, cols], preferred_element_type=F32)


def up_first_kernel(step, width, own_ref, other_ref, up_ref, acc_ref):
    experts, _, units = up_ref.shape
    for expert in range(experts):
        for at in range(0, units, step):
            acc_ref[:, expert * units + at : expert * units + at + step] = up_product(
                own_ref, other_ref, up_ref, expert, 0, width, slice(at, at + step)
            )


def up_last_kernel(step, start, width, own_tag, other_tag, own_ref, other_ref, up_ref, acc_ref, hidden_ref):
    experts, _, units = up_ref.shape
    full = own_tag.shape[1]
    chosen = jnp.concatenate(
        [own_tag[:, full - LANES :].astype(F32)[:, 1:2], other_tag[:, full - LANES :].astype(F32)[:, 1:2]],
        axis=0,
    )
    for expert in range(experts):
        mine = chosen == float(expert + 1)
        for at in range(0, units, step):
            cols = slice(expert * units + at, expert * units + at + step)
            value = acc_ref[:, cols] + up_product(
                own_ref, other_ref, up_ref, expert, start, width, slice(at, at + step)
            )
            value = jnp.where(mine, value / (1.0 + jnp.exp(-value)), 0.0)
            hidden_ref[:, cols] = value.astype(BF16)


def down_kernel(step, start, width, hidden_ref, down_ref, own_ref, other_ref):
    experts, units, _ = down_ref.shape
    half = own_ref.shape[0]
    for at in range(0, width, step):
        total = None
        for expert in range(experts):
            term = jnp.dot(
                hidden_ref[:, expert * units : (expert + 1) * units],
                down_ref[expert, :, start + at : start + at + step],
                preferred_element_type=F32,
            )
            total = term if total is None else total + term
        total = total.astype(BF16)
        own_ref[:, at : at + step] = total[:half]
        other_ref[:, at : at + step] = total[half:]


def dense_block(which, block, rows, onehot_ref, own_ref, other_ref):
    here = slice(which * block, (which + 1) * block)
    slots = jnp.concatenate([own_ref[here, :], other_ref[here, :]], axis=0)
    onehot = onehot_ref[which * rows : (which + 1) * rows, :]
    return jnp.dot(onehot, slots, preferred_element_type=F32).astype(BF16)


def unpack_kernel(onehot_ref, own_ref, other_ref, *out_refs):
    block = onehot_ref.shape[1] // 2
    rows = out_refs[0].shape[0]
    for which, out_ref in enumerate(out_refs):
        here = slice(which * block, (which + 1) * block)
        slots = jnp.concatenate([own_ref[here, :], other_ref[here, :]], axis=0)
        onehot = onehot_ref[which * rows : (which + 1) * rows, :]
        out_ref[...] = jnp.dot(onehot, slots, preferred_element_type=F32).astype(BF16)


def add_kernel(chunks, terms, *refs):
    out_refs = refs[chunks * terms :]
    count = out_refs[0].shape[0]
    start = 0
    for chunk in range(chunks):
        blocks = refs[chunk * terms : (chunk + 1) * terms]
        total = blocks[0][...].astype(F32)
        for ref in blocks[1:]:
            total += ref[...].astype(F32)
        total = total.astype(BF16)
        width = total.shape[1]
        for piece, out_ref in enumerate(out_refs):
            out_ref[:, start : start + width] = total[piece * count : (piece + 1) * count]
        start += width


def finish_kernel(weight_ref, *refs):
    out_ref = refs[-1]
    weight = column(weight_ref, out_ref.shape[0])
    total = refs[0][...].astype(F32)
    for ref in refs[1:-1]:
        total += ref[...].astype(F32)
    out_ref[...] = (total.astype(BF16).astype(F32) * weight).astype(BF16)


def body(pair_rows, group_ids, local_ids, route_weight, w_up, w_down):
    groups = lax.axis_size("group")
    inner = lax.axis_size("inner")
    near, turns = 2, groups // 2
    far = inner // near
    count, model = pair_rows.shape
    experts, _, units = w_up.shape
    capacity = 2 * count // groups
    block = far * capacity
    blocks = turns * near
    rows = far * count
    half = blocks * block
    widths = [model // 2, model // 2]
    chunks = len(widths)
    starts = [sum(widths[:i]) for i in range(chunks)]
    step = min(256, units)


    mixed = far == blocks

    def exchange(value, wide, index):
        pairs = []
        for g in range(groups):
            for i in range(inner):
                if wide != (mixed and g % 2 == 1):
                    to = (g ^ 2 * (index // near)) * inner + (i ^ index % near)
                else:
                    to = g * inner + (i ^ near * index)
                pairs.append((g * inner + i, to))
        return lax.ppermute(value, ("group", "inner"), pairs)

    def along_group(value, flip):
        return lax.ppermute(value, "group", [(g, g ^ flip) for g in range(groups)])

    full = model + LANES
    named = group_ids * experts + local_ids
    (tagged,) = call(
        functools.partial(tag_kernel, capacity, experts),
        "tag_rows",
        [((count, full), BF16)],
        [pair_rows, named.reshape(1, count)],
    )

    def load(name, after, weight, limit):
        return call(
            load_kernel,
            name,
            [(weight.shape, BF16), ((8, LANES), F32)],
            [after, weight],
            specs=[ANY_SPEC, HBM_SPEC],
            scratch=[pltpu.SemaphoreType.DMA((experts,))],
            moved=4 * weight.size,
            limit=limit,
        )

    pieces = [exchange(tagged, False, s) for s in range(far - 1, 0, -1)] + [tagged]
    pieces.reverse()
    (held,) = call(
        functools.partial(stack_kernel, far), "stack_far", [((rows, full), BF16)], pieces
    )
    up_held, up_token = load("load_up", held, w_up, 38)
    down_held, down_token = load("load_down", up_token, w_down, 38)
    arrived = [held] + [exchange(held, True, s) for s in range(1, blocks)]

    onehot = None
    slots = []
    for chunk, width in enumerate(widths):
        first = chunk == 0
        outs = [((half, width + LANES * first), BF16)] * 2
        if first:
            outs.append(((blocks * rows, 2 * block), BF16))
        packed = call(
            functools.partial(pack_kernel, capacity, far, blocks, starts[chunk], width, first),
            f"pack_{chunk}",
            outs,
            [*arrived, down_token] if first else [*arrived, onehot],
        )
        if first:
            onehot = packed[2]
        slots.append((packed[0], along_group(packed[1], 1)))

    work = 2 * 2 * half * experts * units
    acc = call(
        functools.partial(up_first_kernel, step, widths[0]),
        "up_first",
        [((2 * half, experts * units), F32)],
        [*slots[0], up_held],
        limit=8,
        flops=work * widths[0],
    )[0]
    (hidden,) = call(
        functools.partial(up_last_kernel, step, starts[1], widths[1]),
        "up_last",
        [((2 * half, experts * units), BF16)],
        [*slots[0], *slots[1], up_held, acc],
        limit=8,
        flops=work * widths[1],
    )

    terms = [None] * chunks
    for chunk in reversed(range(chunks)):
        width = widths[chunk]
        own, other = call(
            functools.partial(down_kernel, min(256, width), starts[chunk], width),
            f"down_{chunk}",
            [((half, width), BF16)] * 2,
            [hidden, down_held],
            limit=8,
            flops=work * width,
        )
        dense = call(
            unpack_kernel,
            "unpack_slots",
            [((rows, width), BF16)] * blocks,
            [onehot, own, along_group(other, 1)],
        )
        terms[chunk] = [dense[0]] + [exchange(dense[s], True, s) for s in range(blocks - 1, 0, -1)]
    sums = call(
        functools.partial(add_kernel, chunks, blocks),
        "add_plane",
        [((count, model), BF16)] * far,
        sum(terms, []),
    )
    parts = [sums[0]] + [exchange(sums[s], False, s) for s in range(far - 1, 0, -1)]
    return call(
        finish_kernel, "finish", [((count, model), BF16)], [route_weight.reshape(1, count), *parts]
    )[0]


def solution(mesh):
    placed = (
        P(("group", "inner"), None),
        P(("group", "inner"), None),
        P(("group", "inner"), None),
        P(("group", "inner")),
        P("group", None, "inner"),
        P("group", "inner", None),
    )
    return jax.shard_map(
        body, mesh=mesh, in_specs=placed, out_specs=P(("group", "inner"), None), check_vma=False
    )
```

```python
import functools

import jax
import jax.numpy as jnp
from jax import lax
from jax.experimental import pallas as pl
from jax.experimental.pallas import tpu as pltpu
from jax.sharding import PartitionSpec as P

LANES = 128
STACK_FLOPS = 6 * 10**9
PACK_FLOPS = 15 * 10**8
MIB = 2**20
BF16 = jnp.bfloat16
F32 = jnp.float32
VMEM_SPEC = pl.BlockSpec(memory_space=pltpu.VMEM)


def call(kernel, name, outs, args, limit=4, scratch=(), flops=0, moved=0, specs=None):
    shapes = [jax.ShapeDtypeStruct(shape, dtype) for shape, dtype in outs]
    return pl.pallas_call(
        kernel,
        out_shape=shapes,
        in_specs=specs or [VMEM_SPEC] * len(args),
        out_specs=[VMEM_SPEC] * len(shapes),
        scratch_shapes=list(scratch),
        compiler_params=pltpu.CompilerParams(vmem_limit_bytes=limit * MIB),
        cost_estimate=pl.CostEstimate(flops=flops, bytes_accessed=moved, transcendentals=0),
        name=name,
    )(*args)


def column(row_ref, count):
    across = lax.broadcasted_iota(jnp.int32, (count, count), 1)
    down = lax.broadcasted_iota(jnp.int32, (count, count), 0)
    spread = jnp.broadcast_to(row_ref[...], (count, count))
    return jnp.sum(jnp.where(across == down, spread, jnp.zeros_like(spread)), axis=1, keepdims=True)


def tag_kernel(capacity, experts, rows_ref, expert_ref, out_ref):
    count, width = rows_ref.shape
    across = lax.broadcasted_iota(jnp.int32, (count, count), 1)
    down = lax.broadcasted_iota(jnp.int32, (count, count), 0)
    lane = lax.broadcasted_iota(jnp.int32, (count, LANES), 1)
    group_across = expert_ref[...] // experts
    expert_down = column(expert_ref, count)
    group_down = expert_down // experts
    before = (jnp.broadcast_to(group_across, (count, count)) == group_down) & (across < down)
    slot = group_down * capacity + jnp.sum(jnp.where(before, 1, 0), axis=1, keepdims=True)
    local_down = expert_down % experts
    tags = jnp.where(lane == 0, slot, jnp.where(lane == 1, local_down + 1, 0))
    out_ref[:, :width] = rows_ref[...]
    out_ref[:, width:] = tags.astype(F32).astype(BF16)


def stack_kernel(owners, *refs):
    out_refs = refs[owners:]
    count, full = refs[0].shape
    for which in range(owners):
        here = slice(which * count, (which + 1) * count)
        start = 0
        for part, out_ref in enumerate(out_refs):
            width = out_ref.shape[1] - (LANES if part == 0 else 0)
            out_ref[here, :width] = refs[which][:, start : start + width]
            start += width
        out_refs[0][here, out_refs[0].shape[1] - LANES :] = refs[which][:, full - LANES :]


def pack_kernel(capacity, owners, blocks, width, first, *refs):
    if first:
        own_ref, other_ref, onehot_ref = refs[blocks:]
    else:
        onehot_ref, own_ref, other_ref = refs[blocks:]
    block = owners * capacity
    rows = refs[0].shape[0]
    count = rows // owners
    if first:
        me = lax.axis_index("group")
        col = lax.broadcasted_iota(jnp.int32, (rows, 2 * block), 1)
        owner_col = (col % block) // capacity
        owner_row = lax.broadcasted_iota(jnp.int32, (rows, 2 * block), 0) // count
        wanted = (me ^ (col // block)) * capacity + col % capacity
    for which in range(blocks):
        ref = refs[which]
        here = slice(which * block, (which + 1) * block)
        if first:
            tags = ref[:, width:]
            slot = tags.astype(F32)[:, 0:1].astype(jnp.int32)
            onehot = ((slot == wanted) & (owner_col == owner_row)).astype(F32).astype(BF16)
            onehot_ref[which * rows : (which + 1) * rows, :] = onehot
        else:
            onehot = onehot_ref[which * rows : (which + 1) * rows, :]

        def packed(value):
            return lax.dot_general(
                onehot, value, (((0,), (0,)), ((), ())), preferred_element_type=F32
            ).astype(BF16)

        value = packed(ref[:, :width])
        own_ref[here, :width] = value[:block]
        other_ref[here, :width] = value[block:]
        if first:
            value = packed(tags)
            own_ref[here, width:] = value[:block]
            other_ref[here, width:] = value[block:]


def up_product(own_ref, other_ref, up_ref, expert, start, width, cols):
    rows = jnp.concatenate([own_ref[:, :width], other_ref[:, :width]], axis=0)
    return jnp.dot(rows, up_ref[expert, start : start + width, cols], preferred_element_type=F32)


def up_first_kernel(step, width, own_ref, other_ref, up_ref, acc_ref):
    experts, _, units = up_ref.shape
    for expert in range(experts):
        for at in range(0, units, step):
            acc_ref[:, expert * units + at : expert * units + at + step] = up_product(
                own_ref, other_ref, up_ref, expert, 0, width, slice(at, at + step)
            )


def up_last_kernel(step, start, width, own_tag, other_tag, own_ref, other_ref, up_ref, acc_ref, hidden_ref):
    experts, _, units = up_ref.shape
    full = own_tag.shape[1]
    chosen = jnp.concatenate(
        [own_tag[:, full - LANES :].astype(F32)[:, 1:2], other_tag[:, full - LANES :].astype(F32)[:, 1:2]],
        axis=0,
    )
    for expert in range(experts):
        mine = chosen == float(expert + 1)
        for at in range(0, units, step):
            cols = slice(expert * units + at, expert * units + at + step)
            value = acc_ref[:, cols] + up_product(
                own_ref, other_ref, up_ref, expert, start, width, slice(at, at + step)
            )
            value = jnp.where(mine, value / (1.0 + jnp.exp(-value)), 0.0)
            hidden_ref[:, cols] = value.astype(BF16)


def down_kernel(step, start, width, hidden_ref, down_ref, own_ref, other_ref):
    experts, units, _ = down_ref.shape
    half = own_ref.shape[0]
    for at in range(0, width, step):
        total = None
        for expert in range(experts):
            term = jnp.dot(
                hidden_ref[:, expert * units : (expert + 1) * units],
                down_ref[expert, :, start + at : start + at + step],
                preferred_element_type=F32,
            )
            total = term if total is None else total + term
        total = total.astype(BF16)
        own_ref[:, at : at + step] = total[:half]
        other_ref[:, at : at + step] = total[half:]


def dense_block(which, block, rows, onehot_ref, own_ref, other_ref):
    here = slice(which * block, (which + 1) * block)
    slots = jnp.concatenate([own_ref[here, :], other_ref[here, :]], axis=0)
    onehot = onehot_ref[which * rows : (which + 1) * rows, :]
    return jnp.dot(onehot, slots, preferred_element_type=F32).astype(BF16)


def unpack_kernel(onehot_ref, own_ref, other_ref, *out_refs):
    block = onehot_ref.shape[1] // 2
    rows = out_refs[0].shape[0]
    for which, out_ref in enumerate(out_refs):
        here = slice(which * block, (which + 1) * block)
        slots = jnp.concatenate([own_ref[here, :], other_ref[here, :]], axis=0)
        onehot = onehot_ref[which * rows : (which + 1) * rows, :]
        out_ref[...] = jnp.dot(onehot, slots, preferred_element_type=F32).astype(BF16)


def add_kernel(chunks, terms, *refs):
    out_refs = refs[chunks * terms :]
    count = out_refs[0].shape[0]
    start = 0
    for chunk in range(chunks):
        blocks = refs[chunk * terms : (chunk + 1) * terms]
        total = blocks[0][...].astype(F32)
        for ref in blocks[1:]:
            total += ref[...].astype(F32)
        total = total.astype(BF16)
        width = total.shape[1]
        for piece, out_ref in enumerate(out_refs):
            out_ref[:, start : start + width] = total[piece * count : (piece + 1) * count]
        start += width


def finish_kernel(weight_ref, *refs):
    out_ref = refs[-1]
    weight = column(weight_ref, out_ref.shape[0])
    total = refs[0][...].astype(F32)
    for ref in refs[1:-1]:
        total += ref[...].astype(F32)
    out_ref[...] = (total.astype(BF16).astype(F32) * weight).astype(BF16)


def body(pair_rows, group_ids, local_ids, route_weight, w_up, w_down):
    groups = lax.axis_size("group")
    inner = lax.axis_size("inner")
    near, turns = 2, groups // 2
    far = inner // near
    count, model = pair_rows.shape
    experts, _, units = w_up.shape
    capacity = 2 * count // groups
    block = far * capacity
    blocks = turns * near
    rows = far * count
    half = blocks * block
    widths = [model // 2, model // 2]
    chunks = len(widths)
    starts = [sum(widths[:i]) for i in range(chunks)]
    step = min(256, units)


    mixed = far == blocks

    def exchange(value, wide, index):
        pairs = []
        for g in range(groups):
            for i in range(inner):
                if wide != (mixed and g % 2 == 1):
                    to = (g ^ 2 * (index // near)) * inner + (i ^ index % near)
                else:
                    to = g * inner + (i ^ near * index)
                pairs.append((g * inner + i, to))
        return lax.ppermute(value, ("group", "inner"), pairs)

    def along_group(value, flip):
        return lax.ppermute(value, "group", [(g, g ^ flip) for g in range(groups)])

    full = model + LANES
    named = group_ids * experts + local_ids
    (tagged,) = call(
        functools.partial(tag_kernel, capacity, experts),
        "tag_rows",
        [((count, full), BF16)],
        [pair_rows, named.reshape(1, count)],
    )

    pieces = [exchange(tagged, False, s) for s in range(far - 1, 0, -1)] + [tagged]
    pieces.reverse()
    parts = call(
        functools.partial(stack_kernel, far),
        "stack_rows",
        [((rows, w + (LANES if i == 0 else 0)), BF16) for i, w in enumerate(widths)],
        pieces,
        flops=STACK_FLOPS,
    )

    onehot = None
    slots = []
    for chunk, width in enumerate(widths):
        first = chunk == 0
        arrived = [parts[chunk]] + [exchange(parts[chunk], True, s) for s in range(1, blocks)]
        outs = [((half, width + LANES * first), BF16)] * 2
        if first:
            outs.append(((blocks * rows, 2 * block), BF16))
        packed = call(
            functools.partial(pack_kernel, capacity, far, blocks, width, first),
            f"pack_{chunk}",
            outs,
            arrived if first else [*arrived, onehot],
            flops=PACK_FLOPS,
        )
        if first:
            onehot = packed[2]
        slots.append((packed[0], along_group(packed[1], 1)))

    work = 2 * 2 * half * experts * units
    acc = call(
        functools.partial(up_first_kernel, step, widths[0]),
        "up_first",
        [((2 * half, experts * units), F32)],
        [*slots[0], w_up],
        limit=8,
        flops=work * widths[0],
    )[0]
    (hidden,) = call(
        functools.partial(up_last_kernel, step, starts[1], widths[1]),
        "up_last",
        [((2 * half, experts * units), BF16)],
        [*slots[0], *slots[1], w_up, acc],
        limit=8,
        flops=work * widths[1],
    )

    terms = [None] * chunks
    for chunk in reversed(range(chunks)):
        width = widths[chunk]
        own, other = call(
            functools.partial(down_kernel, min(256, width), starts[chunk], width),
            f"down_{chunk}",
            [((half, width), BF16)] * 2,
            [hidden, w_down],
            limit=8,
            flops=work * width,
        )
        dense = call(
            unpack_kernel,
            "unpack_slots",
            [((rows, width), BF16)] * blocks,
            [onehot, own, along_group(other, 1)],
        )
        terms[chunk] = [dense[0]] + [exchange(dense[s], True, s) for s in range(blocks - 1, 0, -1)]
    sums = call(
        functools.partial(add_kernel, chunks, blocks),
        "add_plane",
        [((count, model), BF16)] * far,
        sum(terms, []),
    )
    parts = [sums[0]] + [exchange(sums[s], False, s) for s in range(far - 1, 0, -1)]
    return call(
        finish_kernel, "finish", [((count, model), BF16)], [route_weight.reshape(1, count), *parts]
    )[0]


def solution(mesh):
    placed = (
        P(("group", "inner"), None),
        P(("group", "inner"), None),
        P(("group", "inner"), None),
        P(("group", "inner")),
        P("group", None, "inner"),
        P("group", "inner", None),
    )
    return jax.shard_map(
        body, mesh=mesh, in_specs=placed, out_specs=P(("group", "inner"), None), check_vma=False
    )
```

```python
import functools

import jax
import jax.numpy as jnp
from jax import lax
from jax.experimental import pallas as pl
from jax.experimental.pallas import tpu as pltpu
from jax.sharding import PartitionSpec as P

LANES = 128
STACK_FLOPS = 6 * 10**9
PACK_FLOPS = 15 * 10**8
MIB = 2**20
BF16 = jnp.bfloat16
F32 = jnp.float32
VMEM_SPEC = pl.BlockSpec(memory_space=pltpu.VMEM)


def call(kernel, name, outs, args, limit=4, scratch=(), flops=0, moved=0, specs=None):
    shapes = [jax.ShapeDtypeStruct(shape, dtype) for shape, dtype in outs]
    return pl.pallas_call(
        kernel,
        out_shape=shapes,
        in_specs=specs or [VMEM_SPEC] * len(args),
        out_specs=[VMEM_SPEC] * len(shapes),
        scratch_shapes=list(scratch),
        compiler_params=pltpu.CompilerParams(vmem_limit_bytes=limit * MIB),
        cost_estimate=pl.CostEstimate(flops=flops, bytes_accessed=moved, transcendentals=0),
        name=name,
    )(*args)


def column(row_ref, count):
    across = lax.broadcasted_iota(jnp.int32, (count, count), 1)
    down = lax.broadcasted_iota(jnp.int32, (count, count), 0)
    spread = jnp.broadcast_to(row_ref[...], (count, count))
    return jnp.sum(jnp.where(across == down, spread, jnp.zeros_like(spread)), axis=1, keepdims=True)


def tag_kernel(capacity, experts, rows_ref, expert_ref, *out_refs):
    count = rows_ref.shape[0]
    across = lax.broadcasted_iota(jnp.int32, (count, count), 1)
    down = lax.broadcasted_iota(jnp.int32, (count, count), 0)
    lane = lax.broadcasted_iota(jnp.int32, (count, LANES), 1)
    group_across = expert_ref[...] // experts
    expert_down = column(expert_ref, count)
    group_down = expert_down // experts
    before = (jnp.broadcast_to(group_across, (count, count)) == group_down) & (across < down)
    slot = group_down * capacity + jnp.sum(jnp.where(before, 1, 0), axis=1, keepdims=True)
    local_down = expert_down % experts
    tags = jnp.where(lane == 0, slot, jnp.where(lane == 1, local_down + 1, 0))
    start = 0
    for which, out_ref in enumerate(out_refs):
        part = out_ref.shape[1] - (LANES if which == 0 else 0)
        out_ref[:, :part] = rows_ref[:, start : start + part]
        start += part
    out_refs[0][:, out_refs[0].shape[1] - LANES :] = tags.astype(F32).astype(BF16)


def stack_kernel(*refs):
    count = refs[0].shape[0]
    for which, ref in enumerate(refs[:-1]):
        refs[-1][which * count : (which + 1) * count, :] = ref[...]


def pack_rows(onehot, rows):
    return lax.dot_general(
        onehot, rows, (((0,), (0,)), ((), ())), preferred_element_type=F32
    ).astype(BF16)


def pack_first_kernel(capacity, owners, blocks, *refs):
    own_ref, other_ref, onehot_ref = refs[blocks:]
    block = owners * capacity
    rows, full = refs[0].shape
    count = rows // owners
    me = lax.axis_index("group")
    col = lax.broadcasted_iota(jnp.int32, (rows, 2 * block), 1)
    owner_col = (col % block) // capacity
    owner_row = lax.broadcasted_iota(jnp.int32, (rows, 2 * block), 0) // count
    wanted = (me ^ (col // block)) * capacity + col % capacity
    for which in range(blocks):
        here = slice(which * block, (which + 1) * block)
        slot = refs[which][:, full - LANES :].astype(F32)[:, 0:1].astype(jnp.int32)
        onehot = ((slot == wanted) & (owner_col == owner_row)).astype(F32).astype(BF16)
        onehot_ref[which * rows : (which + 1) * rows, :] = onehot
        packed = pack_rows(onehot, refs[which][...])
        own_ref[here, :] = packed[:block]
        other_ref[here, :] = packed[block:]


def pack_next_kernel(blocks, crossed, *refs):
    onehot_ref, own_ref, other_ref = refs[blocks:]
    rows = refs[0].shape[0]
    count = rows // blocks
    block = onehot_ref.shape[1] // 2

    def store(which, value):
        here = slice(which * block, (which + 1) * block)
        packed = pack_rows(onehot_ref[which * rows : (which + 1) * rows, :], value)
        own_ref[here, :] = packed[:block]
        other_ref[here, :] = packed[block:]

    def straight():
        for which in range(blocks):
            store(which, refs[which][...])

    def across():
        for which in range(blocks):
            here = slice(which * count, (which + 1) * count)
            store(which, jnp.concatenate([ref[here, :] for ref in refs[:blocks]], axis=0))

    if crossed:
        core = lax.axis_index("group") % 2
        pl.when(core == 0)(straight)
        pl.when(core == 1)(across)
    else:
        straight()


def up_product(own_ref, other_ref, up_ref, expert, start, width, cols):
    rows = jnp.concatenate([own_ref[:, :width], other_ref[:, :width]], axis=0)
    return jnp.dot(rows, up_ref[expert, start : start + width, cols], preferred_element_type=F32)


def up_first_kernel(step, width, own_ref, other_ref, up_ref, acc_ref):
    experts, _, units = up_ref.shape
    for expert in range(experts):
        for at in range(0, units, step):
            acc_ref[:, expert * units + at : expert * units + at + step] = up_product(
                own_ref, other_ref, up_ref, expert, 0, width, slice(at, at + step)
            )


def up_last_kernel(step, start, width, own_tag, other_tag, own_ref, other_ref, up_ref, acc_ref, hidden_ref):
    experts, _, units = up_ref.shape
    full = own_tag.shape[1]
    chosen = jnp.concatenate(
        [own_tag[:, full - LANES :].astype(F32)[:, 1:2], other_tag[:, full - LANES :].astype(F32)[:, 1:2]],
        axis=0,
    )
    for expert in range(experts):
        mine = chosen == float(expert + 1)
        for at in range(0, units, step):
            cols = slice(expert * units + at, expert * units + at + step)
            value = acc_ref[:, cols] + up_product(
                own_ref, other_ref, up_ref, expert, start, width, slice(at, at + step)
            )
            value = jnp.where(mine, value / (1.0 + jnp.exp(-value)), 0.0)
            hidden_ref[:, cols] = value.astype(BF16)


def down_kernel(step, start, width, hidden_ref, down_ref, own_ref, other_ref):
    experts, units, _ = down_ref.shape
    half = own_ref.shape[0]
    for at in range(0, width, step):
        total = None
        for expert in range(experts):
            term = jnp.dot(
                hidden_ref[:, expert * units : (expert + 1) * units],
                down_ref[expert, :, start + at : start + at + step],
                preferred_element_type=F32,
            )
            total = term if total is None else total + term
        total = total.astype(BF16)
        own_ref[:, at : at + step] = total[:half]
        other_ref[:, at : at + step] = total[half:]


def dense_block(which, block, rows, onehot_ref, own_ref, other_ref):
    here = slice(which * block, (which + 1) * block)
    slots = jnp.concatenate([own_ref[here, :], other_ref[here, :]], axis=0)
    onehot = onehot_ref[which * rows : (which + 1) * rows, :]
    return jnp.dot(onehot, slots, preferred_element_type=F32).astype(BF16)


def unpack_kernel(crossed, onehot_ref, own_ref, other_ref, *out_refs):
    block = onehot_ref.shape[1] // 2
    rows = out_refs[0].shape[0]
    count = rows // len(out_refs)

    def dense(which):
        here = slice(which * block, (which + 1) * block)
        slots = jnp.concatenate([own_ref[here, :], other_ref[here, :]], axis=0)
        onehot = onehot_ref[which * rows : (which + 1) * rows, :]
        return jnp.dot(onehot, slots, preferred_element_type=F32).astype(BF16)

    def straight():
        for which, out_ref in enumerate(out_refs):
            out_ref[...] = dense(which)

    def across():
        for which in range(len(out_refs)):
            value = dense(which)
            for owner, out_ref in enumerate(out_refs):
                piece = value[owner * count : (owner + 1) * count]
                out_ref[which * count : (which + 1) * count, :] = piece

    if crossed:
        core = lax.axis_index("group") % 2
        pl.when(core == 0)(straight)
        pl.when(core == 1)(across)
    else:
        straight()


def add_kernel(terms, *refs):
    out_refs = refs[terms:]
    total = refs[0][...].astype(F32)
    for ref in refs[1:terms]:
        total += ref[...].astype(F32)
    total = total.astype(BF16)
    count = out_refs[0].shape[0]
    for piece, out_ref in enumerate(out_refs):
        out_ref[...] = total[piece * count : (piece + 1) * count]


def finish_kernel(terms, weight_ref, *refs):
    out_ref = refs[-1]
    weight = column(weight_ref, out_ref.shape[0])
    start = 0
    for first in range(0, len(refs) - 1, terms):
        total = refs[first][...].astype(F32)
        for ref in refs[first + 1 : first + terms]:
            total += ref[...].astype(F32)
        here = slice(start, start + total.shape[1])
        out_ref[:, here] = (total.astype(BF16).astype(F32) * weight).astype(BF16)
        start += total.shape[1]


def body(pair_rows, group_ids, local_ids, route_weight, w_up, w_down):
    groups = lax.axis_size("group")
    inner = lax.axis_size("inner")
    near, turns = 2, groups // 2
    far = inner // near
    count, model = pair_rows.shape
    experts, _, units = w_up.shape
    capacity = 2 * count // groups
    block = far * capacity
    blocks = turns * near
    rows = far * count
    half = blocks * block
    widths = [model // 2, model // 2]
    chunks = len(widths)
    starts = [sum(widths[:i]) for i in range(chunks)]
    step = min(256, units)


    mixed = far == blocks

    def exchange(value, wide, index, chunk):
        pairs = []
        for g in range(groups):
            for i in range(inner):
                if wide != (mixed and chunk == 0 and g % 2 == 1):
                    to = (g ^ 2 * (index // near)) * inner + (i ^ index % near)
                else:
                    to = g * inner + (i ^ near * index)
                pairs.append((g * inner + i, to))
        return lax.ppermute(value, ("group", "inner"), pairs)

    def along_group(value, flip):
        return lax.ppermute(value, "group", [(g, g ^ flip) for g in range(groups)])

    named = group_ids * experts + local_ids
    tagged = call(
        functools.partial(tag_kernel, capacity, experts),
        "tag_rows",
        [((count, w + (LANES if i == 0 else 0)), BF16) for i, w in enumerate(widths)],
        [pair_rows, named.reshape(1, count)],
    )

    onehot = None
    slots = []
    for chunk, width in enumerate(widths):
        part = tagged[chunk]
        pieces = [part] + [exchange(part, False, s, chunk) for s in range(1, far)]
        (held,) = call(
            stack_kernel, "stack_rows", [((rows, part.shape[1]), BF16)], pieces, flops=STACK_FLOPS
        )
        arrived = [held] + [exchange(held, True, s, chunk) for s in range(1, blocks)]
        outs = [((half, part.shape[1]), BF16)] * 2
        if chunk == 0:
            own, other, onehot = call(
                functools.partial(pack_first_kernel, capacity, far, blocks),
                "pack_first",
                outs + [((blocks * rows, 2 * block), BF16)],
                arrived,
                flops=PACK_FLOPS,
            )
        else:
            own, other = call(
                functools.partial(pack_next_kernel, blocks, mixed),
                "pack_next",
                outs,
                [*arrived, onehot],
                flops=PACK_FLOPS,
            )
        slots.append((own, along_group(other, 1)))

    work = 2 * 2 * half * experts * units
    acc = call(
        functools.partial(up_first_kernel, step, widths[0]),
        "up_first",
        [((2 * half, experts * units), F32)],
        [*slots[0], w_up],
        limit=8,
        flops=work * widths[0],
    )[0]
    (hidden,) = call(
        functools.partial(up_last_kernel, step, starts[1], widths[1]),
        "up_last",
        [((2 * half, experts * units), BF16)],
        [*slots[0], *slots[1], w_up, acc],
        limit=8,
        flops=work * widths[1],
    )

    parts = [None] * chunks
    for chunk in reversed(range(chunks)):
        width = widths[chunk]
        own, other = call(
            functools.partial(down_kernel, min(256, width), starts[chunk], width),
            f"down_{chunk}",
            [((half, width), BF16)] * 2,
            [hidden, w_down],
            limit=8,
            flops=work * width,
        )
        dense = call(
            functools.partial(unpack_kernel, mixed and chunk > 0),
            "unpack_slots",
            [((rows, width), BF16)] * blocks,
            [onehot, own, along_group(other, 1)],
        )
        terms = [dense[0]] + [exchange(dense[s], True, s, chunk) for s in range(blocks - 1, 0, -1)]
        sums = call(
            functools.partial(add_kernel, blocks), "add_rows", [((count, width), BF16)] * far, terms
        )
        parts[chunk] = [sums[0]] + [exchange(sums[s], False, s, chunk) for s in range(far - 1, 0, -1)]
    return call(
        functools.partial(finish_kernel, far),
        "finish",
        [((count, model), BF16)],
        [route_weight.reshape(1, count), *sum(parts, [])],
    )[0]


def solution(mesh):
    placed = (
        P(("group", "inner"), None),
        P(("group", "inner"), None),
        P(("group", "inner"), None),
        P(("group", "inner")),
        P("group", None, "inner"),
        P("group", "inner", None),
    )
    return jax.shard_map(
        body, mesh=mesh, in_specs=placed, out_specs=P(("group", "inner"), None), check_vma=False
    )
```

```python
import functools

import jax
import jax.numpy as jnp
from jax import lax
from jax.experimental import pallas as pl
from jax.experimental.pallas import tpu as pltpu
from jax.sharding import PartitionSpec as P

LANES = 128
STACK_FLOPS = 6 * 10**9
PACK_FLOPS = 15 * 10**8
MIB = 2**20
BF16 = jnp.bfloat16
F32 = jnp.float32
VMEM_SPEC = pl.BlockSpec(memory_space=pltpu.VMEM)
ANY_SPEC = pl.BlockSpec(memory_space=pl.ANY)
HBM_SPEC = pl.BlockSpec(memory_space=pltpu.HBM)


def call(kernel, name, outs, args, limit=4, scratch=(), flops=0, moved=0, specs=None):
    shapes = [jax.ShapeDtypeStruct(shape, dtype) for shape, dtype in outs]
    return pl.pallas_call(
        kernel,
        out_shape=shapes,
        in_specs=specs or [VMEM_SPEC] * len(args),
        out_specs=[VMEM_SPEC] * len(shapes),
        scratch_shapes=list(scratch),
        compiler_params=pltpu.CompilerParams(vmem_limit_bytes=limit * MIB),
        cost_estimate=pl.CostEstimate(flops=flops, bytes_accessed=moved, transcendentals=0),
        name=name,
    )(*args)


def column(row_ref, count):
    across = lax.broadcasted_iota(jnp.int32, (count, count), 1)
    down = lax.broadcasted_iota(jnp.int32, (count, count), 0)
    spread = jnp.broadcast_to(row_ref[...], (count, count))
    return jnp.sum(jnp.where(across == down, spread, jnp.zeros_like(spread)), axis=1, keepdims=True)


def tag_kernel(capacity, experts, rows_ref, expert_ref, out_ref):
    count, width = rows_ref.shape
    across = lax.broadcasted_iota(jnp.int32, (count, count), 1)
    down = lax.broadcasted_iota(jnp.int32, (count, count), 0)
    lane = lax.broadcasted_iota(jnp.int32, (count, LANES), 1)
    group_across = expert_ref[...] // experts
    expert_down = column(expert_ref, count)
    group_down = expert_down // experts
    before = (jnp.broadcast_to(group_across, (count, count)) == group_down) & (across < down)
    slot = group_down * capacity + jnp.sum(jnp.where(before, 1, 0), axis=1, keepdims=True)
    local_down = expert_down % experts
    tags = jnp.where(lane == 0, slot, jnp.where(lane == 1, local_down + 1, 0))
    out_ref[:, :width] = rows_ref[...]
    out_ref[:, width:] = tags.astype(F32).astype(BF16)


def stack_kernel(owners, *refs):
    out_refs = refs[owners:]
    count, full = refs[0].shape
    for which in range(owners):
        here = slice(which * count, (which + 1) * count)
        start = 0
        for part, out_ref in enumerate(out_refs):
            width = out_ref.shape[1] - (LANES if part == 0 else 0)
            out_ref[here, :width] = refs[which][:, start : start + width]
            start += width
        out_refs[0][here, out_refs[0].shape[1] - LANES :] = refs[which][:, full - LANES :]


def pack_kernel(capacity, owners, blocks, width, first, *refs):
    if first:
        own_ref, other_ref, onehot_ref = refs[blocks + 1 :]
    else:
        onehot_ref, own_ref, other_ref = refs[blocks:]
    block = owners * capacity
    rows = refs[0].shape[0]
    count = rows // owners
    if first:
        me = lax.axis_index("group")
        col = lax.broadcasted_iota(jnp.int32, (rows, 2 * block), 1)
        owner_col = (col % block) // capacity
        owner_row = lax.broadcasted_iota(jnp.int32, (rows, 2 * block), 0) // count
        wanted = (me ^ (col // block)) * capacity + col % capacity
    for which in range(blocks):
        ref = refs[which]
        here = slice(which * block, (which + 1) * block)
        if first:
            tags = ref[:, width:]
            slot = tags.astype(F32)[:, 0:1].astype(jnp.int32)
            onehot = ((slot == wanted) & (owner_col == owner_row)).astype(F32).astype(BF16)
            onehot_ref[which * rows : (which + 1) * rows, :] = onehot
        else:
            onehot = onehot_ref[which * rows : (which + 1) * rows, :]

        def packed(value):
            return lax.dot_general(
                onehot, value, (((0,), (0,)), ((), ())), preferred_element_type=F32
            ).astype(BF16)

        value = packed(ref[:, :width])
        own_ref[here, :width] = value[:block]
        other_ref[here, :width] = value[block:]
        if first:
            value = packed(tags)
            own_ref[here, width:] = value[:block]
            other_ref[here, width:] = value[block:]


def load_kernel(after_ref, weight_ref, held_ref, token_ref, sem):
    copies = [
        pltpu.make_async_copy(weight_ref.at[e], held_ref.at[e], sem.at[e])
        for e in range(weight_ref.shape[0])
    ]
    for copy in copies:
        copy.start()
    token_ref[...] = jnp.zeros_like(token_ref)
    for copy in copies:
        copy.wait()


def up_product(own_ref, other_ref, up_ref, expert, start, width, cols):
    rows = jnp.concatenate([own_ref[:, :width], other_ref[:, :width]], axis=0)
    return jnp.dot(rows, up_ref[expert, start : start + width, cols], preferred_element_type=F32)


def up_first_kernel(step, width, own_ref, other_ref, up_ref, acc_ref):
    experts, _, units = up_ref.shape
    for expert in range(experts):
        for at in range(0, units, step):
            acc_ref[:, expert * units + at : expert * units + at + step] = up_product(
                own_ref, other_ref, up_ref, expert, 0, width, slice(at, at + step)
            )


def up_last_kernel(step, start, width, own_tag, other_tag, own_ref, other_ref, up_ref, acc_ref, hidden_ref):
    experts, _, units = up_ref.shape
    full = own_tag.shape[1]
    chosen = jnp.concatenate(
        [own_tag[:, full - LANES :].astype(F32)[:, 1:2], other_tag[:, full - LANES :].astype(F32)[:, 1:2]],
        axis=0,
    )
    for expert in range(experts):
        mine = chosen == float(expert + 1)
        for at in range(0, units, step):
            cols = slice(expert * units + at, expert * units + at + step)
            value = acc_ref[:, cols] + up_product(
                own_ref, other_ref, up_ref, expert, start, width, slice(at, at + step)
            )
            value = jnp.where(mine, value / (1.0 + jnp.exp(-value)), 0.0)
            hidden_ref[:, cols] = value.astype(BF16)


def down_kernel(step, start, width, hidden_ref, down_ref, own_ref, other_ref):
    experts, units, _ = down_ref.shape
    half = own_ref.shape[0]
    for at in range(0, width, step):
        total = None
        for expert in range(experts):
            term = jnp.dot(
                hidden_ref[:, expert * units : (expert + 1) * units],
                down_ref[expert, :, start + at : start + at + step],
                preferred_element_type=F32,
            )
            total = term if total is None else total + term
        total = total.astype(BF16)
        own_ref[:, at : at + step] = total[:half]
        other_ref[:, at : at + step] = total[half:]


def dense_block(which, block, rows, onehot_ref, own_ref, other_ref):
    here = slice(which * block, (which + 1) * block)
    slots = jnp.concatenate([own_ref[here, :], other_ref[here, :]], axis=0)
    onehot = onehot_ref[which * rows : (which + 1) * rows, :]
    return jnp.dot(onehot, slots, preferred_element_type=F32).astype(BF16)


def unpack_kernel(onehot_ref, own_ref, other_ref, *out_refs):
    block = onehot_ref.shape[1] // 2
    rows = out_refs[0].shape[0]
    for which, out_ref in enumerate(out_refs):
        here = slice(which * block, (which + 1) * block)
        slots = jnp.concatenate([own_ref[here, :], other_ref[here, :]], axis=0)
        onehot = onehot_ref[which * rows : (which + 1) * rows, :]
        out_ref[...] = jnp.dot(onehot, slots, preferred_element_type=F32).astype(BF16)


def add_kernel(chunks, terms, *refs):
    out_refs = refs[chunks * terms :]
    count = out_refs[0].shape[0]
    start = 0
    for chunk in range(chunks):
        blocks = refs[chunk * terms : (chunk + 1) * terms]
        total = blocks[0][...].astype(F32)
        for ref in blocks[1:]:
            total += ref[...].astype(F32)
        total = total.astype(BF16)
        width = total.shape[1]
        for piece, out_ref in enumerate(out_refs):
            out_ref[:, start : start + width] = total[piece * count : (piece + 1) * count]
        start += width


def finish_kernel(weight_ref, *refs):
    out_ref = refs[-1]
    weight = column(weight_ref, out_ref.shape[0])
    total = refs[0][...].astype(F32)
    for ref in refs[1:-1]:
        total += ref[...].astype(F32)
    out_ref[...] = (total.astype(BF16).astype(F32) * weight).astype(BF16)


def body(pair_rows, group_ids, local_ids, route_weight, w_up, w_down):
    groups = lax.axis_size("group")
    inner = lax.axis_size("inner")
    near, turns = 2, groups // 2
    far = inner // near
    count, model = pair_rows.shape
    experts, _, units = w_up.shape
    capacity = 2 * count // groups
    block = far * capacity
    blocks = turns * near
    rows = far * count
    half = blocks * block
    widths = [model // 2, model // 2]
    chunks = len(widths)
    starts = [sum(widths[:i]) for i in range(chunks)]
    step = min(256, units)


    mixed = far == blocks

    def exchange(value, wide, index):
        pairs = []
        for g in range(groups):
            for i in range(inner):
                if wide != (mixed and g % 2 == 0):
                    to = (g ^ 2 * (index // near)) * inner + (i ^ index % near)
                else:
                    to = g * inner + (i ^ near * index)
                pairs.append((g * inner + i, to))
        return lax.ppermute(value, ("group", "inner"), pairs)

    def along_group(value, flip):
        return lax.ppermute(value, "group", [(g, g ^ flip) for g in range(groups)])

    full = model + LANES
    named = group_ids * experts + local_ids
    (tagged,) = call(
        functools.partial(tag_kernel, capacity, experts),
        "tag_rows",
        [((count, full), BF16)],
        [pair_rows, named.reshape(1, count)],
    )

    pieces = [exchange(tagged, False, s) for s in range(far - 1, 0, -1)] + [tagged]
    pieces.reverse()
    parts = call(
        functools.partial(stack_kernel, far),
        "stack_rows",
        [((rows, w + (LANES if i == 0 else 0)), BF16) for i, w in enumerate(widths)],
        pieces,
        flops=STACK_FLOPS,
    )

    onehot = None
    slots = []
    for chunk, width in enumerate(widths):
        first = chunk == 0
        arrived = [parts[chunk]] + [exchange(parts[chunk], True, s) for s in range(1, blocks)]
        if first:
            down_held, down_token = call(
                load_kernel,
                "load_down",
                [(w_down.shape, BF16), ((8, LANES), F32)],
                [arrived[-1], w_down],
                specs=[ANY_SPEC, HBM_SPEC],
                scratch=[pltpu.SemaphoreType.DMA((experts,))],
                moved=4 * w_down.size,
                limit=38,
            )
        outs = [((half, width + LANES * first), BF16)] * 2
        if first:
            outs.append(((blocks * rows, 2 * block), BF16))
        packed = call(
            functools.partial(pack_kernel, capacity, far, blocks, width, first),
            f"pack_{chunk}",
            outs,
            [*arrived, down_token] if first else [*arrived, onehot],
            flops=PACK_FLOPS,
        )
        if first:
            onehot = packed[2]
        slots.append((packed[0], along_group(packed[1], 1)))

    work = 2 * 2 * half * experts * units
    acc = call(
        functools.partial(up_first_kernel, step, widths[0]),
        "up_first",
        [((2 * half, experts * units), F32)],
        [*slots[0], w_up],
        limit=8,
        flops=work * widths[0],
    )[0]
    (hidden,) = call(
        functools.partial(up_last_kernel, step, starts[1], widths[1]),
        "up_last",
        [((2 * half, experts * units), BF16)],
        [*slots[0], *slots[1], w_up, acc],
        limit=8,
        flops=work * widths[1],
    )

    terms = [None] * chunks
    for chunk in reversed(range(chunks)):
        width = widths[chunk]
        own, other = call(
            functools.partial(down_kernel, min(256, width), starts[chunk], width),
            f"down_{chunk}",
            [((half, width), BF16)] * 2,
            [hidden, down_held],
            limit=8,
            flops=work * width,
        )
        dense = call(
            unpack_kernel,
            "unpack_slots",
            [((rows, width), BF16)] * blocks,
            [onehot, own, along_group(other, 1)],
        )
        terms[chunk] = [dense[0]] + [exchange(dense[s], True, s) for s in range(blocks - 1, 0, -1)]
    sums = call(
        functools.partial(add_kernel, chunks, blocks),
        "add_plane",
        [((count, model), BF16)] * far,
        sum(terms, []),
    )
    parts = [sums[0]] + [exchange(sums[s], False, s) for s in range(far - 1, 0, -1)]
    return call(
        finish_kernel, "finish", [((count, model), BF16)], [route_weight.reshape(1, count), *parts]
    )[0]


def solution(mesh):
    placed = (
        P(("group", "inner"), None),
        P(("group", "inner"), None),
        P(("group", "inner"), None),
        P(("group", "inner")),
        P("group", None, "inner"),
        P("group", "inner", None),
    )
    return jax.shard_map(
        body, mesh=mesh, in_specs=placed, out_specs=P(("group", "inner"), None), check_vma=False
    )
```

```python
import functools

import jax
import jax.numpy as jnp
from jax import lax
from jax.experimental import pallas as pl
from jax.experimental.pallas import tpu as pltpu
from jax.sharding import PartitionSpec as P

LANES = 128
STACK_FLOPS = 6 * 10**9
PACK_FLOPS = 15 * 10**8
MIB = 2**20
BF16 = jnp.bfloat16
F32 = jnp.float32
VMEM_SPEC = pl.BlockSpec(memory_space=pltpu.VMEM)
ANY_SPEC = pl.BlockSpec(memory_space=pl.ANY)
HBM_SPEC = pl.BlockSpec(memory_space=pltpu.HBM)


def call(kernel, name, outs, args, limit=4, scratch=(), flops=0, moved=0, specs=None):
    shapes = [jax.ShapeDtypeStruct(shape, dtype) for shape, dtype in outs]
    return pl.pallas_call(
        kernel,
        out_shape=shapes,
        in_specs=specs or [VMEM_SPEC] * len(args),
        out_specs=[VMEM_SPEC] * len(shapes),
        scratch_shapes=list(scratch),
        compiler_params=pltpu.CompilerParams(vmem_limit_bytes=limit * MIB),
        cost_estimate=pl.CostEstimate(flops=flops, bytes_accessed=moved, transcendentals=0),
        name=name,
    )(*args)


def column(row_ref, count):
    across = lax.broadcasted_iota(jnp.int32, (count, count), 1)
    down = lax.broadcasted_iota(jnp.int32, (count, count), 0)
    spread = jnp.broadcast_to(row_ref[...], (count, count))
    return jnp.sum(jnp.where(across == down, spread, jnp.zeros_like(spread)), axis=1, keepdims=True)


def tag_kernel(capacity, experts, rows_ref, expert_ref, out_ref):
    count, width = rows_ref.shape
    across = lax.broadcasted_iota(jnp.int32, (count, count), 1)
    down = lax.broadcasted_iota(jnp.int32, (count, count), 0)
    lane = lax.broadcasted_iota(jnp.int32, (count, LANES), 1)
    group_across = expert_ref[...] // experts
    expert_down = column(expert_ref, count)
    group_down = expert_down // experts
    before = (jnp.broadcast_to(group_across, (count, count)) == group_down) & (across < down)
    slot = group_down * capacity + jnp.sum(jnp.where(before, 1, 0), axis=1, keepdims=True)
    local_down = expert_down % experts
    tags = jnp.where(lane == 0, slot, jnp.where(lane == 1, local_down + 1, 0))
    out_ref[:, :width] = rows_ref[...]
    out_ref[:, width:] = tags.astype(F32).astype(BF16)


def stack_kernel(owners, *refs):
    out_refs = refs[owners:]
    count, full = refs[0].shape
    for which in range(owners):
        here = slice(which * count, (which + 1) * count)
        start = 0
        for part, out_ref in enumerate(out_refs):
            width = out_ref.shape[1] - (LANES if part == 0 else 0)
            out_ref[here, :width] = refs[which][:, start : start + width]
            start += width
        out_refs[0][here, out_refs[0].shape[1] - LANES :] = refs[which][:, full - LANES :]


def pack_kernel(capacity, owners, blocks, width, first, *refs):
    if first:
        own_ref, other_ref, onehot_ref = refs[blocks + 1 :]
    else:
        onehot_ref, own_ref, other_ref = refs[blocks:]
    block = owners * capacity
    rows = refs[0].shape[0]
    count = rows // owners
    if first:
        me = lax.axis_index("group")
        col = lax.broadcasted_iota(jnp.int32, (rows, 2 * block), 1)
        owner_col = (col % block) // capacity
        owner_row = lax.broadcasted_iota(jnp.int32, (rows, 2 * block), 0) // count
        wanted = (me ^ (col // block)) * capacity + col % capacity
    for which in range(blocks):
        ref = refs[which]
        here = slice(which * block, (which + 1) * block)
        if first:
            tags = ref[:, width:]
            slot = tags.astype(F32)[:, 0:1].astype(jnp.int32)
            onehot = ((slot == wanted) & (owner_col == owner_row)).astype(F32).astype(BF16)
            onehot_ref[which * rows : (which + 1) * rows, :] = onehot
        else:
            onehot = onehot_ref[which * rows : (which + 1) * rows, :]

        def packed(value):
            return lax.dot_general(
                onehot, value, (((0,), (0,)), ((), ())), preferred_element_type=F32
            ).astype(BF16)

        value = packed(ref[:, :width])
        own_ref[here, :width] = value[:block]
        other_ref[here, :width] = value[block:]
        if first:
            value = packed(tags)
            own_ref[here, width:] = value[:block]
            other_ref[here, width:] = value[block:]


def load_kernel(after_ref, weight_ref, held_ref, token_ref, sem):
    copies = [
        pltpu.make_async_copy(weight_ref.at[e], held_ref.at[e], sem.at[e])
        for e in range(weight_ref.shape[0])
    ]
    for copy in copies:
        copy.start()
    token_ref[...] = jnp.zeros_like(token_ref)
    for copy in copies:
        copy.wait()


def up_product(own_ref, other_ref, up_ref, expert, start, width, cols):
    rows = jnp.concatenate([own_ref[:, :width], other_ref[:, :width]], axis=0)
    return jnp.dot(rows, up_ref[expert, start : start + width, cols], preferred_element_type=F32)


def up_first_kernel(step, width, own_ref, other_ref, up_ref, acc_ref):
    experts, _, units = up_ref.shape
    for expert in range(experts):
        for at in range(0, units, step):
            acc_ref[:, expert * units + at : expert * units + at + step] = up_product(
                own_ref, other_ref, up_ref, expert, 0, width, slice(at, at + step)
            )


def up_last_kernel(step, start, width, own_tag, other_tag, own_ref, other_ref, up_ref, acc_ref, hidden_ref):
    experts, _, units = up_ref.shape
    full = own_tag.shape[1]
    chosen = jnp.concatenate(
        [own_tag[:, full - LANES :].astype(F32)[:, 1:2], other_tag[:, full - LANES :].astype(F32)[:, 1:2]],
        axis=0,
    )
    for expert in range(experts):
        mine = chosen == float(expert + 1)
        for at in range(0, units, step):
            cols = slice(expert * units + at, expert * units + at + step)
            value = acc_ref[:, cols] + up_product(
                own_ref, other_ref, up_ref, expert, start, width, slice(at, at + step)
            )
            value = jnp.where(mine, value / (1.0 + jnp.exp(-value)), 0.0)
            hidden_ref[:, cols] = value.astype(BF16)


def down_kernel(step, start, width, hidden_ref, down_ref, own_ref, other_ref):
    experts, units, _ = down_ref.shape
    half = own_ref.shape[0]
    for at in range(0, width, step):
        total = None
        for expert in range(experts):
            term = jnp.dot(
                hidden_ref[:, expert * units : (expert + 1) * units],
                down_ref[expert, :, start + at : start + at + step],
                preferred_element_type=F32,
            )
            total = term if total is None else total + term
        total = total.astype(BF16)
        own_ref[:, at : at + step] = total[:half]
        other_ref[:, at : at + step] = total[half:]


def dense_block(which, block, rows, onehot_ref, own_ref, other_ref):
    here = slice(which * block, (which + 1) * block)
    slots = jnp.concatenate([own_ref[here, :], other_ref[here, :]], axis=0)
    onehot = onehot_ref[which * rows : (which + 1) * rows, :]
    return jnp.dot(onehot, slots, preferred_element_type=F32).astype(BF16)


def unpack_kernel(onehot_ref, own_ref, other_ref, *out_refs):
    block = onehot_ref.shape[1] // 2
    rows = out_refs[0].shape[0]
    for which, out_ref in enumerate(out_refs):
        here = slice(which * block, (which + 1) * block)
        slots = jnp.concatenate([own_ref[here, :], other_ref[here, :]], axis=0)
        onehot = onehot_ref[which * rows : (which + 1) * rows, :]
        out_ref[...] = jnp.dot(onehot, slots, preferred_element_type=F32).astype(BF16)


def add_kernel(chunks, terms, *refs):
    out_refs = refs[chunks * terms :]
    count = out_refs[0].shape[0]
    start = 0
    for chunk in range(chunks):
        blocks = refs[chunk * terms : (chunk + 1) * terms]
        total = blocks[0][...].astype(F32)
        for ref in blocks[1:]:
            total += ref[...].astype(F32)
        total = total.astype(BF16)
        width = total.shape[1]
        for piece, out_ref in enumerate(out_refs):
            out_ref[:, start : start + width] = total[piece * count : (piece + 1) * count]
        start += width


def finish_kernel(weight_ref, *refs):
    out_ref = refs[-1]
    weight = column(weight_ref, out_ref.shape[0])
    total = refs[0][...].astype(F32)
    for ref in refs[1:-1]:
        total += ref[...].astype(F32)
    out_ref[...] = (total.astype(BF16).astype(F32) * weight).astype(BF16)


def body(pair_rows, group_ids, local_ids, route_weight, w_up, w_down):
    groups = lax.axis_size("group")
    inner = lax.axis_size("inner")
    near, turns = 2, groups // 2
    far = inner // near
    count, model = pair_rows.shape
    experts, _, units = w_up.shape
    capacity = 2 * count // groups
    block = far * capacity
    blocks = turns * near
    rows = far * count
    half = blocks * block
    widths = [model // 2, model // 2]
    chunks = len(widths)
    starts = [sum(widths[:i]) for i in range(chunks)]
    step = min(256, units)


    mixed = far == blocks

    def exchange(value, wide, index):
        pairs = []
        for g in range(groups):
            for i in range(inner):
                if wide != (mixed and g % 2 == 1):
                    to = (g ^ 2 * (index // near)) * inner + (i ^ index % near)
                else:
                    to = g * inner + (i ^ near * index)
                pairs.append((g * inner + i, to))
        return lax.ppermute(value, ("group", "inner"), pairs)

    def along_group(value, flip):
        return lax.ppermute(value, "group", [(g, g ^ flip) for g in range(groups)])

    full = model + LANES
    named = group_ids * experts + local_ids
    (tagged,) = call(
        functools.partial(tag_kernel, capacity, experts),
        "tag_rows",
        [((count, full), BF16)],
        [pair_rows, named.reshape(1, count)],
    )

    pieces = [exchange(tagged, False, s) for s in range(far - 1, 0, -1)] + [tagged]
    pieces.reverse()
    parts = call(
        functools.partial(stack_kernel, far),
        "stack_rows",
        [((rows, w + (LANES if i == 0 else 0)), BF16) for i, w in enumerate(widths)],
        pieces,
        flops=STACK_FLOPS,
    )

    onehot = None
    slots = []
    for chunk, width in enumerate(widths):
        first = chunk == 0
        arrived = [parts[chunk]] + [exchange(parts[chunk], True, s) for s in range(1, blocks)]
        if first:
            down_held, down_token = call(
                load_kernel,
                "load_down",
                [(w_down.shape, BF16), ((8, LANES), F32)],
                [arrived[-1], w_down],
                specs=[ANY_SPEC, HBM_SPEC],
                scratch=[pltpu.SemaphoreType.DMA((experts,))],
                moved=4 * w_down.size,
                limit=38,
            )
        outs = [((half, width + LANES * first), BF16)] * 2
        if first:
            outs.append(((blocks * rows, 2 * block), BF16))
        packed = call(
            functools.partial(pack_kernel, capacity, far, blocks, width, first),
            f"pack_{chunk}",
            outs,
            [*arrived, down_token] if first else [*arrived, onehot],
            flops=PACK_FLOPS,
        )
        if first:
            onehot = packed[2]
        slots.append((packed[0], along_group(packed[1], 1)))

    work = 2 * 2 * half * experts * units
    acc = call(
        functools.partial(up_first_kernel, step, widths[0]),
        "up_first",
        [((2 * half, experts * units), F32)],
        [*slots[0], w_up],
        limit=8,
        flops=work * widths[0],
    )[0]
    (hidden,) = call(
        functools.partial(up_last_kernel, step, starts[1], widths[1]),
        "up_last",
        [((2 * half, experts * units), BF16)],
        [*slots[0], *slots[1], w_up, acc],
        limit=8,
        flops=work * widths[1],
    )

    terms = [None] * chunks
    for chunk in reversed(range(chunks)):
        width = widths[chunk]
        own, other = call(
            functools.partial(down_kernel, min(256, width), starts[chunk], width),
            f"down_{chunk}",
            [((half, width), BF16)] * 2,
            [hidden, down_held],
            limit=8,
            flops=work * width,
        )
        dense = call(
            unpack_kernel,
            "unpack_slots",
            [((rows, width), BF16)] * blocks,
            [onehot, own, along_group(other, 1)],
        )
        terms[chunk] = [dense[0]] + [exchange(dense[s], True, s) for s in range(blocks - 1, 0, -1)]
    sums = call(
        functools.partial(add_kernel, chunks, blocks),
        "add_plane",
        [((count, model), BF16)] * far,
        sum(terms, []),
    )
    parts = [sums[0]] + [exchange(sums[s], False, s) for s in range(far - 1, 0, -1)]
    return call(
        finish_kernel, "finish", [((count, model), BF16)], [route_weight.reshape(1, count), *parts]
    )[0]


def solution(mesh):
    placed = (
        P(("group", "inner"), None),
        P(("group", "inner"), None),
        P(("group", "inner"), None),
        P(("group", "inner")),
        P("group", None, "inner"),
        P("group", "inner", None),
    )
    return jax.shard_map(
        body, mesh=mesh, in_specs=placed, out_specs=P(("group", "inner"), None), check_vma=False
    )
```

```python
import functools

import jax
import jax.numpy as jnp
from jax import lax
from jax.experimental import pallas as pl
from jax.experimental.pallas import tpu as pltpu
from jax.sharding import PartitionSpec as P

LANES = 128
STACK_FLOPS = 6 * 10**9
PACK_FLOPS = 15 * 10**8
MIB = 2**20
BF16 = jnp.bfloat16
F32 = jnp.float32
VMEM_SPEC = pl.BlockSpec(memory_space=pltpu.VMEM)
ANY_SPEC = pl.BlockSpec(memory_space=pl.ANY)
HBM_SPEC = pl.BlockSpec(memory_space=pltpu.HBM)


def call(kernel, name, outs, args, limit=4, scratch=(), flops=0, moved=0, specs=None):
    shapes = [jax.ShapeDtypeStruct(shape, dtype) for shape, dtype in outs]
    return pl.pallas_call(
        kernel,
        out_shape=shapes,
        in_specs=specs or [VMEM_SPEC] * len(args),
        out_specs=[VMEM_SPEC] * len(shapes),
        scratch_shapes=list(scratch),
        compiler_params=pltpu.CompilerParams(vmem_limit_bytes=limit * MIB),
        cost_estimate=pl.CostEstimate(flops=flops, bytes_accessed=moved, transcendentals=0),
        name=name,
    )(*args)


def column(row_ref, count):
    across = lax.broadcasted_iota(jnp.int32, (count, count), 1)
    down = lax.broadcasted_iota(jnp.int32, (count, count), 0)
    spread = jnp.broadcast_to(row_ref[...], (count, count))
    return jnp.sum(jnp.where(across == down, spread, jnp.zeros_like(spread)), axis=1, keepdims=True)


def tag_kernel(capacity, experts, rows_ref, expert_ref, out_ref):
    count, width = rows_ref.shape
    across = lax.broadcasted_iota(jnp.int32, (count, count), 1)
    down = lax.broadcasted_iota(jnp.int32, (count, count), 0)
    lane = lax.broadcasted_iota(jnp.int32, (count, LANES), 1)
    group_across = expert_ref[...] // experts
    expert_down = column(expert_ref, count)
    group_down = expert_down // experts
    before = (jnp.broadcast_to(group_across, (count, count)) == group_down) & (across < down)
    slot = group_down * capacity + jnp.sum(jnp.where(before, 1, 0), axis=1, keepdims=True)
    local_down = expert_down % experts
    tags = jnp.where(lane == 0, slot, jnp.where(lane == 1, local_down + 1, 0))
    out_ref[:, :width] = rows_ref[...]
    out_ref[:, width:] = tags.astype(F32).astype(BF16)


def stack_kernel(owners, *refs):
    out_refs = refs[owners:]
    count, full = refs[0].shape
    for which in range(owners):
        here = slice(which * count, (which + 1) * count)
        start = 0
        for part, out_ref in enumerate(out_refs):
            width = out_ref.shape[1] - (LANES if part == 0 else 0)
            out_ref[here, :width] = refs[which][:, start : start + width]
            start += width
        out_refs[0][here, out_refs[0].shape[1] - LANES :] = refs[which][:, full - LANES :]


def pack_kernel(capacity, blocks, first, *refs):
    row_refs = refs[:blocks]
    if first:
        own_ref, other_ref, onehot_ref, held = refs[blocks + 1 :]
    else:
        onehot_ref, own_ref, other_ref, held = refs[blocks:]
    rows, full = row_refs[0].shape
    half = own_ref.shape[0]
    for which, ref in enumerate(row_refs):
        held[which * rows : (which + 1) * rows, :] = ref[...]
    if first:
        me = lax.axis_index("group")
        lane = lax.broadcasted_iota(jnp.int32, (rows, LANES), 1)
        place = lax.broadcasted_iota(jnp.int32, (rows, 2 * half), 1)
        down = lax.broadcasted_iota(jnp.int32, (rows, rows), 0)
        across = lax.broadcasted_iota(jnp.int32, (rows, rows), 1)
        earlier = (across < down).astype(F32).astype(BF16)
        taken = jnp.zeros((1, LANES), F32)
        for which, ref in enumerate(row_refs):
            tags = ref[:, full - LANES :].astype(F32)
            group = tags[:, 0:1].astype(jnp.int32) // capacity
            expert = tags[:, 1:2].astype(jnp.int32) - 1
            side = jnp.where(group == me, 0, jnp.where(group == (me ^ 1), 1, LANES))
            named = jnp.where(lane == 2 * side + expert, 1.0, 0.0)
            ahead = jnp.dot(earlier, named.astype(BF16), preferred_element_type=F32) + taken
            rank = jnp.sum(named * ahead, axis=1, keepdims=True).astype(jnp.int32)
            spot = jnp.where(expert == 0, rank, half - 1 - rank) + side * half
            onehot = (place == spot).astype(F32).astype(BF16)
            onehot_ref[which * rows : (which + 1) * rows, :] = onehot
            taken += jnp.sum(named, axis=0, keepdims=True)
    packed = lax.dot_general(
        onehot_ref[...], held[...], (((0,), (0,)), ((), ())), preferred_element_type=F32
    ).astype(BF16)
    own_ref[...] = packed[:half]
    other_ref[...] = packed[half:]


def load_kernel(after_ref, weight_ref, held_ref, token_ref, sem):
    copies = [
        pltpu.make_async_copy(weight_ref.at[e], held_ref.at[e], sem.at[e])
        for e in range(weight_ref.shape[0])
    ]
    for copy in copies:
        copy.start()
    token_ref[...] = jnp.zeros_like(token_ref)
    for copy in copies:
        copy.wait()


def chosen(own_tag, other_tag):
    full, half = own_tag.shape[1], own_tag.shape[0]
    row = lax.broadcasted_iota(jnp.int32, (half, 1), 0)
    parts, crossed = [], 0.0
    for ref in (own_tag, other_tag):
        part = ref[:, full - LANES :].astype(F32)[:, 1:2]
        wrong = ((part == 1.0) & (row >= half // 2)) | ((part == 2.0) & (row < half // 2))
        crossed = jnp.maximum(crossed, jnp.max(jnp.where(wrong, 1.0, 0.0)))
        parts.append(part)
    return jnp.concatenate(parts, axis=0), crossed > 0.0


def by_expert(own_tag, other_tag, pieces, product, store):
    half = own_tag.shape[0]
    fit = half // 2
    tags, crossed = chosen(own_tag, other_tag)

    @pl.when(jnp.logical_not(crossed))
    def _():
        for expert in range(2):
            here = slice(expert * fit, (expert + 1) * fit)
            for piece in range(pieces):
                value = product(expert, piece, here)
                store(piece, here, value[:fit], value[fit:])

    @pl.when(crossed)
    def _():
        here = slice(0, half)
        for piece in range(pieces):
            value = jnp.where(tags == 2.0, product(1, piece, here), product(0, piece, here))
            store(piece, here, value[:half], value[half:])


def up_first_kernel(step, width, own_ref, other_ref, up_ref, acc_ref):
    half = own_ref.shape[0]

    def product(expert, piece, here):
        rows = jnp.concatenate([own_ref[here, :width], other_ref[here, :width]], axis=0)
        cols = slice(piece * step, (piece + 1) * step)
        return jnp.dot(rows, up_ref[expert, :width, cols], preferred_element_type=F32)

    def store(piece, here, own, other):
        cols = slice(piece * step, (piece + 1) * step)
        acc_ref[here, cols] = own
        acc_ref[half + here.start : half + here.stop, cols] = other

    by_expert(own_ref, other_ref, up_ref.shape[2] // step, product, store)


def up_last_kernel(step, start, width, own_tag, other_tag, own_ref, other_ref, up_ref, acc_ref, hidden_ref):
    half = own_ref.shape[0]

    def product(expert, piece, here):
        rows = jnp.concatenate([own_ref[here, :width], other_ref[here, :width]], axis=0)
        cols = slice(piece * step, (piece + 1) * step)
        return jnp.dot(rows, up_ref[expert, start : start + width, cols], preferred_element_type=F32)

    def store(piece, here, own, other):
        cols = slice(piece * step, (piece + 1) * step)
        for offset, value in ((0, own), (half, other)):
            rows = slice(offset + here.start, offset + here.stop)
            value = acc_ref[rows, cols] + value
            hidden_ref[rows, cols] = (value / (1.0 + jnp.exp(-value))).astype(BF16)

    by_expert(own_tag, other_tag, up_ref.shape[2] // step, product, store)


def down_kernel(step, start, width, own_tag, other_tag, hidden_ref, down_ref, own_ref, other_ref):
    half = own_ref.shape[0]

    def product(expert, piece, here):
        rows = jnp.concatenate(
            [hidden_ref[here, :], hidden_ref[half + here.start : half + here.stop, :]], axis=0
        )
        cols = slice(start + piece * step, start + (piece + 1) * step)
        return jnp.dot(rows, down_ref[expert, :, cols], preferred_element_type=F32)

    def store(piece, here, own, other):
        cols = slice(piece * step, (piece + 1) * step)
        own_ref[here, cols] = own.astype(BF16)
        other_ref[here, cols] = other.astype(BF16)

    by_expert(own_tag, other_tag, width // step, product, store)


def unpack_kernel(onehot_ref, own_ref, other_ref, *out_refs):
    rows = out_refs[0].shape[0]
    slots = jnp.concatenate([own_ref[...], other_ref[...]], axis=0)
    for which, out_ref in enumerate(out_refs):
        onehot = onehot_ref[which * rows : (which + 1) * rows, :]
        out_ref[...] = jnp.dot(onehot, slots, preferred_element_type=F32).astype(BF16)


def add_kernel(chunks, terms, *refs):
    out_refs = refs[chunks * terms :]
    count = out_refs[0].shape[0]
    start = 0
    for chunk in range(chunks):
        blocks = refs[chunk * terms : (chunk + 1) * terms]
        total = blocks[0][...].astype(F32)
        for ref in blocks[1:]:
            total += ref[...].astype(F32)
        total = total.astype(BF16)
        width = total.shape[1]
        for piece, out_ref in enumerate(out_refs):
            out_ref[:, start : start + width] = total[piece * count : (piece + 1) * count]
        start += width


def finish_kernel(weight_ref, *refs):
    out_ref = refs[-1]
    weight = column(weight_ref, out_ref.shape[0])
    total = refs[0][...].astype(F32)
    for ref in refs[1:-1]:
        total += ref[...].astype(F32)
    out_ref[...] = (total.astype(BF16).astype(F32) * weight).astype(BF16)


def body(pair_rows, group_ids, local_ids, route_weight, w_up, w_down):
    groups = lax.axis_size("group")
    inner = lax.axis_size("inner")
    near, turns = 2, groups // 2
    far = inner // near
    count, model = pair_rows.shape
    experts, _, units = w_up.shape
    capacity = 2 * count // groups
    block = far * capacity
    blocks = turns * near
    rows = far * count
    half = blocks * block
    widths = [model // 2, model // 2]
    chunks = len(widths)
    starts = [sum(widths[:i]) for i in range(chunks)]
    step = min(256, units)


    mixed = far == blocks

    def exchange(value, wide, index):
        pairs = []
        for g in range(groups):
            for i in range(inner):
                if wide != (mixed and g % 2 == 1):
                    to = (g ^ 2 * (index // near)) * inner + (i ^ index % near)
                else:
                    to = g * inner + (i ^ near * index)
                pairs.append((g * inner + i, to))
        return lax.ppermute(value, ("group", "inner"), pairs)

    def along_group(value, flip):
        return lax.ppermute(value, "group", [(g, g ^ flip) for g in range(groups)])

    full = model + LANES
    named = group_ids * experts + local_ids
    (tagged,) = call(
        functools.partial(tag_kernel, capacity, experts),
        "tag_rows",
        [((count, full), BF16)],
        [pair_rows, named.reshape(1, count)],
    )

    pieces = [exchange(tagged, False, s) for s in range(far - 1, 0, -1)] + [tagged]
    pieces.reverse()
    parts = call(
        functools.partial(stack_kernel, far),
        "stack_rows",
        [((rows, w + (LANES if i == 0 else 0)), BF16) for i, w in enumerate(widths)],
        pieces,
        flops=STACK_FLOPS,
    )

    room = 4 + 8 * blocks * rows * half * 2 * 2 // MIB
    onehot = None
    slots = []
    for chunk, width in enumerate(widths):
        first = chunk == 0
        arrived = [parts[chunk]] + [exchange(parts[chunk], True, s) for s in range(1, blocks)]
        if first:
            down_held, down_token = call(
                load_kernel,
                "load_down",
                [(w_down.shape, BF16), ((8, LANES), F32)],
                [arrived[-1], w_down],
                specs=[ANY_SPEC, HBM_SPEC],
                scratch=[pltpu.SemaphoreType.DMA((experts,))],
                moved=4 * w_down.size,
                limit=38,
            )
        outs = [((half, width + LANES * first), BF16)] * 2
        if first:
            outs.append(((blocks * rows, 2 * half), BF16))
        packed = call(
            functools.partial(pack_kernel, capacity, blocks, first),
            f"pack_{chunk}",
            outs,
            [*arrived, down_token] if first else [*arrived, onehot],
            scratch=[pltpu.VMEM((blocks * rows, parts[chunk].shape[1]), BF16)],
            limit=room,
            flops=PACK_FLOPS,
        )
        if first:
            onehot = packed[2]
        slots.append((packed[0], along_group(packed[1], 1)))

    work = 2 * 2 * half * experts * units
    acc = call(
        functools.partial(up_first_kernel, step, widths[0]),
        "up_first",
        [((2 * half, units), F32)],
        [*slots[0], w_up],
        limit=8,
        flops=work * widths[0],
    )[0]
    (hidden,) = call(
        functools.partial(up_last_kernel, step, starts[1], widths[1]),
        "up_last",
        [((2 * half, units), BF16)],
        [*slots[0], *slots[1], w_up, acc],
        limit=8,
        flops=work * widths[1],
    )

    terms = [None] * chunks
    for chunk in reversed(range(chunks)):
        width = widths[chunk]
        own, other = call(
            functools.partial(down_kernel, min(256, width), starts[chunk], width),
            f"down_{chunk}",
            [((half, width), BF16)] * 2,
            [*slots[0], hidden, down_held],
            limit=8,
            flops=work * width,
        )
        dense = call(
            unpack_kernel,
            "unpack_slots",
            [((rows, width), BF16)] * blocks,
            [onehot, own, along_group(other, 1)],
            limit=room,
        )
        terms[chunk] = [dense[0]] + [exchange(dense[s], True, s) for s in range(blocks - 1, 0, -1)]
    sums = call(
        functools.partial(add_kernel, chunks, blocks),
        "add_plane",
        [((count, model), BF16)] * far,
        sum(terms, []),
    )
    parts = [sums[0]] + [exchange(sums[s], False, s) for s in range(far - 1, 0, -1)]
    return call(
        finish_kernel, "finish", [((count, model), BF16)], [route_weight.reshape(1, count), *parts]
    )[0]


def solution(mesh):
    placed = (
        P(("group", "inner"), None),
        P(("group", "inner"), None),
        P(("group", "inner"), None),
        P(("group", "inner")),
        P("group", None, "inner"),
        P("group", "inner", None),
    )
    return jax.shard_map(
        body, mesh=mesh, in_specs=placed, out_specs=P(("group", "inner"), None), check_vma=False
    )
```

```python
import functools

import jax
import jax.numpy as jnp
from jax import lax
from jax.experimental import pallas as pl
from jax.experimental.pallas import tpu as pltpu
from jax.sharding import PartitionSpec as P

LANES = 128
STACK_FLOPS = 6 * 10**9
PACK_FLOPS = 15 * 10**8
MIB = 2**20
BF16 = jnp.bfloat16
F32 = jnp.float32
VMEM_SPEC = pl.BlockSpec(memory_space=pltpu.VMEM)
ANY_SPEC = pl.BlockSpec(memory_space=pl.ANY)
HBM_SPEC = pl.BlockSpec(memory_space=pltpu.HBM)


def call(kernel, name, outs, args, limit=4, scratch=(), flops=0, moved=0, specs=None):
    shapes = [jax.ShapeDtypeStruct(shape, dtype) for shape, dtype in outs]
    return pl.pallas_call(
        kernel,
        out_shape=shapes,
        in_specs=specs or [VMEM_SPEC] * len(args),
        out_specs=[VMEM_SPEC] * len(shapes),
        scratch_shapes=list(scratch),
        compiler_params=pltpu.CompilerParams(vmem_limit_bytes=limit * MIB),
        cost_estimate=pl.CostEstimate(flops=flops, bytes_accessed=moved, transcendentals=0),
        name=name,
    )(*args)


def column(row_ref, count):
    across = lax.broadcasted_iota(jnp.int32, (count, count), 1)
    down = lax.broadcasted_iota(jnp.int32, (count, count), 0)
    spread = jnp.broadcast_to(row_ref[...], (count, count))
    return jnp.sum(jnp.where(across == down, spread, jnp.zeros_like(spread)), axis=1, keepdims=True)


def tag_kernel(capacity, experts, rows_ref, expert_ref, out_ref):
    count, width = rows_ref.shape
    across = lax.broadcasted_iota(jnp.int32, (count, count), 1)
    down = lax.broadcasted_iota(jnp.int32, (count, count), 0)
    lane = lax.broadcasted_iota(jnp.int32, (count, LANES), 1)
    group_across = expert_ref[...] // experts
    expert_down = column(expert_ref, count)
    group_down = expert_down // experts
    before = (jnp.broadcast_to(group_across, (count, count)) == group_down) & (across < down)
    slot = group_down * capacity + jnp.sum(jnp.where(before, 1, 0), axis=1, keepdims=True)
    local_down = expert_down % experts
    tags = jnp.where(lane == 0, slot, jnp.where(lane == 1, local_down + 1, 0))
    out_ref[:, :width] = rows_ref[...]
    out_ref[:, width:] = tags.astype(F32).astype(BF16)


def stack_kernel(owners, *refs):
    out_refs = refs[owners:]
    count, full = refs[0].shape
    for which in range(owners):
        here = slice(which * count, (which + 1) * count)
        start = 0
        for part, out_ref in enumerate(out_refs):
            width = out_ref.shape[1] - (LANES if part == 0 else 0)
            out_ref[here, :width] = refs[which][:, start : start + width]
            start += width
        out_refs[0][here, out_refs[0].shape[1] - LANES :] = refs[which][:, full - LANES :]


def pack_kernel(capacity, blocks, first, *refs):
    row_refs = refs[:blocks]
    if first:
        own_ref, other_ref, onehot_ref, held = refs[blocks + 1 :]
    else:
        onehot_ref, own_ref, other_ref, held = refs[blocks:]
    rows, full = row_refs[0].shape
    half = own_ref.shape[0]
    for which, ref in enumerate(row_refs):
        held[which * rows : (which + 1) * rows, :] = ref[...]
    if first:
        me = lax.axis_index("group")
        lane = lax.broadcasted_iota(jnp.int32, (rows, LANES), 1)
        place = lax.broadcasted_iota(jnp.int32, (rows, 2 * half), 1)
        down = lax.broadcasted_iota(jnp.int32, (rows, rows), 0)
        across = lax.broadcasted_iota(jnp.int32, (rows, rows), 1)
        earlier = (across < down).astype(F32).astype(BF16)
        taken = jnp.zeros((1, LANES), F32)
        for which, ref in enumerate(row_refs):
            tags = ref[:, full - LANES :].astype(F32)
            group = tags[:, 0:1].astype(jnp.int32) // capacity
            expert = tags[:, 1:2].astype(jnp.int32) - 1
            side = jnp.where(group == me, 0, jnp.where(group == (me ^ 1), 1, LANES))
            named = jnp.where(lane == 2 * side + expert, 1.0, 0.0)
            ahead = jnp.dot(earlier, named.astype(BF16), preferred_element_type=F32) + taken
            rank = jnp.sum(named * ahead, axis=1, keepdims=True).astype(jnp.int32)
            spot = jnp.where(expert == 0, rank, half - 1 - rank) + side * half
            onehot = (place == spot).astype(F32).astype(BF16)
            onehot_ref[which * rows : (which + 1) * rows, :] = onehot
            taken += jnp.sum(named, axis=0, keepdims=True)
    packed = lax.dot_general(
        onehot_ref[...], held[...], (((0,), (0,)), ((), ())), preferred_element_type=F32
    ).astype(BF16)
    own_ref[...] = packed[:half]
    other_ref[...] = packed[half:]


def load_kernel(after_ref, weight_ref, held_ref, token_ref, sem):
    copies = [
        pltpu.make_async_copy(weight_ref.at[e], held_ref.at[e], sem.at[e])
        for e in range(weight_ref.shape[0])
    ]
    for copy in copies:
        copy.start()
    token_ref[...] = jnp.zeros_like(token_ref)
    for copy in copies:
        copy.wait()


def chosen(own_tag, other_tag):
    full, half = own_tag.shape[1], own_tag.shape[0]
    row = lax.broadcasted_iota(jnp.int32, (half, 1), 0)
    parts, crossed = [], 0.0
    for ref in (own_tag, other_tag):
        part = ref[:, full - LANES :].astype(F32)[:, 1:2]
        wrong = ((part == 1.0) & (row >= half // 2)) | ((part == 2.0) & (row < half // 2))
        crossed = jnp.maximum(crossed, jnp.max(jnp.where(wrong, 1.0, 0.0)))
        parts.append(part)
    return jnp.concatenate(parts, axis=0), crossed > 0.0


def by_expert(own_tag, other_tag, pieces, product, store):
    half = own_tag.shape[0]
    fit = half // 2
    tags, crossed = chosen(own_tag, other_tag)

    @pl.when(jnp.logical_not(crossed))
    def _():
        for expert in range(2):
            here = slice(expert * fit, (expert + 1) * fit)
            for piece in range(pieces):
                value = product(expert, piece, here)
                store(piece, here, value[:fit], value[fit:])

    @pl.when(crossed)
    def _():
        here = slice(0, half)
        for piece in range(pieces):
            value = jnp.where(tags == 2.0, product(1, piece, here), product(0, piece, here))
            store(piece, here, value[:half], value[half:])


def up_first_kernel(step, width, own_ref, other_ref, up_ref, acc_ref):
    half = own_ref.shape[0]

    def product(expert, piece, here):
        rows = jnp.concatenate([own_ref[here, :width], other_ref[here, :width]], axis=0)
        cols = slice(piece * step, (piece + 1) * step)
        return jnp.dot(rows, up_ref[expert, :width, cols], preferred_element_type=F32)

    def store(piece, here, own, other):
        cols = slice(piece * step, (piece + 1) * step)
        acc_ref[here, cols] = own
        acc_ref[half + here.start : half + here.stop, cols] = other

    by_expert(own_ref, other_ref, up_ref.shape[2] // step, product, store)


def up_last_kernel(step, start, width, own_tag, other_tag, own_ref, other_ref, up_ref, acc_ref, hidden_ref):
    half = own_ref.shape[0]

    def product(expert, piece, here):
        rows = jnp.concatenate([own_ref[here, :width], other_ref[here, :width]], axis=0)
        cols = slice(piece * step, (piece + 1) * step)
        return jnp.dot(rows, up_ref[expert, start : start + width, cols], preferred_element_type=F32)

    def store(piece, here, own, other):
        cols = slice(piece * step, (piece + 1) * step)
        for offset, value in ((0, own), (half, other)):
            rows = slice(offset + here.start, offset + here.stop)
            value = acc_ref[rows, cols] + value
            hidden_ref[rows, cols] = (value / (1.0 + jnp.exp(-value))).astype(BF16)

    by_expert(own_tag, other_tag, up_ref.shape[2] // step, product, store)


def down_kernel(step, start, width, own_tag, other_tag, hidden_ref, down_ref, own_ref, other_ref):
    half = own_ref.shape[0]

    def product(expert, piece, here):
        rows = jnp.concatenate(
            [hidden_ref[here, :], hidden_ref[half + here.start : half + here.stop, :]], axis=0
        )
        cols = slice(start + piece * step, start + (piece + 1) * step)
        return jnp.dot(rows, down_ref[expert, :, cols], preferred_element_type=F32)

    def store(piece, here, own, other):
        cols = slice(piece * step, (piece + 1) * step)
        own_ref[here, cols] = own.astype(BF16)
        other_ref[here, cols] = other.astype(BF16)

    by_expert(own_tag, other_tag, width // step, product, store)


def unpack_kernel(onehot_ref, own_ref, other_ref, *out_refs):
    rows = out_refs[0].shape[0]
    slots = jnp.concatenate([own_ref[...], other_ref[...]], axis=0)
    for which, out_ref in enumerate(out_refs):
        onehot = onehot_ref[which * rows : (which + 1) * rows, :]
        out_ref[...] = jnp.dot(onehot, slots, preferred_element_type=F32).astype(BF16)


def add_kernel(chunks, terms, *refs):
    out_refs = refs[chunks * terms :]
    count = out_refs[0].shape[0]
    start = 0
    for chunk in range(chunks):
        blocks = refs[chunk * terms : (chunk + 1) * terms]
        total = blocks[0][...].astype(F32)
        for ref in blocks[1:]:
            total += ref[...].astype(F32)
        total = total.astype(BF16)
        width = total.shape[1]
        for piece, out_ref in enumerate(out_refs):
            out_ref[:, start : start + width] = total[piece * count : (piece + 1) * count]
        start += width


def finish_kernel(weight_ref, *refs):
    out_ref = refs[-1]
    weight = column(weight_ref, out_ref.shape[0])
    total = refs[0][...].astype(F32)
    for ref in refs[1:-1]:
        total += ref[...].astype(F32)
    out_ref[...] = (total.astype(BF16).astype(F32) * weight).astype(BF16)


def body(pair_rows, group_ids, local_ids, route_weight, w_up, w_down):
    groups = lax.axis_size("group")
    inner = lax.axis_size("inner")
    near, turns = 2, groups // 2
    far = inner // near
    count, model = pair_rows.shape
    experts, _, units = w_up.shape
    capacity = 2 * count // groups
    block = far * capacity
    blocks = turns * near
    rows = far * count
    half = blocks * block
    widths = [model // 2, model // 2]
    chunks = len(widths)
    starts = [sum(widths[:i]) for i in range(chunks)]
    step = min(512, units)


    mixed = far == blocks

    def exchange(value, wide, index):
        pairs = []
        for g in range(groups):
            for i in range(inner):
                if wide != (mixed and g % 2 == 1):
                    to = (g ^ 2 * (index // near)) * inner + (i ^ index % near)
                else:
                    to = g * inner + (i ^ near * index)
                pairs.append((g * inner + i, to))
        return lax.ppermute(value, ("group", "inner"), pairs)

    def along_group(value, flip):
        return lax.ppermute(value, "group", [(g, g ^ flip) for g in range(groups)])

    full = model + LANES
    named = group_ids * experts + local_ids
    (tagged,) = call(
        functools.partial(tag_kernel, capacity, experts),
        "tag_rows",
        [((count, full), BF16)],
        [pair_rows, named.reshape(1, count)],
    )

    pieces = [exchange(tagged, False, s) for s in range(far - 1, 0, -1)] + [tagged]
    pieces.reverse()
    parts = call(
        functools.partial(stack_kernel, far),
        "stack_rows",
        [((rows, w + (LANES if i == 0 else 0)), BF16) for i, w in enumerate(widths)],
        pieces,
        flops=STACK_FLOPS,
    )

    room = 4 + 8 * blocks * rows * half * 2 * 2 // MIB
    onehot = None
    slots = []
    for chunk, width in enumerate(widths):
        first = chunk == 0
        arrived = [parts[chunk]] + [exchange(parts[chunk], True, s) for s in range(1, blocks)]
        if first:
            down_held, down_token = call(
                load_kernel,
                "load_down",
                [(w_down.shape, BF16), ((8, LANES), F32)],
                [arrived[-1], w_down],
                specs=[ANY_SPEC, HBM_SPEC],
                scratch=[pltpu.SemaphoreType.DMA((experts,))],
                moved=4 * w_down.size,
                limit=38,
            )
        outs = [((half, width + LANES * first), BF16)] * 2
        if first:
            outs.append(((blocks * rows, 2 * half), BF16))
        packed = call(
            functools.partial(pack_kernel, capacity, blocks, first),
            f"pack_{chunk}",
            outs,
            [*arrived, down_token] if first else [*arrived, onehot],
            scratch=[pltpu.VMEM((blocks * rows, parts[chunk].shape[1]), BF16)],
            limit=room,
            flops=PACK_FLOPS,
        )
        if first:
            onehot = packed[2]
        slots.append((packed[0], along_group(packed[1], 1)))

    work = 2 * 2 * half * experts * units
    acc = call(
        functools.partial(up_first_kernel, step, widths[0]),
        "up_first",
        [((2 * half, units), F32)],
        [*slots[0], w_up],
        limit=8,
        flops=work * widths[0],
    )[0]
    (hidden,) = call(
        functools.partial(up_last_kernel, step, starts[1], widths[1]),
        "up_last",
        [((2 * half, units), BF16)],
        [*slots[0], *slots[1], w_up, acc],
        limit=8,
        flops=work * widths[1],
    )

    terms = [None] * chunks
    for chunk in reversed(range(chunks)):
        width = widths[chunk]
        own, other = call(
            functools.partial(down_kernel, min(512, width), starts[chunk], width),
            f"down_{chunk}",
            [((half, width), BF16)] * 2,
            [*slots[0], hidden, down_held],
            limit=8,
            flops=work * width,
        )
        dense = call(
            unpack_kernel,
            "unpack_slots",
            [((rows, width), BF16)] * blocks,
            [onehot, own, along_group(other, 1)],
            limit=room,
        )
        terms[chunk] = [dense[0]] + [exchange(dense[s], True, s) for s in range(blocks - 1, 0, -1)]
    sums = call(
        functools.partial(add_kernel, chunks, blocks),
        "add_plane",
        [((count, model), BF16)] * far,
        sum(terms, []),
    )
    parts = [sums[0]] + [exchange(sums[s], False, s) for s in range(far - 1, 0, -1)]
    return call(
        finish_kernel, "finish", [((count, model), BF16)], [route_weight.reshape(1, count), *parts]
    )[0]


def solution(mesh):
    placed = (
        P(("group", "inner"), None),
        P(("group", "inner"), None),
        P(("group", "inner"), None),
        P(("group", "inner")),
        P("group", None, "inner"),
        P("group", "inner", None),
    )
    return jax.shard_map(
        body, mesh=mesh, in_specs=placed, out_specs=P(("group", "inner"), None), check_vma=False
    )
```

```python
import functools

import jax
import jax.numpy as jnp
from jax import lax
from jax.experimental import pallas as pl
from jax.experimental.pallas import tpu as pltpu
from jax.sharding import PartitionSpec as P

LANES = 128
STACK_FLOPS = 6 * 10**9
PACK_FLOPS = 15 * 10**8
MIB = 2**20
BF16 = jnp.bfloat16
F32 = jnp.float32
VMEM_SPEC = pl.BlockSpec(memory_space=pltpu.VMEM)
ANY_SPEC = pl.BlockSpec(memory_space=pl.ANY)
HBM_SPEC = pl.BlockSpec(memory_space=pltpu.HBM)


def call(kernel, name, outs, args, limit=4, scratch=(), flops=0, moved=0, specs=None):
    shapes = [jax.ShapeDtypeStruct(shape, dtype) for shape, dtype in outs]
    return pl.pallas_call(
        kernel,
        out_shape=shapes,
        in_specs=specs or [VMEM_SPEC] * len(args),
        out_specs=[VMEM_SPEC] * len(shapes),
        scratch_shapes=list(scratch),
        compiler_params=pltpu.CompilerParams(vmem_limit_bytes=limit * MIB),
        cost_estimate=pl.CostEstimate(flops=flops, bytes_accessed=moved, transcendentals=0),
        name=name,
    )(*args)


def column(row_ref, count):
    across = lax.broadcasted_iota(jnp.int32, (count, count), 1)
    down = lax.broadcasted_iota(jnp.int32, (count, count), 0)
    spread = jnp.broadcast_to(row_ref[...], (count, count))
    return jnp.sum(jnp.where(across == down, spread, jnp.zeros_like(spread)), axis=1, keepdims=True)


def tag_kernel(capacity, experts, rows_ref, expert_ref, out_ref):
    count, width = rows_ref.shape
    across = lax.broadcasted_iota(jnp.int32, (count, count), 1)
    down = lax.broadcasted_iota(jnp.int32, (count, count), 0)
    lane = lax.broadcasted_iota(jnp.int32, (count, LANES), 1)
    group_across = expert_ref[...] // experts
    expert_down = column(expert_ref, count)
    group_down = expert_down // experts
    before = (jnp.broadcast_to(group_across, (count, count)) == group_down) & (across < down)
    slot = group_down * capacity + jnp.sum(jnp.where(before, 1, 0), axis=1, keepdims=True)
    local_down = expert_down % experts
    tags = jnp.where(lane == 0, slot, jnp.where(lane == 1, local_down + 1, 0))
    out_ref[:, :width] = rows_ref[...]
    out_ref[:, width:] = tags.astype(F32).astype(BF16)


def stack_kernel(owners, *refs):
    out_refs = refs[owners:]
    count, full = refs[0].shape
    for which in range(owners):
        here = slice(which * count, (which + 1) * count)
        start = 0
        for part, out_ref in enumerate(out_refs):
            width = out_ref.shape[1] - (LANES if part == 0 else 0)
            out_ref[here, :width] = refs[which][:, start : start + width]
            start += width
        out_refs[0][here, out_refs[0].shape[1] - LANES :] = refs[which][:, full - LANES :]


def pack_kernel(capacity, blocks, first, *refs):
    row_refs = refs[:blocks]
    if first:
        own_ref, other_ref, onehot_ref, held = refs[blocks + 1 :]
    else:
        onehot_ref, own_ref, other_ref, held = refs[blocks:]
    rows, full = row_refs[0].shape
    half = own_ref.shape[0]
    for which, ref in enumerate(row_refs):
        held[which * rows : (which + 1) * rows, :] = ref[...]
    if first:
        me = lax.axis_index("group")
        lane = lax.broadcasted_iota(jnp.int32, (rows, LANES), 1)
        place = lax.broadcasted_iota(jnp.int32, (rows, 2 * half), 1)
        down = lax.broadcasted_iota(jnp.int32, (rows, rows), 0)
        across = lax.broadcasted_iota(jnp.int32, (rows, rows), 1)
        earlier = (across < down).astype(F32).astype(BF16)
        taken = jnp.zeros((1, LANES), F32)
        for which, ref in enumerate(row_refs):
            tags = ref[:, full - LANES :].astype(F32)
            group = tags[:, 0:1].astype(jnp.int32) // capacity
            expert = tags[:, 1:2].astype(jnp.int32) - 1
            side = jnp.where(group == me, 0, jnp.where(group == (me ^ 1), 1, LANES))
            named = jnp.where(lane == 2 * side + expert, 1.0, 0.0)
            ahead = jnp.dot(earlier, named.astype(BF16), preferred_element_type=F32) + taken
            rank = jnp.sum(named * ahead, axis=1, keepdims=True).astype(jnp.int32)
            spot = jnp.where(expert == 0, rank, half - 1 - rank) + side * half
            onehot = (place == spot).astype(F32).astype(BF16)
            onehot_ref[which * rows : (which + 1) * rows, :] = onehot
            taken += jnp.sum(named, axis=0, keepdims=True)
    packed = lax.dot_general(
        onehot_ref[...], held[...], (((0,), (0,)), ((), ())), preferred_element_type=F32
    ).astype(BF16)
    own_ref[...] = packed[:half]
    other_ref[...] = packed[half:]


def load_kernel(after_ref, weight_ref, held_ref, token_ref, sem):
    copies = [
        pltpu.make_async_copy(weight_ref.at[e], held_ref.at[e], sem.at[e])
        for e in range(weight_ref.shape[0])
    ]
    for copy in copies:
        copy.start()
    token_ref[...] = jnp.zeros_like(token_ref)
    for copy in copies:
        copy.wait()


def chosen(own_tag, other_tag):
    full, half = own_tag.shape[1], own_tag.shape[0]
    row = lax.broadcasted_iota(jnp.int32, (half, 1), 0)
    parts, crossed = [], 0.0
    for ref in (own_tag, other_tag):
        part = ref[:, full - LANES :].astype(F32)[:, 1:2]
        wrong = ((part == 1.0) & (row >= half // 2)) | ((part == 2.0) & (row < half // 2))
        crossed = jnp.maximum(crossed, jnp.max(jnp.where(wrong, 1.0, 0.0)))
        parts.append(part)
    return jnp.concatenate(parts, axis=0), crossed > 0.0


def by_expert(own_tag, other_tag, pieces, product, store):
    half = own_tag.shape[0]
    fit = half // 2
    tags, crossed = chosen(own_tag, other_tag)

    @pl.when(jnp.logical_not(crossed))
    def _():
        for expert in range(2):
            here = slice(expert * fit, (expert + 1) * fit)
            for piece in range(pieces):
                value = product(expert, piece, here)
                store(piece, here, value[:fit], value[fit:])

    @pl.when(crossed)
    def _():
        here = slice(0, half)
        for piece in range(pieces):
            value = jnp.where(tags == 2.0, product(1, piece, here), product(0, piece, here))
            store(piece, here, value[:half], value[half:])


def up_first_kernel(step, width, own_ref, other_ref, up_ref, acc_ref):
    half = own_ref.shape[0]

    def product(expert, piece, here):
        rows = jnp.concatenate([own_ref[here, :width], other_ref[here, :width]], axis=0)
        cols = slice(piece * step, (piece + 1) * step)
        return jnp.dot(rows, up_ref[expert, :width, cols], preferred_element_type=F32)

    def store(piece, here, own, other):
        cols = slice(piece * step, (piece + 1) * step)
        acc_ref[here, cols] = own
        acc_ref[half + here.start : half + here.stop, cols] = other

    by_expert(own_ref, other_ref, up_ref.shape[2] // step, product, store)


def up_last_kernel(step, start, width, own_tag, other_tag, own_ref, other_ref, up_ref, acc_ref, hidden_ref):
    half = own_ref.shape[0]

    def product(expert, piece, here):
        rows = jnp.concatenate([own_ref[here, :width], other_ref[here, :width]], axis=0)
        cols = slice(piece * step, (piece + 1) * step)
        return jnp.dot(rows, up_ref[expert, start : start + width, cols], preferred_element_type=F32)

    def store(piece, here, own, other):
        cols = slice(piece * step, (piece + 1) * step)
        for offset, value in ((0, own), (half, other)):
            rows = slice(offset + here.start, offset + here.stop)
            value = acc_ref[rows, cols] + value
            hidden_ref[rows, cols] = (value / (1.0 + jnp.exp(-value))).astype(BF16)

    by_expert(own_tag, other_tag, up_ref.shape[2] // step, product, store)


def down_kernel(step, start, width, own_tag, other_tag, hidden_ref, down_ref, own_ref, other_ref):
    half = own_ref.shape[0]

    def product(expert, piece, here):
        rows = jnp.concatenate(
            [hidden_ref[here, :], hidden_ref[half + here.start : half + here.stop, :]], axis=0
        )
        cols = slice(start + piece * step, start + (piece + 1) * step)
        return jnp.dot(rows, down_ref[expert, :, cols], preferred_element_type=F32)

    def store(piece, here, own, other):
        cols = slice(piece * step, (piece + 1) * step)
        own_ref[here, cols] = own.astype(BF16)
        other_ref[here, cols] = other.astype(BF16)

    by_expert(own_tag, other_tag, width // step, product, store)


def unpack_kernel(onehot_ref, own_ref, other_ref, *out_refs):
    rows = out_refs[0].shape[0]
    slots = jnp.concatenate([own_ref[...], other_ref[...]], axis=0)
    dense = jnp.dot(onehot_ref[...], slots, preferred_element_type=F32).astype(BF16)
    for which, out_ref in enumerate(out_refs):
        out_ref[...] = dense[which * rows : (which + 1) * rows]


def add_kernel(chunks, terms, *refs):
    out_refs = refs[chunks * terms :]
    count = out_refs[0].shape[0]
    start = 0
    for chunk in range(chunks):
        blocks = refs[chunk * terms : (chunk + 1) * terms]
        total = blocks[0][...].astype(F32)
        for ref in blocks[1:]:
            total += ref[...].astype(F32)
        total = total.astype(BF16)
        width = total.shape[1]
        for piece, out_ref in enumerate(out_refs):
            out_ref[:, start : start + width] = total[piece * count : (piece + 1) * count]
        start += width


def finish_kernel(weight_ref, *refs):
    out_ref = refs[-1]
    weight = column(weight_ref, out_ref.shape[0])
    total = refs[0][...].astype(F32)
    for ref in refs[1:-1]:
        total += ref[...].astype(F32)
    out_ref[...] = (total.astype(BF16).astype(F32) * weight).astype(BF16)


def body(pair_rows, group_ids, local_ids, route_weight, w_up, w_down):
    groups = lax.axis_size("group")
    inner = lax.axis_size("inner")
    near, turns = 2, groups // 2
    far = inner // near
    count, model = pair_rows.shape
    experts, _, units = w_up.shape
    capacity = 2 * count // groups
    block = far * capacity
    blocks = turns * near
    rows = far * count
    half = blocks * block
    widths = [model // 2, model // 2]
    chunks = len(widths)
    starts = [sum(widths[:i]) for i in range(chunks)]
    step = min(256, units)


    mixed = far == blocks

    def exchange(value, wide, index):
        pairs = []
        for g in range(groups):
            for i in range(inner):
                if wide != (mixed and g % 2 == 1):
                    to = (g ^ 2 * (index // near)) * inner + (i ^ index % near)
                else:
                    to = g * inner + (i ^ near * index)
                pairs.append((g * inner + i, to))
        return lax.ppermute(value, ("group", "inner"), pairs)

    def along_group(value, flip):
        return lax.ppermute(value, "group", [(g, g ^ flip) for g in range(groups)])

    full = model + LANES
    named = group_ids * experts + local_ids
    (tagged,) = call(
        functools.partial(tag_kernel, capacity, experts),
        "tag_rows",
        [((count, full), BF16)],
        [pair_rows, named.reshape(1, count)],
    )

    pieces = [exchange(tagged, False, s) for s in range(far - 1, 0, -1)] + [tagged]
    pieces.reverse()
    parts = call(
        functools.partial(stack_kernel, far),
        "stack_rows",
        [((rows, w + (LANES if i == 0 else 0)), BF16) for i, w in enumerate(widths)],
        pieces,
        flops=STACK_FLOPS,
    )

    room = 4 + 8 * blocks * rows * half * 2 * 2 // MIB
    onehot = None
    slots = []
    for chunk, width in enumerate(widths):
        first = chunk == 0
        arrived = [parts[chunk]] + [exchange(parts[chunk], True, s) for s in range(1, blocks)]
        if first:
            down_held, down_token = call(
                load_kernel,
                "load_down",
                [(w_down.shape, BF16), ((8, LANES), F32)],
                [arrived[-1], w_down],
                specs=[ANY_SPEC, HBM_SPEC],
                scratch=[pltpu.SemaphoreType.DMA((experts,))],
                moved=4 * w_down.size,
                limit=38,
            )
        outs = [((half, width + LANES * first), BF16)] * 2
        if first:
            outs.append(((blocks * rows, 2 * half), BF16))
        packed = call(
            functools.partial(pack_kernel, capacity, blocks, first),
            f"pack_{chunk}",
            outs,
            [*arrived, down_token] if first else [*arrived, onehot],
            scratch=[pltpu.VMEM((blocks * rows, parts[chunk].shape[1]), BF16)],
            limit=room,
            flops=PACK_FLOPS,
        )
        if first:
            onehot = packed[2]
        slots.append((packed[0], along_group(packed[1], 1)))

    work = 2 * 2 * half * experts * units
    acc = call(
        functools.partial(up_first_kernel, step, widths[0]),
        "up_first",
        [((2 * half, units), F32)],
        [*slots[0], w_up],
        limit=8,
        flops=work * widths[0],
    )[0]
    (hidden,) = call(
        functools.partial(up_last_kernel, step, starts[1], widths[1]),
        "up_last",
        [((2 * half, units), BF16)],
        [*slots[0], *slots[1], w_up, acc],
        limit=8,
        flops=work * widths[1],
    )

    terms = [None] * chunks
    for chunk in reversed(range(chunks)):
        width = widths[chunk]
        own, other = call(
            functools.partial(down_kernel, min(256, width), starts[chunk], width),
            f"down_{chunk}",
            [((half, width), BF16)] * 2,
            [*slots[0], hidden, down_held],
            limit=8,
            flops=work * width,
        )
        dense = call(
            unpack_kernel,
            "unpack_slots",
            [((rows, width), BF16)] * blocks,
            [onehot, own, along_group(other, 1)],
            limit=room,
        )
        terms[chunk] = [dense[0]] + [exchange(dense[s], True, s) for s in range(blocks - 1, 0, -1)]
    sums = call(
        functools.partial(add_kernel, chunks, blocks),
        "add_plane",
        [((count, model), BF16)] * far,
        sum(terms, []),
    )
    parts = [sums[0]] + [exchange(sums[s], False, s) for s in range(far - 1, 0, -1)]
    return call(
        finish_kernel, "finish", [((count, model), BF16)], [route_weight.reshape(1, count), *parts]
    )[0]


def solution(mesh):
    placed = (
        P(("group", "inner"), None),
        P(("group", "inner"), None),
        P(("group", "inner"), None),
        P(("group", "inner")),
        P("group", None, "inner"),
        P("group", "inner", None),
    )
    return jax.shard_map(
        body, mesh=mesh, in_specs=placed, out_specs=P(("group", "inner"), None), check_vma=False
    )
```

```python
import functools

import jax
import jax.numpy as jnp
from jax import lax
from jax.experimental import pallas as pl
from jax.experimental.pallas import tpu as pltpu
from jax.sharding import PartitionSpec as P

LANES = 128
STACK_FLOPS = 6 * 10**9
PACK_FLOPS = 15 * 10**8
MIB = 2**20
BF16 = jnp.bfloat16
F32 = jnp.float32
VMEM_SPEC = pl.BlockSpec(memory_space=pltpu.VMEM)
ANY_SPEC = pl.BlockSpec(memory_space=pl.ANY)
HBM_SPEC = pl.BlockSpec(memory_space=pltpu.HBM)


def call(kernel, name, outs, args, limit=4, scratch=(), flops=0, moved=0, specs=None):
    shapes = [jax.ShapeDtypeStruct(shape, dtype) for shape, dtype in outs]
    return pl.pallas_call(
        kernel,
        out_shape=shapes,
        in_specs=specs or [VMEM_SPEC] * len(args),
        out_specs=[VMEM_SPEC] * len(shapes),
        scratch_shapes=list(scratch),
        compiler_params=pltpu.CompilerParams(vmem_limit_bytes=limit * MIB),
        cost_estimate=pl.CostEstimate(flops=flops, bytes_accessed=moved, transcendentals=0),
        name=name,
    )(*args)


def column(row_ref, count):
    across = lax.broadcasted_iota(jnp.int32, (count, count), 1)
    down = lax.broadcasted_iota(jnp.int32, (count, count), 0)
    spread = jnp.broadcast_to(row_ref[...], (count, count))
    return jnp.sum(jnp.where(across == down, spread, jnp.zeros_like(spread)), axis=1, keepdims=True)


def tag_kernel(capacity, experts, rows_ref, expert_ref, out_ref):
    count, width = rows_ref.shape
    across = lax.broadcasted_iota(jnp.int32, (count, count), 1)
    down = lax.broadcasted_iota(jnp.int32, (count, count), 0)
    lane = lax.broadcasted_iota(jnp.int32, (count, LANES), 1)
    group_across = expert_ref[...] // experts
    expert_down = column(expert_ref, count)
    group_down = expert_down // experts
    before = (jnp.broadcast_to(group_across, (count, count)) == group_down) & (across < down)
    slot = group_down * capacity + jnp.sum(jnp.where(before, 1, 0), axis=1, keepdims=True)
    local_down = expert_down % experts
    tags = jnp.where(lane == 0, slot, jnp.where(lane == 1, local_down + 1, 0))
    out_ref[:, :width] = rows_ref[...]
    out_ref[:, width:] = tags.astype(F32).astype(BF16)


def stack_kernel(owners, *refs):
    out_refs = refs[owners:]
    count, full = refs[0].shape
    for which in range(owners):
        here = slice(which * count, (which + 1) * count)
        start = 0
        for part, out_ref in enumerate(out_refs):
            width = out_ref.shape[1] - (LANES if part == 0 else 0)
            out_ref[here, :width] = refs[which][:, start : start + width]
            start += width
        out_refs[0][here, out_refs[0].shape[1] - LANES :] = refs[which][:, full - LANES :]


def pack_kernel(capacity, blocks, first, *refs):
    row_refs = refs[:blocks]
    if first:
        own_ref, other_ref, onehot_ref, held = refs[blocks + 1 :]
    else:
        onehot_ref, own_ref, other_ref, held = refs[blocks:]
    rows, full = row_refs[0].shape
    half = own_ref.shape[0]
    for which, ref in enumerate(row_refs):
        held[which * rows : (which + 1) * rows, :] = ref[...]
    if first:
        me = lax.axis_index("group")
        lane = lax.broadcasted_iota(jnp.int32, (rows, LANES), 1)
        place = lax.broadcasted_iota(jnp.int32, (rows, 2 * half), 1)
        down = lax.broadcasted_iota(jnp.int32, (rows, rows), 0)
        across = lax.broadcasted_iota(jnp.int32, (rows, rows), 1)
        earlier = (across < down).astype(F32).astype(BF16)
        taken = jnp.zeros((1, LANES), F32)
        for which, ref in enumerate(row_refs):
            tags = ref[:, full - LANES :].astype(F32)
            group = tags[:, 0:1].astype(jnp.int32) // capacity
            expert = tags[:, 1:2].astype(jnp.int32) - 1
            side = jnp.where(group == me, 0, jnp.where(group == (me ^ 1), 1, LANES))
            named = jnp.where(lane == 2 * side + expert, 1.0, 0.0)
            ahead = jnp.dot(earlier, named.astype(BF16), preferred_element_type=F32) + taken
            rank = jnp.sum(named * ahead, axis=1, keepdims=True).astype(jnp.int32)
            spot = jnp.where(expert == 0, rank, half - 1 - rank) + side * half
            onehot = (place == spot).astype(F32).astype(BF16)
            onehot_ref[which * rows : (which + 1) * rows, :] = onehot
            taken += jnp.sum(named, axis=0, keepdims=True)
    packed = lax.dot_general(
        onehot_ref[...], held[...], (((0,), (0,)), ((), ())), preferred_element_type=F32
    ).astype(BF16)
    own_ref[...] = packed[:half]
    other_ref[...] = packed[half:]


def load_kernel(after_ref, weight_ref, held_ref, token_ref, sem):
    copies = [
        pltpu.make_async_copy(weight_ref.at[e], held_ref.at[e], sem.at[e])
        for e in range(weight_ref.shape[0])
    ]
    for copy in copies:
        copy.start()
    token_ref[...] = jnp.zeros_like(token_ref)
    for copy in copies:
        copy.wait()


def by_expert(own_tag, other_tag, pieces, product, store):
    half, full = own_tag.shape
    tags = [ref[:, full - LANES :].astype(F32)[:, 1:2] for ref in (own_tag, other_tag)]
    tags = jnp.concatenate(tags, axis=0)
    row = lax.broadcasted_iota(jnp.int32, (2 * half, 1), 0) % half
    first = jnp.max(jnp.where(tags == 1.0, row + 1, 0).astype(F32))
    last = jnp.max(jnp.where(tags == 2.0, half - row, 0).astype(F32))
    free = jnp.bool_(True)
    for cut in (half // 2, half * 5 // 8, half * 3 // 8):
        fits = (first <= float(cut)) & (last <= float(half - cut))

        @pl.when(free & fits)
        def _():
            for expert, here in enumerate((slice(0, cut), slice(cut, half))):
                count = here.stop - here.start
                for piece in range(pieces):
                    value = product(expert, piece, here)
                    store(piece, here, value[:count], value[count:])

        free = free & jnp.logical_not(fits)

    @pl.when(free)
    def _():
        here = slice(0, half)
        for piece in range(pieces):
            value = jnp.where(tags == 2.0, product(1, piece, here), product(0, piece, here))
            store(piece, here, value[:half], value[half:])


def up_first_kernel(step, width, own_ref, other_ref, up_ref, acc_ref):
    half = own_ref.shape[0]

    def product(expert, piece, here):
        rows = jnp.concatenate([own_ref[here, :width], other_ref[here, :width]], axis=0)
        cols = slice(piece * step, (piece + 1) * step)
        return jnp.dot(rows, up_ref[expert, :width, cols], preferred_element_type=F32)

    def store(piece, here, own, other):
        cols = slice(piece * step, (piece + 1) * step)
        acc_ref[here, cols] = own
        acc_ref[half + here.start : half + here.stop, cols] = other

    by_expert(own_ref, other_ref, up_ref.shape[2] // step, product, store)


def up_last_kernel(step, start, width, own_tag, other_tag, own_ref, other_ref, up_ref, acc_ref, hidden_ref):
    half = own_ref.shape[0]

    def product(expert, piece, here):
        rows = jnp.concatenate([own_ref[here, :width], other_ref[here, :width]], axis=0)
        cols = slice(piece * step, (piece + 1) * step)
        return jnp.dot(rows, up_ref[expert, start : start + width, cols], preferred_element_type=F32)

    def store(piece, here, own, other):
        cols = slice(piece * step, (piece + 1) * step)
        for offset, value in ((0, own), (half, other)):
            rows = slice(offset + here.start, offset + here.stop)
            value = acc_ref[rows, cols] + value
            hidden_ref[rows, cols] = (value / (1.0 + jnp.exp(-value))).astype(BF16)

    by_expert(own_tag, other_tag, up_ref.shape[2] // step, product, store)


def down_kernel(step, start, width, own_tag, other_tag, hidden_ref, down_ref, own_ref, other_ref):
    half = own_ref.shape[0]

    def product(expert, piece, here):
        rows = jnp.concatenate(
            [hidden_ref[here, :], hidden_ref[half + here.start : half + here.stop, :]], axis=0
        )
        cols = slice(start + piece * step, start + (piece + 1) * step)
        return jnp.dot(rows, down_ref[expert, :, cols], preferred_element_type=F32)

    def store(piece, here, own, other):
        cols = slice(piece * step, (piece + 1) * step)
        own_ref[here, cols] = own.astype(BF16)
        other_ref[here, cols] = other.astype(BF16)

    by_expert(own_tag, other_tag, width // step, product, store)


def unpack_kernel(onehot_ref, own_ref, other_ref, *out_refs):
    rows = out_refs[0].shape[0]
    slots = jnp.concatenate([own_ref[...], other_ref[...]], axis=0)
    dense = jnp.dot(onehot_ref[...], slots, preferred_element_type=F32).astype(BF16)
    for which, out_ref in enumerate(out_refs):
        out_ref[...] = dense[which * rows : (which + 1) * rows]


def add_kernel(chunks, terms, *refs):
    out_refs = refs[chunks * terms :]
    count = out_refs[0].shape[0]
    start = 0
    for chunk in range(chunks):
        blocks = refs[chunk * terms : (chunk + 1) * terms]
        total = blocks[0][...].astype(F32)
        for ref in blocks[1:]:
            total += ref[...].astype(F32)
        total = total.astype(BF16)
        width = total.shape[1]
        for piece, out_ref in enumerate(out_refs):
            out_ref[:, start : start + width] = total[piece * count : (piece + 1) * count]
        start += width


def finish_kernel(weight_ref, *refs):
    out_ref = refs[-1]
    weight = column(weight_ref, out_ref.shape[0])
    total = refs[0][...].astype(F32)
    for ref in refs[1:-1]:
        total += ref[...].astype(F32)
    out_ref[...] = (total.astype(BF16).astype(F32) * weight).astype(BF16)


def body(pair_rows, group_ids, local_ids, route_weight, w_up, w_down):
    groups = lax.axis_size("group")
    inner = lax.axis_size("inner")
    near, turns = 2, groups // 2
    far = inner // near
    count, model = pair_rows.shape
    experts, _, units = w_up.shape
    capacity = 2 * count // groups
    block = far * capacity
    blocks = turns * near
    rows = far * count
    half = blocks * block
    widths = [model // 2, model // 2]
    chunks = len(widths)
    starts = [sum(widths[:i]) for i in range(chunks)]
    step = min(256, units)


    mixed = far == blocks

    def exchange(value, wide, index):
        pairs = []
        for g in range(groups):
            for i in range(inner):
                if wide != (mixed and g % 2 == 1):
                    to = (g ^ 2 * (index // near)) * inner + (i ^ index % near)
                else:
                    to = g * inner + (i ^ near * index)
                pairs.append((g * inner + i, to))
        return lax.ppermute(value, ("group", "inner"), pairs)

    def along_group(value, flip):
        return lax.ppermute(value, "group", [(g, g ^ flip) for g in range(groups)])

    full = model + LANES
    named = group_ids * experts + local_ids
    (tagged,) = call(
        functools.partial(tag_kernel, capacity, experts),
        "tag_rows",
        [((count, full), BF16)],
        [pair_rows, named.reshape(1, count)],
    )

    pieces = [exchange(tagged, False, s) for s in range(far - 1, 0, -1)] + [tagged]
    pieces.reverse()
    parts = call(
        functools.partial(stack_kernel, far),
        "stack_rows",
        [((rows, w + (LANES if i == 0 else 0)), BF16) for i, w in enumerate(widths)],
        pieces,
        flops=STACK_FLOPS,
    )

    room = 4 + 8 * blocks * rows * half * 2 * 2 // MIB
    onehot = None
    slots = []
    for chunk, width in enumerate(widths):
        first = chunk == 0
        arrived = [parts[chunk]] + [exchange(parts[chunk], True, s) for s in range(1, blocks)]
        if first:
            down_held, down_token = call(
                load_kernel,
                "load_down",
                [(w_down.shape, BF16), ((8, LANES), F32)],
                [arrived[-1], w_down],
                specs=[ANY_SPEC, HBM_SPEC],
                scratch=[pltpu.SemaphoreType.DMA((experts,))],
                moved=4 * w_down.size,
                limit=38,
            )
        outs = [((half, width + LANES * first), BF16)] * 2
        if first:
            outs.append(((blocks * rows, 2 * half), BF16))
        packed = call(
            functools.partial(pack_kernel, capacity, blocks, first),
            f"pack_{chunk}",
            outs,
            [*arrived, down_token] if first else [*arrived, onehot],
            scratch=[pltpu.VMEM((blocks * rows, parts[chunk].shape[1]), BF16)],
            limit=room,
            flops=PACK_FLOPS,
        )
        if first:
            onehot = packed[2]
        slots.append((packed[0], along_group(packed[1], 1)))

    work = 2 * 2 * half * experts * units
    acc = call(
        functools.partial(up_first_kernel, step, widths[0]),
        "up_first",
        [((2 * half, units), F32)],
        [*slots[0], w_up],
        limit=8,
        flops=work * widths[0],
    )[0]
    (hidden,) = call(
        functools.partial(up_last_kernel, step, starts[1], widths[1]),
        "up_last",
        [((2 * half, units), BF16)],
        [*slots[0], *slots[1], w_up, acc],
        limit=8,
        flops=work * widths[1],
    )

    terms = [None] * chunks
    for chunk in reversed(range(chunks)):
        width = widths[chunk]
        own, other = call(
            functools.partial(down_kernel, min(256, width), starts[chunk], width),
            f"down_{chunk}",
            [((half, width), BF16)] * 2,
            [*slots[0], hidden, down_held],
            limit=8,
            flops=work * width,
        )
        dense = call(
            unpack_kernel,
            "unpack_slots",
            [((rows, width), BF16)] * blocks,
            [onehot, own, along_group(other, 1)],
            limit=room,
        )
        terms[chunk] = [dense[0]] + [exchange(dense[s], True, s) for s in range(blocks - 1, 0, -1)]
    sums = call(
        functools.partial(add_kernel, chunks, blocks),
        "add_plane",
        [((count, model), BF16)] * far,
        sum(terms, []),
    )
    parts = [sums[0]] + [exchange(sums[s], False, s) for s in range(far - 1, 0, -1)]
    return call(
        finish_kernel, "finish", [((count, model), BF16)], [route_weight.reshape(1, count), *parts]
    )[0]


def solution(mesh):
    placed = (
        P(("group", "inner"), None),
        P(("group", "inner"), None),
        P(("group", "inner"), None),
        P(("group", "inner")),
        P("group", None, "inner"),
        P("group", "inner", None),
    )
    return jax.shard_map(
        body, mesh=mesh, in_specs=placed, out_specs=P(("group", "inner"), None), check_vma=False
    )
```

```python
import functools

import jax
import jax.numpy as jnp
from jax import lax
from jax.experimental import pallas as pl
from jax.experimental.pallas import tpu as pltpu
from jax.sharding import PartitionSpec as P

LANES = 128
STACK_FLOPS = 6 * 10**9
PACK_FLOPS = 15 * 10**8
MIB = 2**20
BF16 = jnp.bfloat16
F32 = jnp.float32
VMEM_SPEC = pl.BlockSpec(memory_space=pltpu.VMEM)
ANY_SPEC = pl.BlockSpec(memory_space=pl.ANY)
HBM_SPEC = pl.BlockSpec(memory_space=pltpu.HBM)


def call(kernel, name, outs, args, limit=4, scratch=(), flops=0, moved=0, specs=None):
    shapes = [jax.ShapeDtypeStruct(shape, dtype) for shape, dtype in outs]
    return pl.pallas_call(
        kernel,
        out_shape=shapes,
        in_specs=specs or [VMEM_SPEC] * len(args),
        out_specs=[VMEM_SPEC] * len(shapes),
        scratch_shapes=list(scratch),
        compiler_params=pltpu.CompilerParams(vmem_limit_bytes=limit * MIB),
        cost_estimate=pl.CostEstimate(flops=flops, bytes_accessed=moved, transcendentals=0),
        name=name,
    )(*args)


def column(row_ref, count):
    across = lax.broadcasted_iota(jnp.int32, (count, count), 1)
    down = lax.broadcasted_iota(jnp.int32, (count, count), 0)
    spread = jnp.broadcast_to(row_ref[...], (count, count))
    return jnp.sum(jnp.where(across == down, spread, jnp.zeros_like(spread)), axis=1, keepdims=True)


def tag_kernel(capacity, experts, rows_ref, expert_ref, out_ref):
    count, width = rows_ref.shape
    across = lax.broadcasted_iota(jnp.int32, (count, count), 1)
    down = lax.broadcasted_iota(jnp.int32, (count, count), 0)
    lane = lax.broadcasted_iota(jnp.int32, (count, LANES), 1)
    group_across = expert_ref[...] // experts
    expert_down = column(expert_ref, count)
    group_down = expert_down // experts
    before = (jnp.broadcast_to(group_across, (count, count)) == group_down) & (across < down)
    slot = group_down * capacity + jnp.sum(jnp.where(before, 1, 0), axis=1, keepdims=True)
    local_down = expert_down % experts
    tags = jnp.where(lane == 0, slot, jnp.where(lane == 1, local_down + 1, 0))
    out_ref[:, :width] = rows_ref[...]
    out_ref[:, width:] = tags.astype(F32).astype(BF16)


def stack_kernel(owners, *refs):
    out_refs = refs[owners:]
    count, full = refs[0].shape
    for which in range(owners):
        here = slice(which * count, (which + 1) * count)
        start = 0
        for part, out_ref in enumerate(out_refs):
            width = out_ref.shape[1] - (LANES if part == 0 else 0)
            out_ref[here, :width] = refs[which][:, start : start + width]
            start += width
        out_refs[0][here, out_refs[0].shape[1] - LANES :] = refs[which][:, full - LANES :]


def pack_kernel(capacity, blocks, first, *refs):
    row_refs = refs[:blocks]
    if first:
        own_ref, other_ref, onehot_ref, held = refs[blocks + 1 :]
    else:
        onehot_ref, own_ref, other_ref, held = refs[blocks:]
    rows, full = row_refs[0].shape
    half = own_ref.shape[0]
    for which, ref in enumerate(row_refs):
        held[which * rows : (which + 1) * rows, :] = ref[...]
    if first:
        me = lax.axis_index("group")
        lane = lax.broadcasted_iota(jnp.int32, (rows, LANES), 1)
        place = lax.broadcasted_iota(jnp.int32, (rows, 2 * half), 1)
        down = lax.broadcasted_iota(jnp.int32, (rows, rows), 0)
        across = lax.broadcasted_iota(jnp.int32, (rows, rows), 1)
        earlier = (across < down).astype(F32).astype(BF16)
        taken = jnp.zeros((1, LANES), F32)
        for which, ref in enumerate(row_refs):
            tags = ref[:, full - LANES :].astype(F32)
            group = tags[:, 0:1].astype(jnp.int32) // capacity
            expert = tags[:, 1:2].astype(jnp.int32) - 1
            side = jnp.where(group == me, 0, jnp.where(group == (me ^ 1), 1, LANES))
            named = jnp.where(lane == 2 * side + expert, 1.0, 0.0)
            ahead = jnp.dot(earlier, named.astype(BF16), preferred_element_type=F32) + taken
            rank = jnp.sum(named * ahead, axis=1, keepdims=True).astype(jnp.int32)
            spot = jnp.where(expert == 0, rank, half - 1 - rank) + side * half
            onehot = (place == spot).astype(F32).astype(BF16)
            onehot_ref[which * rows : (which + 1) * rows, :] = onehot
            taken += jnp.sum(named, axis=0, keepdims=True)
    packed = lax.dot_general(
        onehot_ref[...], held[...], (((0,), (0,)), ((), ())), preferred_element_type=F32
    ).astype(BF16)
    own_ref[...] = packed[:half]
    other_ref[...] = packed[half:]


def load_kernel(after_ref, weight_ref, held_ref, token_ref, sem):
    copies = [
        pltpu.make_async_copy(weight_ref.at[e], held_ref.at[e], sem.at[e])
        for e in range(weight_ref.shape[0])
    ]
    for copy in copies:
        copy.start()
    token_ref[...] = jnp.zeros_like(token_ref)
    for copy in copies:
        copy.wait()


def chosen(own_tag, other_tag):
    full, half = own_tag.shape[1], own_tag.shape[0]
    row = lax.broadcasted_iota(jnp.int32, (half, 1), 0)
    parts, crossed = [], 0.0
    for ref in (own_tag, other_tag):
        part = ref[:, full - LANES :].astype(F32)[:, 1:2]
        wrong = ((part == 1.0) & (row >= half * 5 // 8)) | ((part == 2.0) & (row < half * 3 // 8))
        crossed = jnp.maximum(crossed, jnp.max(jnp.where(wrong, 1.0, 0.0)))
        parts.append(part)
    return jnp.concatenate(parts, axis=0), crossed > 0.0


def by_expert(own_tag, other_tag, pieces, product, store):
    half = own_tag.shape[0]
    low, high = half * 3 // 8, half * 5 // 8
    tags, crossed = chosen(own_tag, other_tag)

    def joined(first, last, tag):
        shared = jnp.where(tag[low:high] == 2.0, last[: high - low], first[low:])
        return jnp.concatenate([first[:low], shared, last[high - low :]], axis=0)

    @pl.when(jnp.logical_not(crossed))
    def _():
        for piece in range(pieces):
            first = product(0, piece, slice(0, high))
            last = product(1, piece, slice(low, half))
            own = joined(first[:high], last[:high], tags[:half])
            other = joined(first[high:], last[high:], tags[half:])
            store(piece, slice(0, half), own, other)

    @pl.when(crossed)
    def _():
        here = slice(0, half)
        for piece in range(pieces):
            value = jnp.where(tags == 2.0, product(1, piece, here), product(0, piece, here))
            store(piece, here, value[:half], value[half:])


def up_first_kernel(step, width, own_ref, other_ref, up_ref, acc_ref):
    half = own_ref.shape[0]

    def product(expert, piece, here):
        rows = jnp.concatenate([own_ref[here, :width], other_ref[here, :width]], axis=0)
        cols = slice(piece * step, (piece + 1) * step)
        return jnp.dot(rows, up_ref[expert, :width, cols], preferred_element_type=F32)

    def store(piece, here, own, other):
        cols = slice(piece * step, (piece + 1) * step)
        acc_ref[here, cols] = own
        acc_ref[half + here.start : half + here.stop, cols] = other

    by_expert(own_ref, other_ref, up_ref.shape[2] // step, product, store)


def up_last_kernel(step, start, width, own_tag, other_tag, own_ref, other_ref, up_ref, acc_ref, hidden_ref):
    half = own_ref.shape[0]

    def product(expert, piece, here):
        rows = jnp.concatenate([own_ref[here, :width], other_ref[here, :width]], axis=0)
        cols = slice(piece * step, (piece + 1) * step)
        return jnp.dot(rows, up_ref[expert, start : start + width, cols], preferred_element_type=F32)

    def store(piece, here, own, other):
        cols = slice(piece * step, (piece + 1) * step)
        for offset, value in ((0, own), (half, other)):
            rows = slice(offset + here.start, offset + here.stop)
            value = acc_ref[rows, cols] + value
            hidden_ref[rows, cols] = (value / (1.0 + jnp.exp(-value))).astype(BF16)

    by_expert(own_tag, other_tag, up_ref.shape[2] // step, product, store)


def down_kernel(step, start, width, own_tag, other_tag, hidden_ref, down_ref, own_ref, other_ref):
    half = own_ref.shape[0]

    def product(expert, piece, here):
        rows = jnp.concatenate(
            [hidden_ref[here, :], hidden_ref[half + here.start : half + here.stop, :]], axis=0
        )
        cols = slice(start + piece * step, start + (piece + 1) * step)
        return jnp.dot(rows, down_ref[expert, :, cols], preferred_element_type=F32)

    def store(piece, here, own, other):
        cols = slice(piece * step, (piece + 1) * step)
        own_ref[here, cols] = own.astype(BF16)
        other_ref[here, cols] = other.astype(BF16)

    by_expert(own_tag, other_tag, width // step, product, store)


def unpack_kernel(onehot_ref, own_ref, other_ref, *out_refs):
    rows = out_refs[0].shape[0]
    slots = jnp.concatenate([own_ref[...], other_ref[...]], axis=0)
    dense = jnp.dot(onehot_ref[...], slots, preferred_element_type=F32).astype(BF16)
    for which, out_ref in enumerate(out_refs):
        out_ref[...] = dense[which * rows : (which + 1) * rows]


def add_kernel(chunks, terms, *refs):
    out_refs = refs[chunks * terms :]
    count = out_refs[0].shape[0]
    start = 0
    for chunk in range(chunks):
        blocks = refs[chunk * terms : (chunk + 1) * terms]
        total = blocks[0][...].astype(F32)
        for ref in blocks[1:]:
            total += ref[...].astype(F32)
        total = total.astype(BF16)
        width = total.shape[1]
        for piece, out_ref in enumerate(out_refs):
            out_ref[:, start : start + width] = total[piece * count : (piece + 1) * count]
        start += width


def finish_kernel(weight_ref, *refs):
    out_ref = refs[-1]
    weight = column(weight_ref, out_ref.shape[0])
    total = refs[0][...].astype(F32)
    for ref in refs[1:-1]:
        total += ref[...].astype(F32)
    out_ref[...] = (total.astype(BF16).astype(F32) * weight).astype(BF16)


def body(pair_rows, group_ids, local_ids, route_weight, w_up, w_down):
    groups = lax.axis_size("group")
    inner = lax.axis_size("inner")
    near, turns = 2, groups // 2
    far = inner // near
    count, model = pair_rows.shape
    experts, _, units = w_up.shape
    capacity = 2 * count // groups
    block = far * capacity
    blocks = turns * near
    rows = far * count
    half = blocks * block
    widths = [model // 2, model // 2]
    chunks = len(widths)
    starts = [sum(widths[:i]) for i in range(chunks)]
    step = min(256, units)


    mixed = far == blocks

    def exchange(value, wide, index):
        pairs = []
        for g in range(groups):
            for i in range(inner):
                if wide != (mixed and g % 2 == 1):
                    to = (g ^ 2 * (index // near)) * inner + (i ^ index % near)
                else:
                    to = g * inner + (i ^ near * index)
                pairs.append((g * inner + i, to))
        return lax.ppermute(value, ("group", "inner"), pairs)

    def along_group(value, flip):
        return lax.ppermute(value, "group", [(g, g ^ flip) for g in range(groups)])

    full = model + LANES
    named = group_ids * experts + local_ids
    (tagged,) = call(
        functools.partial(tag_kernel, capacity, experts),
        "tag_rows",
        [((count, full), BF16)],
        [pair_rows, named.reshape(1, count)],
    )

    pieces = [exchange(tagged, False, s) for s in range(far - 1, 0, -1)] + [tagged]
    pieces.reverse()
    parts = call(
        functools.partial(stack_kernel, far),
        "stack_rows",
        [((rows, w + (LANES if i == 0 else 0)), BF16) for i, w in enumerate(widths)],
        pieces,
        flops=STACK_FLOPS,
    )

    room = 4 + 8 * blocks * rows * half * 2 * 2 // MIB
    onehot = None
    slots = []
    for chunk, width in enumerate(widths):
        first = chunk == 0
        arrived = [parts[chunk]] + [exchange(parts[chunk], True, s) for s in range(1, blocks)]
        if first:
            down_held, down_token = call(
                load_kernel,
                "load_down",
                [(w_down.shape, BF16), ((8, LANES), F32)],
                [arrived[-1], w_down],
                specs=[ANY_SPEC, HBM_SPEC],
                scratch=[pltpu.SemaphoreType.DMA((experts,))],
                moved=4 * w_down.size,
                limit=38,
            )
        outs = [((half, width + LANES * first), BF16)] * 2
        if first:
            outs.append(((blocks * rows, 2 * half), BF16))
        packed = call(
            functools.partial(pack_kernel, capacity, blocks, first),
            f"pack_{chunk}",
            outs,
            [*arrived, down_token] if first else [*arrived, onehot],
            scratch=[pltpu.VMEM((blocks * rows, parts[chunk].shape[1]), BF16)],
            limit=room,
            flops=PACK_FLOPS,
        )
        if first:
            onehot = packed[2]
        slots.append((packed[0], along_group(packed[1], 1)))

    work = 2 * 2 * half * experts * units
    acc = call(
        functools.partial(up_first_kernel, step, widths[0]),
        "up_first",
        [((2 * half, units), F32)],
        [*slots[0], w_up],
        limit=8,
        flops=work * widths[0],
    )[0]
    (hidden,) = call(
        functools.partial(up_last_kernel, step, starts[1], widths[1]),
        "up_last",
        [((2 * half, units), BF16)],
        [*slots[0], *slots[1], w_up, acc],
        limit=8,
        flops=work * widths[1],
    )

    terms = [None] * chunks
    for chunk in reversed(range(chunks)):
        width = widths[chunk]
        own, other = call(
            functools.partial(down_kernel, min(256, width), starts[chunk], width),
            f"down_{chunk}",
            [((half, width), BF16)] * 2,
            [*slots[0], hidden, down_held],
            limit=8,
            flops=work * width,
        )
        dense = call(
            unpack_kernel,
            "unpack_slots",
            [((rows, width), BF16)] * blocks,
            [onehot, own, along_group(other, 1)],
            limit=room,
        )
        terms[chunk] = [dense[0]] + [exchange(dense[s], True, s) for s in range(blocks - 1, 0, -1)]
    sums = call(
        functools.partial(add_kernel, chunks, blocks),
        "add_plane",
        [((count, model), BF16)] * far,
        sum(terms, []),
    )
    parts = [sums[0]] + [exchange(sums[s], False, s) for s in range(far - 1, 0, -1)]
    return call(
        finish_kernel, "finish", [((count, model), BF16)], [route_weight.reshape(1, count), *parts]
    )[0]


def solution(mesh):
    placed = (
        P(("group", "inner"), None),
        P(("group", "inner"), None),
        P(("group", "inner"), None),
        P(("group", "inner")),
        P("group", None, "inner"),
        P("group", "inner", None),
    )
    return jax.shard_map(
        body, mesh=mesh, in_specs=placed, out_specs=P(("group", "inner"), None), check_vma=False
    )
```
